32 devices in a mesh: dp: 16 (over z, y, core), cond: 2 (over x).
Axes of the slice: x: 2, y: 2, z: 4, core: 2. Of those that a mesh axis runs over, the one named last changes fastest.
Arguments:
- inputs: bfloat16 [1024, 16, 1152], P(('dp', 'cond')), may hold values from -6 to 6
- out_grad: bfloat16 [1024, 16, 1152], P(('dp', 'cond')), may hold values from -6 to 6
- frame_counts: int32 [4], replicated, may hold values from 8 to 16
- timesteps: int32 [4], replicated, may hold values from 0 to 999
- labels: int32 [4], replicated, may hold values from 0 to 100
- owners: int32 [7], replicated, may hold values from 0 to 1, as said below
- w_time: float32 [2, 256, 1152], P('cond', None, 'dp'), as said below
- w_table: float32 [2, 101, 1152], P('cond', None, 'dp'), as said below
- w_modulate: float32 [2, 1152, 6912], P('cond', None, 'dp'), as said below
- w_attend: float32 [2, 1152, 3456], P('cond', None, 'dp'), as said below
- w_merge: float32 [2, 1152, 1152], P('cond', None, 'dp'), as said below
- w_up: float32 [2, 1152, 4608], P('cond', None, 'dp'), as said below
- w_down: float32 [2, 4608, 1152], P('cond', None, 'dp'), as said below
- mean_time: float32 [2, 256, 1152], P('cond', None, 'dp'), as said below
- mean_table: float32 [2, 101, 1152], P('cond', None, 'dp'), as said below
- mean_modulate: float32 [2, 1152, 6912], P('cond', None, 'dp'), as said below
- mean_attend: float32 [2, 1152, 3456], P('cond', None, 'dp'), as said below
- mean_merge: float32 [2, 1152, 1152], P('cond', None, 'dp'), as said below
- mean_up: float32 [2, 1152, 4608], P('cond', None, 'dp'), as said below
- mean_down: float32 [2, 4608, 1152], P('cond', None, 'dp'), as said below
- square_time: float32 [2, 256, 1152], P('cond', None, 'dp'), as said below
- square_table: float32 [2, 101, 1152], P('cond', None, 'dp'), as said below
- square_modulate: float32 [2, 1152, 6912], P('cond', None, 'dp'), as said below
- square_attend: float32 [2, 1152, 3456], P('cond', None, 'dp'), as said below
- square_merge: float32 [2, 1152, 1152], P('cond', None, 'dp'), as said below
- square_up: float32 [2, 1152, 4608], P('cond', None, 'dp'), as said below
- square_down: float32 [2, 4608, 1152], P('cond', None, 'dp'), as said below
Outputs:
- block_out: bfloat16 [1024, 16, 1152], P(('dp', 'cond'))
- input_grad: bfloat16 [1024, 16, 1152], P(('dp', 'cond'))
- new_time: float32 [2, 256, 1152], P('cond', None, 'dp')
- new_table: float32 [2, 101, 1152], P('cond', None, 'dp')
- new_modulate: float32 [2, 1152, 6912], P('cond', None, 'dp')
- new_attend: float32 [2, 1152, 3456], P('cond', None, 'dp')
- new_merge: float32 [2, 1152, 1152], P('cond', None, 'dp')
- new_up: float32 [2, 1152, 4608], P('cond', None, 'dp')
- new_down: float32 [2, 4608, 1152], P('cond', None, 'dp')
- first_time: float32 [2, 256, 1152], P('cond', None, 'dp')
- first_table: float32 [2, 101, 1152], P('cond', None, 'dp')
- first_modulate: float32 [2, 1152, 6912], P('cond', None, 'dp')
- first_attend: float32 [2, 1152, 3456], P('cond', None, 'dp')
- first_merge: float32 [2, 1152, 1152], P('cond', None, 'dp')
- first_up: float32 [2, 1152, 4608], P('cond', None, 'dp')
- first_down: float32 [2, 4608, 1152], P('cond', None, 'dp')
- second_time: float32 [2, 256, 1152], P('cond', None, 'dp')
- second_table: float32 [2, 101, 1152], P('cond', None, 'dp')
- second_modulate: float32 [2, 1152, 6912], P('cond', None, 'dp')
- second_attend: float32 [2, 1152, 3456], P('cond', None, 'dp')
- second_merge: float32 [2, 1152, 1152], P('cond', None, 'dp')
- second_up: float32 [2, 1152, 4608], P('cond', None, 'dp')
- second_down: float32 [2, 4608, 1152], P('cond', None, 'dp')
- copy_time: bfloat16 [2, 256, 1152], P('cond', None, 'dp')
- copy_table: bfloat16 [2, 101, 1152], P('cond', None, 'dp')
- copy_modulate: bfloat16 [2, 1152, 6912], P('cond', None, 'dp')
- copy_attend: bfloat16 [2, 1152, 3456], P('cond', None, 'dp')
- copy_merge: bfloat16 [2, 1152, 1152], P('cond', None, 'dp')
- copy_up: bfloat16 [2, 1152, 4608], P('cond', None, 'dp')
- copy_down: bfloat16 [2, 4608, 1152], P('cond', None, 'dp')
The draws below stay inside these ranges and needn't reach their ends.
Inputs may be any that keep to these rules, and one draw needn't show every extreme that they name: owners[k] is the slot of matrix k that holds it; the matrices are time, table, modulate, attend, merge, up, down in this order. `w_time`: slot owners[0] holds the matrix, the other slot zeros. `w_table`: slot owners[1] holds the matrix, the other slot zeros. `w_modulate`: slot owners[2] holds the matrix, the other slot zeros. `w_attend`: slot owners[3] holds the matrix, the other slot zeros. `w_merge`: slot owners[4] holds the matrix, the other slot zeros. `w_up`: slot owners[5] holds the matrix, the other slot zeros. `w_down`: slot owners[6] holds the matrix, the other slot zeros. `mean_time`: slot owners[0] holds the moment, the other slot zeros. `mean_table`: slot owners[1] holds the moment, the other slot zeros. `mean_modulate`: slot owners[2] holds the moment, the other slot zeros. `mean_attend`: slot owners[3] holds the moment, the other slot zeros. `mean_merge`: slot owners[4] holds the moment, the other slot zeros. `mean_up`: slot owners[5] holds the moment, the other slot zeros. `mean_down`: slot owners[6] holds the moment, the other slot zeros. `square_time`: slot owners[0] holds the moment, positive, the other slot zeros. `square_table`: slot owners[1] holds the moment, positive, the other slot zeros. `square_modulate`: slot owners[2] holds the moment, positive, the other slot zeros. `square_attend`: slot owners[3] holds the moment, positive, the other slot zeros. `square_merge`: slot owners[4] holds the moment, positive, the other slot zeros. `square_up`: slot owners[5] holds the moment, positive, the other slot zeros. `square_down`: slot owners[6] holds the moment, positive, the other slot zeros.
All inputs are finite; a program needn't handle non-finite values.
Results may differ from the reference program's by a relative error of at most 0.014.
The reference program's roundings to bfloat16 on the way count: a program that leaves them out, or rounds other values in their place, can miss the bound.
Values may be sent and summed in bfloat16 or wider, within the bound.
No kernel may reach another device: no remote copies, remote signals or barrier semaphores. Data moves between devices by JAX's collectives and lax.ppermute only.
A program may use at most 192 MiB of HBM per device.

```python
import math
from functools import partial
import jax
import jax.numpy as jnp
from jax import lax

D = 1152
HEADS = 16
HEAD = 72
FF = 4608
FREQ = 256
LABELS = 101
FRAMES = 16
PATCHES = 256
STEP = 5
POSITIONS = 1024
CLIPS = 4


def owner_list(key):
    return jax.random.randint(jax.random.fold_in(key, 7001), (7,), 0, 2).astype(jnp.int32)


def matrix_shape(number):
    shapes = [(FREQ, D), (LABELS, D), (D, 6 * D), (D, 3 * D), (D, D), (D, FF), (FF, D)]
    return (2,) + shapes[number]


def weight_scale(number):
    scales = [FREQ ** (-0.5), 1.0, D ** (-0.5), D ** (-0.5), 2.0 * D ** (-0.5), D ** (-0.5), FF ** (-0.5)]
    return scales[number]


def grad_scale(number):
    tokens = math.sqrt(POSITIONS * FRAMES)
    scales = [0.6 * tokens, 1.5 * math.sqrt(PATCHES * FRAMES), 0.7 * tokens, tokens, 0.6 * tokens, 0.3 * tokens, 0.6 * tokens]
    return scales[number]


def in_slot(owners, number, values):
    keep = (jnp.arange(2) == owners[number]).astype(jnp.float32)[:, None, None]
    return values * keep


def master_values(key, owners, number):
    values = jax.random.normal(key, matrix_shape(number), jnp.float32) * weight_scale(number)
    return in_slot(owners, number, values)


def first_values(key, owners, number):
    values = jax.random.normal(key, matrix_shape(number), jnp.float32) * grad_scale(number)
    return in_slot(owners, number, values)


def second_values(key, owners, number):
    factor = jnp.exp(jax.random.uniform(key, matrix_shape(number), jnp.float32, 0.0, math.log(4.0)))
    return in_slot(owners, number, factor * grad_scale(number) ** 2)


def draw_owners(key, part):
    return owner_list(key)


def draw_w_time(key, part):
    owners = owner_list(key)
    key = jax.random.fold_in(key, 10)
    return master_values(key, owners, 0)


def draw_w_table(key, part):
    owners = owner_list(key)
    key = jax.random.fold_in(key, 11)
    return master_values(key, owners, 1)


def draw_w_modulate(key, part):
    owners = owner_list(key)
    key = jax.random.fold_in(key, 12)
    return master_values(key, owners, 2)


def draw_w_attend(key, part):
    owners = owner_list(key)
    key = jax.random.fold_in(key, 13)
    return master_values(key, owners, 3)


def draw_w_merge(key, part):
    owners = owner_list(key)
    key = jax.random.fold_in(key, 14)
    return master_values(key, owners, 4)


def draw_w_up(key, part):
    owners = owner_list(key)
    key = jax.random.fold_in(key, 15)
    return master_values(key, owners, 5)


def draw_w_down(key, part):
    owners = owner_list(key)
    key = jax.random.fold_in(key, 16)
    return master_values(key, owners, 6)


def draw_mean_time(key, part):
    owners = owner_list(key)
    key = jax.random.fold_in(key, 20)
    return first_values(key, owners, 0)


def draw_mean_table(key, part):
    owners = owner_list(key)
    key = jax.random.fold_in(key, 21)
    return first_values(key, owners, 1)


def draw_mean_modulate(key, part):
    owners = owner_list(key)
    key = jax.random.fold_in(key, 22)
    return first_values(key, owners, 2)


def draw_mean_attend(key, part):
    owners = owner_list(key)
    key = jax.random.fold_in(key, 23)
    return first_values(key, owners, 3)


def draw_mean_merge(key, part):
    owners = owner_list(key)
    key = jax.random.fold_in(key, 24)
    return first_values(key, owners, 4)


def draw_mean_up(key, part):
    owners = owner_list(key)
    key = jax.random.fold_in(key, 25)
    return first_values(key, owners, 5)


def draw_mean_down(key, part):
    owners = owner_list(key)
    key = jax.random.fold_in(key, 26)
    return first_values(key, owners, 6)


def draw_square_time(key, part):
    owners = owner_list(key)
    key = jax.random.fold_in(key, 30)
    return second_values(key, owners, 0)


def draw_square_table(key, part):
    owners = owner_list(key)
    key = jax.random.fold_in(key, 31)
    return second_values(key, owners, 1)


def draw_square_modulate(key, part):
    owners = owner_list(key)
    key = jax.random.fold_in(key, 32)
    return second_values(key, owners, 2)


def draw_square_attend(key, part):
    owners = owner_list(key)
    key = jax.random.fold_in(key, 33)
    return second_values(key, owners, 3)


def draw_square_merge(key, part):
    owners = owner_list(key)
    key = jax.random.fold_in(key, 34)
    return second_values(key, owners, 4)


def draw_square_up(key, part):
    owners = owner_list(key)
    key = jax.random.fold_in(key, 35)
    return second_values(key, owners, 5)


def draw_square_down(key, part):
    owners = owner_list(key)
    key = jax.random.fold_in(key, 36)
    return second_values(key, owners, 6)


def with_ends(array, key, smallest, top_value):
    spot = [jax.random.randint(jax.random.fold_in(key, axis), (), 0, length) for axis, length in enumerate(array.shape)]
    longest = array.shape.index(max(array.shape))
    next_to = spot[:longest] + [(spot[longest] + 1) % array.shape[longest]] + spot[longest + 1:]
    return array.at[tuple(spot)].set(smallest).at[tuple(next_to)].set(top_value)


def steps_of(stream_key, shape, shards, least, high):
    level, own = 1.0, jax.random.fold_in(stream_key, 6)
    for axis_at, blocks in shards:
        steps = jnp.exp(jax.random.uniform(jax.random.fold_in(own, axis_at), (blocks,), jnp.float32, least / len(shards), high / len(shards)))
        level = level * jnp.repeat(steps, shape[axis_at] // blocks).reshape([-1 if axis == axis_at else 1 for axis in range(len(shape))])
    return level


def scatter_about(stream_key, extent, deviation, limit, cuts=(), held_as=jnp.bfloat16):
    values = deviation * jax.random.normal(stream_key, extent, jnp.float32)
    if cuts:
        values = values * steps_of(stream_key, extent, cuts, -0.22, 0.18)
    return jnp.clip(values, -limit, limit).astype(held_as)


def setup_inputs(seed: int = 0) -> dict:
    seeds = jax.random.split(jax.random.key(seed), 28)
    return {
        "inputs": scatter_about(seeds[0], (POSITIONS, FRAMES, D), 1.0, 6.0, ((0, 32),)),
        "out_grad": scatter_about(seeds[1], (POSITIONS, FRAMES, D), 1.0, 6.0, ((0, 32),)),
        "frame_counts": with_ends(jax.random.randint(seeds[2], (CLIPS,), 8, FRAMES + 1), jax.random.fold_in(seeds[2], 1), 8, FRAMES).astype(jnp.int32),
        "timesteps": with_ends(jax.random.randint(seeds[3], (CLIPS,), 0, 1000), jax.random.fold_in(seeds[3], 1), 0, 999).astype(jnp.int32),
        "labels": with_ends(jax.random.randint(seeds[4], (CLIPS,), 0, LABELS), jax.random.fold_in(seeds[4], 1), 0, LABELS - 1).astype(jnp.int32),
        "owners": draw_owners(jax.random.fold_in(seeds[27], 71), 0),
        "w_time": draw_w_time(jax.random.fold_in(seeds[27], 71), 0),
        "w_table": draw_w_table(jax.random.fold_in(seeds[27], 71), 0),
        "w_modulate": draw_w_modulate(jax.random.fold_in(seeds[27], 71), 0),
        "w_attend": draw_w_attend(jax.random.fold_in(seeds[27], 71), 0),
        "w_merge": draw_w_merge(jax.random.fold_in(seeds[27], 71), 0),
        "w_up": draw_w_up(jax.random.fold_in(seeds[27], 71), 0),
        "w_down": draw_w_down(jax.random.fold_in(seeds[27], 71), 0),
        "mean_time": draw_mean_time(jax.random.fold_in(seeds[27], 71), 0),
        "mean_table": draw_mean_table(jax.random.fold_in(seeds[27], 71), 0),
        "mean_modulate": draw_mean_modulate(jax.random.fold_in(seeds[27], 71), 0),
        "mean_attend": draw_mean_attend(jax.random.fold_in(seeds[27], 71), 0),
        "mean_merge": draw_mean_merge(jax.random.fold_in(seeds[27], 71), 0),
        "mean_up": draw_mean_up(jax.random.fold_in(seeds[27], 71), 0),
        "mean_down": draw_mean_down(jax.random.fold_in(seeds[27], 71), 0),
        "square_time": draw_square_time(jax.random.fold_in(seeds[27], 71), 0),
        "square_table": draw_square_table(jax.random.fold_in(seeds[27], 71), 0),
        "square_modulate": draw_square_modulate(jax.random.fold_in(seeds[27], 71), 0),
        "square_attend": draw_square_attend(jax.random.fold_in(seeds[27], 71), 0),
        "square_merge": draw_square_merge(jax.random.fold_in(seeds[27], 71), 0),
        "square_up": draw_square_up(jax.random.fold_in(seeds[27], 71), 0),
        "square_down": draw_square_down(jax.random.fold_in(seeds[27], 71), 0),
    }


HIGHEST = lax.Precision.HIGHEST
EPSILON = 1e-06

@jax.custom_vjp
def low(v):
    return lax.optimization_barrier(v.astype(jnp.bfloat16)).astype(jnp.float32)

@jax.custom_vjp
def low_back(v):
    return v

def low_keep(v):
    return (low(v), None)

def low_pass(kept, grad):
    return (grad,)

def back_keep(v):
    return (v, None)

def back_low(kept, grad):
    return (low(grad),)
low.defvjp(low_keep, low_pass)
low_back.defvjp(back_keep, back_low)

def timestep_features(timesteps):
    half_count = FREQ // 2
    freqs = jnp.exp(-math.log(10000.0) * jnp.arange(half_count, dtype=jnp.float32) / half_count)
    angles = timesteps.astype(jnp.float32)[:, None] * freqs[None, :]
    return jnp.concatenate([jnp.cos(angles), jnp.sin(angles)], axis=1)

def normalize(values):
    centre = values - lax.optimization_barrier(jnp.mean(values, axis=-1, keepdims=True))
    spread = lax.rsqrt(lax.optimization_barrier(jnp.mean(centre * centre, axis=-1, keepdims=True)) + EPSILON)
    return centre * spread

def trunk_block(matrices, mod_rows, counts, block_in):
    attend_w, merge_w, up_w, down_w = matrices
    positions = block_in.shape[0]
    pieces = [mod_rows[:, None, part * D:(part + 1) * D] for part in range(6)]
    shift_one, scale_one, gate_one, shift_two, scale_two, gate_two = pieces
    hidden_one = low(normalize(block_in) * (1.0 + scale_one) + shift_one)
    qkv = low(low_back(jnp.einsum('pfd,de->pfe', hidden_one, attend_w, precision=HIGHEST)))
    queries = qkv[..., :D].reshape(positions, FRAMES, HEADS, HEAD)
    key_rows = qkv[..., D:2 * D].reshape(positions, FRAMES, HEADS, HEAD)
    value_rows = qkv[..., 2 * D:].reshape(positions, FRAMES, HEADS, HEAD)
    scores = low_back(jnp.einsum('pfhe,pghe->phfg', queries, key_rows, precision=HIGHEST) / math.sqrt(HEAD))
    valid = jnp.arange(FRAMES)[None, :] < counts[:, None]
    scores = jnp.where(valid[:, None, None, :], scores, -1e+30)
    top = lax.optimization_barrier(jnp.max(scores, axis=-1, keepdims=True))
    expo = jnp.exp(scores - top)
    probs = expo / lax.optimization_barrier(jnp.sum(expo, axis=-1, keepdims=True))
    attended = jnp.einsum('phfg,pghe->pfhe', low(probs), value_rows, precision=HIGHEST)
    attended = low(low_back(attended.reshape(positions, FRAMES, D)))
    branch = low_back(jnp.einsum('pfd,de->pfe', attended, merge_w, precision=HIGHEST))
    middle = block_in + gate_one * branch
    hidden_two = low(normalize(middle) * (1.0 + scale_two) + shift_two)
    upper = low_back(jnp.einsum('pfd,de->pfe', hidden_two, up_w, precision=HIGHEST))
    activ = low(jax.nn.gelu(upper, approximate=True))
    mlp_out = low_back(jnp.einsum('pfd,de->pfe', activ, down_w, precision=HIGHEST))
    return jnp.where(valid[:, :, None], middle + gate_two * mlp_out, 0.0)

def reference(inputs, out_grad, frame_counts, timesteps, labels, owners, w_time, w_table, w_modulate, w_attend, w_merge, w_up, w_down, mean_time, mean_table, mean_modulate, mean_attend, mean_merge, mean_up, mean_down, square_time, square_table, square_modulate, square_attend, square_merge, square_up, square_down):
    masters = [w_time, w_table, w_modulate, w_attend, w_merge, w_up, w_down]
    means = [mean_time, mean_table, mean_modulate, mean_attend, mean_merge, mean_up, mean_down]
    squares = [square_time, square_table, square_modulate, square_attend, square_merge, square_up, square_down]
    live = [master[owners[number]] for number, master in enumerate(masters)]
    copies = [low(weight) for weight in live]
    features = timestep_features(timesteps)
    clip_of = jnp.arange(POSITIONS) // PATCHES
    counts = frame_counts[clip_of]
    block = math.gcd(POSITIONS, 256)
    blocks = POSITIONS // block

    def forward(time_w, table_w, modulate_w, attend_w, merge_w, up_w, down_w, tokens):
        time_pre = jnp.dot(low(features), time_w, precision=HIGHEST)
        cond = table_w[labels] + jax.nn.silu(time_pre)
        modulation = jnp.dot(low(jax.nn.silu(cond)), modulate_w, precision=HIGHEST)
        mod_rows = modulation[clip_of]
        step_fn = jax.checkpoint(partial(trunk_block, (attend_w, merge_w, up_w, down_w)))

        def scan_fn(carry, inputs_block):
            block_in, block_mod, block_counts = inputs_block
            return (carry, step_fn(block_mod, block_counts, block_in))
        carry, outs = lax.scan(scan_fn, jnp.zeros((), jnp.float32), (tokens.reshape(blocks, block, FRAMES, D), mod_rows.reshape(blocks, block, 6 * D), counts.reshape(blocks, block)))
        return outs.reshape(POSITIONS, FRAMES, D)
    outputs, pullback = jax.vjp(forward, *copies, inputs.astype(jnp.float32))
    grads = pullback(out_grad.astype(jnp.float32))
    rates = [0.5 * FREQ ** (-0.5), 0.5, 0.5 * D ** (-0.5), 0.5 * D ** (-0.5), D ** (-0.5), 0.5 * D ** (-0.5), 0.5 * FF ** (-0.5)]
    slots = jnp.arange(2)[:, None, None]
    correct = 1.0 - 0.5 ** STEP
    new_list, first_list, second_list, copy_list = ([], [], [], [])
    for number in range(7):
        grad = grads[number]
        first = 0.5 * means[number][owners[number]] + 0.5 * grad
        second = 0.5 * squares[number][owners[number]] + 0.5 * grad * grad
        update = first / correct / (jnp.sqrt(second / correct) + 1e-08)
        fresh = live[number] - rates[number] * (update + 0.01 * live[number])
        keep = slots == owners[number]
        new_list.append(jnp.where(keep, fresh[None], 0.0))
        first_list.append(jnp.where(keep, first[None], 0.0))
        second_list.append(jnp.where(keep, second[None], 0.0))
        copy_list.append(jnp.where(keep, fresh[None], 0.0).astype(jnp.bfloat16))
    return (outputs.astype(jnp.bfloat16), grads[7].astype(jnp.bfloat16), *new_list, *first_list, *second_list, *copy_list)
```

```python
from functools import partial
import math

import jax
import jax.numpy as jnp
from jax import lax
from jax.experimental import pallas as pl
from jax.experimental.pallas import tpu as pltpu
from jax.sharding import Mesh, PartitionSpec as P

D = 1152
HEADS = 16
HEAD = 72
FF = 4608
FREQ = 256
LABELS = 101
FRAMES = 16
PATCHES = 256
STEP = 5


HIGHEST = lax.Precision.HIGHEST
EPSILON = 1e-06


def contract_rows(left, right, precision=None):
    return lax.dot_general(
        left,
        right,
        (((0,), (0,)), ((), ())),
        precision=precision,
        preferred_element_type=jnp.float32,
    )


def contract_cols(left, right, precision=None):
    return lax.dot_general(
        left,
        right,
        (((1,), (1,)), ((), ())),
        precision=precision,
        preferred_element_type=jnp.float32,
    )


def normalize(values):
    centre = values - jnp.mean(values, axis=-1, keepdims=True)
    spread = lax.rsqrt(jnp.mean(centre * centre, axis=-1, keepdims=True) + EPSILON)
    return (centre * spread, spread)


def normalize_back(upstream, normed, spread):
    return spread * (
        upstream
        - jnp.mean(upstream, axis=-1, keepdims=True)
        - normed * jnp.mean(upstream * normed, axis=-1, keepdims=True)
    )


def timestep_features(timesteps):
    half_count = FREQ // 2
    freqs = jnp.exp(-math.log(10000.0) * jnp.arange(half_count, dtype=jnp.float32) / half_count)
    angles = timesteps.astype(jnp.float32)[:, None] * freqs[None, :]
    return jnp.concatenate([jnp.cos(angles), jnp.sin(angles)], axis=1)


def adamw_step(master, first, second, grad, rate):
    first_new = 0.5 * first + 0.5 * grad
    second_new = 0.5 * second + 0.5 * grad * grad
    correct = 1.0 - 0.5**STEP
    update = first_new / correct / (jnp.sqrt(second_new / correct) + 1e-08)
    return (master - rate * (update + 0.01 * master), first_new, second_new)


BF16, F32 = jnp.bfloat16, jnp.float32
SLAB = 16
GROUP = 128
WIDE = 256


def vmem(*shape, dtype=BF16):
    return pltpu.VMEM(shape, dtype)


def any_spec():
    return pl.BlockSpec(memory_space=pl.ANY)


def smem_spec():
    return pl.BlockSpec(memory_space=pltpu.SMEM)


def vmem_spec():
    return pl.BlockSpec(memory_space=pltpu.VMEM)


def dot_nn(left, right):
    return lax.dot_general(left, right, (((1,), (0,)), ((), ())), preferred_element_type=F32)


def dot_nt(left, right):
    return lax.dot_general(left, right, (((1,), (1,)), ((), ())), preferred_element_type=F32)


def run_kernel(body, operands, outs, scratch, ordered_after=(), mib=56, **kw):
    arrays = [array for array, _ in operands] + list(ordered_after)
    specs = [spec for _, spec in operands] + [any_spec() for _ in ordered_after]
    n_in, n_dep = len(operands), len(ordered_after)

    def kernel(*refs):
        body(*refs[:n_in], *refs[n_in + n_dep :])

    return pl.pallas_call(
        kernel,
        out_shape=[jax.ShapeDtypeStruct(shape, dtype) for shape, dtype in outs],
        in_specs=specs,
        out_specs=[vmem_spec() for _ in outs],
        scratch_shapes=scratch,
        compiler_params=pltpu.CompilerParams(vmem_limit_bytes=mib * 2**20),
        cost_estimate=pl.CostEstimate(flops=1000, bytes_accessed=1000, transcendentals=0),
        **kw,
    )(*arrays)


def block_order(place):
    y, c = place[1], place[2]
    for dc in range(2):
        for dy in range(2):
            yy = y if dy == 0 else 1 - y
            cc = c if dc == 0 else 1 - c
            for zz in range(4):
                yield dc * 2 + dy, zz, (zz * 2 + yy) * 2 + cc


def start_all(copies, sems):
    made = [pltpu.make_async_copy(src, dst, sems.at[i]) for i, (src, dst) in enumerate(copies)]
    for copy in made:
        copy.start()
    return made


def attend_copies(pieces, place, wide):
    x = place[3]
    for pair, zz, b in block_order(place):
        main, late = pieces[2 * pair], pieces[2 * pair + 1]
        yield main.at[zz, 0], wide.at[b * 3]
        yield main.at[zz, 2], wide.at[b * 3 + 1 + x]
        yield late.at[zz], wide.at[b * 3 + 2 - x]


def merge_copies(pieces, place, wide):
    for pair, zz, b in block_order(place):
        yield pieces[2 * pair].at[zz, 1], wide.at[b]


UP_E, UP_L = 128, 80


def up_copies(pieces, place, wide):
    x = place[3]
    size = UP_E + 2 * UP_L
    for pair, zz, b in block_order(place):
        main, late = pieces[2 * pair], pieces[2 * pair + 1]
        row = pl.multiple_of(b * size, 16)
        near = pl.multiple_of(b * size + UP_E + UP_L * x, 16)
        other = pl.multiple_of(b * size + UP_E + UP_L - UP_L * x, 16)
        yield main.at[zz, pl.ds(0, UP_E)], wide.at[pl.ds(row, UP_E)]
        yield main.at[zz, pl.ds(UP_E, UP_L)], wide.at[pl.ds(near, UP_L)]
        yield late.at[zz], wide.at[pl.ds(other, UP_L)]


DOWN_E, DOWN_L = 2048, 1280


def down_copies(pieces, place, wide):
    x = place[3]
    near = pl.multiple_of(DOWN_E + DOWN_L * x, 128)
    other = pl.multiple_of(DOWN_E + DOWN_L - DOWN_L * x, 128)
    for pair, zz, b in block_order(place):
        main, late = pieces[2 * pair], pieces[2 * pair + 1]
        yield main.at[zz, :, pl.ds(0, DOWN_E)], wide.at[b, :, pl.ds(0, DOWN_E)]
        yield main.at[zz, :, pl.ds(DOWN_E, DOWN_L)], wide.at[b, :, pl.ds(near, DOWN_L)]
        yield late.at[zz], wide.at[b, :, pl.ds(other, DOWN_L)]


def rows_of(wide, first, count, cols=None):
    value = wide[pl.ds(first, count)] if cols is None else wide[pl.ds(first, count), :, cols]
    return value.astype(F32).reshape(count * HEAD, value.shape[-1]).astype(BF16)


def norm_slab(values):
    mean = jnp.sum(values, axis=1, keepdims=True) * (1.0 / D)
    centre = values - mean
    spread = lax.rsqrt(jnp.sum(centre * centre, axis=1, keepdims=True) * (1.0 / D) + EPSILON)
    return centre * spread, spread


def back_slab(upstream, normed, spread):
    first = jnp.sum(upstream, axis=1, keepdims=True) * (1.0 / D)
    second = jnp.sum(upstream * normed, axis=1, keepdims=True) * (1.0 / D)
    return spread * (upstream - first - normed * second)


def slabs(rows, size, body):
    @pl.loop(0, rows // size)
    def _(i):
        body(pl.ds(pl.multiple_of(i * size, size), size))


def fold(ref, value):
    ref[...] += jnp.sum(value.reshape(value.shape[0] // 8, 8, value.shape[1]), axis=0)


def turn(src, dst):
    @pl.loop(0, src.shape[0] // GROUP)
    def _(i):
        at = pl.ds(pl.multiple_of(i * GROUP, GROUP), GROUP)
        dst[:, at] = src[at].astype(F32).T


def store_relative(ref, turned, y, c):
    for b in range(16):
        zz, yy, cc = b // 4, (b // 2) % 2, b % 2
        dy = y if yy == 0 else 1 - y
        dc = c if cc == 0 else 1 - c
        ref[dc, dy * 4 + zz] = turned[b * HEAD : (b + 1) * HEAD].astype(BF16)


def frame_mask(count):
    keys = lax.broadcasted_iota(jnp.int32, (GROUP, GROUP), 0)
    asks = lax.broadcasted_iota(jnp.int32, (GROUP, GROUP), 1)
    return (keys // FRAMES == asks // FRAMES) & (keys % FRAMES < count)


def probs_of(key, query, mask):
    scores = dot_nn(key.astype(F32).T.astype(BF16), query) * (1.0 / math.sqrt(HEAD))
    scores = jnp.where(mask, scores, -1e30)
    top = jnp.max(scores, axis=0, keepdims=True)
    expo = jnp.where(mask, jnp.exp(scores - top), 0.0)
    return expo / jnp.sum(expo, axis=0, keepdims=True)


def first_half_kernel(place, tokens, mods, *rest):
    pieces, rest = rest[:8], rest[8:]
    h1, qkv, attended, branch, h2, wide, merge, turned, sems = rest
    copies = list(attend_copies(pieces, place, wide)) + list(merge_copies(pieces, place, merge))
    copies = start_all(copies, sems)
    rows = tokens.shape[0]

    def norm_one(at):
        normed, _ = norm_slab(tokens[at].astype(F32))
        h1[at] = (normed * (1.0 + mods[1:2]) + mods[0:1]).astype(BF16)

    slabs(rows, SLAB, norm_one)
    for copy in copies:
        copy.wait()

    @pl.loop(0, 12)
    def _(i):
        value = dot_nt(rows_of(wide, i * 4, 4), h1[...])
        for j in range(4):
            qkv[i * 4 + j] = value[j * HEAD : (j + 1) * HEAD].astype(BF16)

    mask = frame_mask(place[4])

    @pl.loop(0, HEADS)
    def _(head):
        for group in range(rows // GROUP):
            at = pl.ds(group * GROUP, GROUP)
            probs = probs_of(qkv[HEADS + head, :, at], qkv[head, :, at], mask)
            turned[head, :, at] = dot_nn(qkv[2 * HEADS + head, :, at], probs.astype(BF16))

    for group in range(rows // GROUP):
        at = pl.ds(group * GROUP, GROUP)
        attended[at] = turned[:, :, at].reshape(D, GROUP).T.astype(BF16)
    branch[...] = dot_nt(attended[...], rows_of(merge, 0, 16))

    def norm_two(at):
        middle = tokens[at].astype(F32) + mods[2:3] * branch[at]
        normed, _ = norm_slab(middle)
        h2[at] = (normed * (1.0 + mods[4:5]) + mods[3:4]).astype(BF16)

    slabs(rows, SLAB, norm_two)


def up_kernel(place, h2, *rest):
    pieces, rest = rest[:8], rest[8:]
    act, slope, wide, upper, sems = rest
    for copy in start_all(list(up_copies(pieces, place, wide)), sems):
        copy.wait()
    rows = h2.shape[0]
    root = math.sqrt(2.0 / math.pi)

    @pl.loop(0, FF // WIDE)
    def _(i):
        cols = pl.ds(pl.multiple_of(i * WIDE, WIDE), WIDE)
        upper[...] = dot_nt(h2[...], wide[cols])

        def gelu(at):
            u = upper[at]
            square = u * u
            bent = jnp.tanh(root * u * (1.0 + 0.044715 * square))
            half = 0.5 * (1.0 + bent)
            act[at, cols] = (u * half).astype(BF16)
            rise = root * (1.0 + 3.0 * 0.044715 * square)
            slope[at, cols] = (half + 0.5 * u * (1.0 - bent * bent) * rise).astype(BF16)

        slabs(rows, 32, gelu)


def start_back_kernel(place, out_grad, mods, d_mlp, relative, turned):
    rows = out_grad.shape[0]

    def scale(at):
        frame = lax.broadcasted_iota(jnp.int32, (SLAB, 1), 0) % FRAMES
        dy = jnp.where(frame < place[4], out_grad[at].astype(F32), 0.0)
        d_mlp[at] = (dy * mods[5:6]).astype(BF16)

    slabs(rows, SLAB, scale)
    turn(d_mlp, turned)
    store_relative(relative, turned, place[1], place[2])


def d_upper_kernel(place, d_mlp, slope, *rest):
    pieces, rest = rest[:8], rest[8:]
    d_upper, d_upper_t, wide, value, sems = rest
    for copy in start_all(list(down_copies(pieces, place, wide)), sems):
        copy.wait()
    rows = d_mlp.shape[0]

    @pl.loop(0, FF // WIDE)
    def _(i):
        cols = pl.ds(pl.multiple_of(i * WIDE, WIDE), WIDE)
        value[...] = dot_nn(d_mlp[...], rows_of(wide, 0, 16, cols))

        @pl.loop(0, rows // GROUP)
        def _(j):
            at = pl.ds(pl.multiple_of(j * GROUP, GROUP), GROUP)
            part = value[at] * slope[at, cols].astype(F32)
            d_upper[at, cols] = part.astype(BF16)
            d_upper_t[cols, at] = part.T.astype(BF16)


def middle_back_kernel(place, d_upper, tokens, out_grad, branch, mods, *rest):
    ups, firsts, rest = rest[:8], rest[8:16], rest[16:]
    d_middle, d_branch, relative, d_att, sums, wide, merge, value, turned, fold_a, fold_b, fold_c, sems = rest
    copies = list(up_copies(ups, place, wide)) + list(merge_copies(firsts, place, merge))
    copies = start_all(copies, sems)
    for copy in copies:
        copy.wait()
    rows = tokens.shape[0]
    value[...] = dot_nn(d_upper[...], wide[...])
    for ref in (fold_a, fold_b, fold_c):
        ref[...] = jnp.zeros_like(ref)

    def back(at):
        d_h2 = value[at]
        arm = branch[at]
        normed, spread = norm_slab(tokens[at].astype(F32) + mods[2:3] * arm)
        frame = lax.broadcasted_iota(jnp.int32, (SLAB, 1), 0) % FRAMES
        dy = jnp.where(frame < place[4], out_grad[at].astype(F32), 0.0)
        d_mid = dy + back_slab(d_h2 * (1.0 + mods[4:5]), normed, spread)
        d_middle[at] = d_mid
        d_branch[at] = (d_mid * mods[2:3]).astype(BF16)
        fold(fold_a, d_mid * arm)
        fold(fold_b, d_h2)
        fold(fold_c, d_h2 * normed)

    slabs(rows, SLAB, back)
    sums[...] = jnp.zeros_like(sums)
    sums[0:1] = jnp.sum(fold_a[...], axis=0, keepdims=True)
    sums[1:2] = jnp.sum(fold_b[...], axis=0, keepdims=True)
    sums[2:3] = jnp.sum(fold_c[...], axis=0, keepdims=True)
    turn(d_branch, turned)
    store_relative(relative, turned, place[1], place[2])
    value[...] = dot_nn(d_branch[...], rows_of(merge, 0, 16))
    turn(value, turned)
    for head in range(HEADS):
        d_att[head] = turned[head * HEAD : (head + 1) * HEAD].astype(BF16)


def attend_back_kernel(place, qkv, d_att, d_qkv, relative, d_q, d_k, d_v):
    rows = qkv.shape[2]
    y, c = place[1], place[2]
    mask = frame_mask(place[4])
    scale = 1.0 / math.sqrt(HEAD)

    @pl.loop(0, HEADS)
    def _(head):
        for group in range(rows // GROUP):
            at = pl.ds(group * GROUP, GROUP)
            query, key = qkv[head, :, at], qkv[HEADS + head, :, at]
            val, grad = qkv[2 * HEADS + head, :, at], d_att[head, :, at]
            probs = probs_of(key, query, mask)
            d_probs = dot_nn(val.astype(F32).T.astype(BF16), grad)
            d_v[head, :, at] = dot_nt(grad, probs.astype(BF16))
            inner = jnp.sum(probs * d_probs, axis=0, keepdims=True)
            d_scores = (probs * (d_probs - inner)).astype(BF16)
            d_q[head, :, at] = dot_nn(key, d_scores) * scale
            d_k[head, :, at] = dot_nt(query, d_scores) * scale

    for part, ref in enumerate((d_q, d_k, d_v)):
        for group in range(rows // GROUP):
            at = pl.ds(group * GROUP, GROUP)
            d_qkv[at, part * D : (part + 1) * D] = ref[:, :, at].reshape(D, GROUP).T.astype(BF16)
        for head in range(HEADS):
            number = part * HEADS + head
            b, tile = number // 3, number % 3
            zz, yy, cc = b // 4, (b // 2) % 2, b % 2
            dy = y if yy == 0 else 1 - y
            dc = c if cc == 0 else 1 - c
            relative[dc, dy * 4 + zz, tile] = ref[head].astype(BF16)


def input_back_kernel(place, d_qkv, tokens, d_middle, mods, *rest):
    pieces, rest = rest[:8], rest[8:]
    input_grad, sums, wide, value, fold_a, fold_b, sems = rest
    for copy in start_all(list(attend_copies(pieces, place, wide)), sems):
        copy.wait()
    rows = tokens.shape[0]
    for part in range(3):
        add = dot_nn(d_qkv[:, part * D : (part + 1) * D], rows_of(wide, part * 16, 16))
        if part == 0:
            value[...] = add
        else:
            value[...] += add
    for ref in (fold_a, fold_b):
        ref[...] = jnp.zeros_like(ref)

    def back(at):
        d_h1 = value[at]
        normed, spread = norm_slab(tokens[at].astype(F32))
        d_token = d_middle[at] + back_slab(d_h1 * (1.0 + mods[1:2]), normed, spread)
        input_grad[at] = d_token.astype(BF16)
        fold(fold_a, d_h1)
        fold(fold_b, d_h1 * normed)

    slabs(rows, SLAB, back)
    sums[...] = jnp.zeros_like(sums)
    sums[0:1] = jnp.sum(fold_a[...], axis=0, keepdims=True)
    sums[1:2] = jnp.sum(fold_b[...], axis=0, keepdims=True)


def output_kernel(place, act, tokens, branch, out_grad, mods, *rest):
    pieces, rest = rest[:8], rest[8:]
    block_out, sums, wide, value, fold_a, sems = rest
    for copy in start_all(list(down_copies(pieces, place, wide)), sems):
        copy.wait()
    rows = tokens.shape[0]
    value[...] = jnp.zeros_like(value)

    @pl.loop(0, FF // WIDE)
    def _(i):
        cols = pl.ds(pl.multiple_of(i * WIDE, WIDE), WIDE)
        value[...] += dot_nt(act[:, cols], rows_of(wide, 0, 16, cols))

    fold_a[...] = jnp.zeros_like(fold_a)

    def finish(at):
        mlp = value[at]
        frame = lax.broadcasted_iota(jnp.int32, (SLAB, 1), 0) % FRAMES
        keep = frame < place[4]
        middle = tokens[at].astype(F32) + mods[2:3] * branch[at]
        block_out[at] = jnp.where(keep, middle + mods[5:6] * mlp, 0.0).astype(BF16)
        fold(fold_a, jnp.where(keep, out_grad[at].astype(F32), 0.0) * mlp)

    slabs(rows, SLAB, finish)
    sums[...] = jnp.zeros_like(sums)
    sums[0:1] = jnp.sum(fold_a[...], axis=0, keepdims=True)


def pair_grads(left, right, ordered_after=(), row_block=288):
    _, rows, depth = left.shape
    cols = right.shape[1]
    n_dep = len(ordered_after)

    def kernel(keep_l, send_l, right_ref, *rest):
        keep, send = rest[n_dep:]
        send[...] = dot_nn(send_l[0], right_ref[...]).astype(BF16)
        keep[...] = dot_nn(keep_l[0], right_ref[...]).astype(BF16)

    col_block = WIDE * 5 if cols > D else cols
    col_block = cols // 4 if cols > D else cols
    grid = (cols // col_block, rows // row_block)
    return pl.pallas_call(
        kernel,
        grid=grid,
        out_shape=[jax.ShapeDtypeStruct((rows, cols), BF16)] * 2,
        in_specs=[
            pl.BlockSpec((1, row_block, depth), lambda j, i: (0, i, 0)),
            pl.BlockSpec((1, row_block, depth), lambda j, i: (1, i, 0)),
            pl.BlockSpec((depth, col_block), lambda j, i: (0, j)),
        ]
        + [any_spec()] * n_dep,
        out_specs=[pl.BlockSpec((row_block, col_block), lambda j, i: (i, j))] * 2,
        compiler_params=pltpu.CompilerParams(vmem_limit_bytes=40 * 2**20),
        cost_estimate=pl.CostEstimate(flops=1000, bytes_accessed=1000, transcendentals=0),
    )(left, left, right, *ordered_after)


def up_grads(place, left, right, ordered_after=()):
    depth, cols = right.shape
    size = left.shape[0] // 16
    n_dep = len(ordered_after)

    def kernel(place_ref, keep_l, send_l, right_ref, *rest):
        keep, send = rest[n_dep:]
        send[0] = dot_nn(send_l[...], right_ref[...]).astype(BF16)
        keep[0] = dot_nn(keep_l[...], right_ref[...]).astype(BF16)

    def index(dc):
        def block(i, place_ref):
            yy = (place_ref[1] + i // 4) % 2
            return ((i % 4 * 2 + yy) * 2 + (place_ref[2] + dc) % 2, 0)

        return block

    return pl.pallas_call(
        kernel,
        out_shape=[jax.ShapeDtypeStruct((8, size, cols), BF16)] * 2,
        grid_spec=pltpu.PrefetchScalarGridSpec(
            num_scalar_prefetch=1,
            grid=(8,),
            in_specs=[
                pl.BlockSpec((size, depth), index(0)),
                pl.BlockSpec((size, depth), index(1)),
                pl.BlockSpec((depth, cols), lambda i, place_ref: (0, 0)),
            ]
            + [any_spec()] * n_dep,
            out_specs=[pl.BlockSpec((1, size, cols), lambda i, place_ref: (i, 0, 0))] * 2,
        ),
        compiler_params=pltpu.CompilerParams(vmem_limit_bytes=40 * 2**20),
        cost_estimate=pl.CostEstimate(flops=1000, bytes_accessed=1000, transcendentals=0),
    )(place, left, left, right, *ordered_after)


def flat_mesh(mesh):
    n_dp, n_cond = mesh.shape["dp"], mesh.shape["cond"]
    return Mesh(mesh.devices.reshape(n_dp // 4, 2, 2, n_cond), ("z", "y", "c", "x"))


def swap(value, axis):
    return lax.ppermute(value, axis, [(0, 1), (1, 0)])


def sum_all(value):
    for axis in ("c", "x", "y"):
        value = value + swap(value, axis)
    for step in (1, 2):
        value = value + lax.ppermute(value, "z", [(i, i ^ step) for i in range(4)])
    return value


def add_low(*terms):
    total = terms[0].astype(F32)
    for term in terms[1:]:
        total = total + term.astype(F32)
    return total.astype(BF16)


def gather_pieces(early, late, flag_early, flag_late, axis, cut, x):
    first = x == 0
    near_late, far_late = jnp.where(first, late[0], late[1]), jnp.where(first, late[1], late[0])
    flag = jnp.concatenate(
        [
            jnp.broadcast_to(flag_early, early.shape),
            jnp.broadcast_to(jnp.where(first, flag_late[0], flag_late[1]), near_late.shape),
        ],
        axis=axis,
    )
    got = swap(jnp.concatenate([early, far_late], axis=axis), "x")
    mine = jnp.where(flag, jnp.concatenate([early, near_late], axis=axis), got)
    near = lax.all_gather(mine, "z", axis=0, tiled=False)
    far = swap(near, "y")
    pieces = [near, swap(cut(near), "x"), far, swap(cut(far), "x")]
    return pieces + [swap(piece, "c") for piece in pieces]


def split_sum(keep, send, cut, x):
    got = swap(send, "c")
    first = x == 0
    (ke, k0, k1), (ge, g0, g1) = cut(keep), cut(got)
    late_send = add_low(jnp.where(first, k1, k0), jnp.where(first, g1, g0))
    late_got = swap(late_send, "x")
    kl, gl = jnp.where(first, k0, k1), jnp.where(first, g0, g1)
    early = [add_low(ke[i], ge[i]) for i in range(2)]
    late = [add_low(kl[i], gl[i], late_got[i]) for i in range(2)]
    return early, late


def over_y(halves):
    return add_low(halves[0], swap(halves[1], "y"))


def over_z(value):
    flat = value.reshape(value.shape[0] * value.shape[1], -1)
    part = lax.psum_scatter(flat, "z", scatter_dimension=0, tiled=True)
    return part.reshape(value.shape[1:])


def on_grid(inputs, out_grad, frame_counts, timesteps, labels, owners, *matrices):
    masters, means, squares = matrices[:7], matrices[7:14], matrices[14:]
    z, y, c, x = (lax.axis_index(axis) for axis in ("z", "y", "c", "x"))
    block = (z * 2 + y) * 2 + c
    device = block * 2 + x
    positions, frames, width = inputs.shape
    rows = positions * frames
    span = width // 16
    clips = timesteps.shape[0]
    clip_index = device * positions // PATCHES
    frame_count = lax.dynamic_index_in_dim(frame_counts, clip_index, 0, keepdims=False)
    place = jnp.stack([z, y, c, x, frame_count, z, z, z]).astype(jnp.int32)
    own = [owners[number] == x for number in range(7)]
    own_low = [master[0].T.astype(BF16) for master in masters]

    attend_t, merge_t, up_t, down_t = own_low[3:]
    tiles = attend_t.reshape(3, span, width)
    flags = jnp.stack([own[3], own[4]])[:, None, None]
    firsts = gather_pieces(
        jnp.stack([tiles[0], merge_t]),
        (tiles[1:2], tiles[2:3]),
        flags,
        (own[3], own[3]),
        0,
        lambda main: main[:, 2],
        x,
    )
    ups = gather_pieces(
        up_t[:UP_E],
        (up_t[UP_E : UP_E + UP_L], up_t[UP_E + UP_L :]),
        own[5],
        (own[5], own[5]),
        0,
        lambda main: main[:, UP_E:],
        x,
    )
    downs = gather_pieces(
        down_t[:, :DOWN_E],
        (down_t[:, DOWN_E : DOWN_E + DOWN_L], down_t[:, DOWN_E + DOWN_L :]),
        own[6],
        (own[6], own[6]),
        1,
        lambda main: main[:, :, DOWN_E:],
        x,
    )

    features = timestep_features(timesteps).astype(BF16)
    one_hot = (labels[:, None] == jnp.arange(LABELS)[None, :]).astype(BF16)
    time_part = jnp.where(own[0], contract_cols(features, own_low[0]), 0.0)
    table_part = jnp.where(own[1], contract_cols(one_hot, own_low[1]), 0.0)
    parts = lax.dynamic_update_slice_in_dim(
        jnp.zeros((2, clips, width), F32), jnp.stack([time_part, table_part]), block * span, 2
    )
    parts = sum_all(parts)
    time_pre = parts[0]
    cond_vec = parts[1] + jax.nn.silu(time_pre)
    cond_act, silu_back = jax.vjp(jax.nn.silu, cond_vec)
    cond_act = cond_act.astype(BF16)
    mod_part = jnp.where(own[2], contract_cols(cond_act, own_low[2]), 0.0)
    mod_span = mod_part.shape[1]
    modulation = sum_all(
        lax.dynamic_update_slice_in_dim(
            jnp.zeros((clips, 6 * width), F32), mod_part, block * mod_span, 1
        )
    )
    mod_row = lax.dynamic_index_in_dim(modulation, clip_index, 0, keepdims=False)
    mods = jnp.concatenate([mod_row.reshape(6, width), jnp.zeros((2, width), F32)])

    tokens = inputs.reshape(rows, width)
    grad_out = out_grad.reshape(rows, width)
    spot = (place, smem_spec())
    whole = vmem_spec()
    in_vmem = lambda *arrays: [(array, whole) for array in arrays]
    in_place = lambda arrays: [(array, any_spec()) for array in arrays]
    sems = lambda count: pltpu.SemaphoreType.DMA((count,))
    d_mlp, d_mlp_rel = run_kernel(
        start_back_kernel,
        [spot] + in_vmem(grad_out, mods),
        [((rows, width), BF16), ((2, 8, span, rows), BF16)],
        [vmem(width, rows, dtype=F32)],
    )
    h1, qkv, attended, branch, h2 = run_kernel(
        first_half_kernel,
        [spot] + in_vmem(tokens, mods) + in_place(firsts),
        [
            ((rows, width), BF16),
            ((48, span, rows), BF16),
            ((rows, width), BF16),
            ((rows, width), F32),
            ((rows, width), BF16),
        ],
        [
            vmem(48, span, width),
            vmem(16, span, width),
            vmem(16, span, rows, dtype=F32),
            sems(64),
        ],
    )
    act, slope = run_kernel(
        up_kernel,
        [spot] + in_vmem(h2) + in_place(ups),
        [((rows, FF), BF16)] * 2,
        [vmem(FF, width), vmem(rows, WIDE, dtype=F32), sems(48)],
    )
    down_keep, down_send = pair_grads(d_mlp_rel.reshape(2, 8 * span, rows), act)
    cut_down = lambda v: (
        v[..., :DOWN_E],
        v[..., DOWN_E : DOWN_E + DOWN_L],
        v[..., DOWN_E + DOWN_L :],
    )
    shape = (2, 4, span, FF)
    early, late = split_sum(down_keep.reshape(shape), down_send.reshape(shape), cut_down, x)
    down_part = over_z(jnp.concatenate([over_y(early), over_y(late)], axis=-1))
    down_got = swap(down_part, "x")

    d_upper, d_upper_t = run_kernel(
        d_upper_kernel,
        [spot] + in_vmem(d_mlp, slope) + in_place(downs),
        [((rows, FF), BF16), ((FF, rows), BF16)],
        [vmem(16, span, FF), vmem(rows, WIDE, dtype=F32), sems(48)],
    )
    up_keep, up_send = up_grads(place, d_upper_t, h2)
    cut_up = lambda v: (v[:, :, :UP_E], v[:, :, UP_E : UP_E + UP_L], v[:, :, UP_E + UP_L :])
    shape = (2, 4, 4 * span, width)
    early, late = split_sum(up_keep.reshape(shape), up_send.reshape(shape), cut_up, x)
    up_total = jnp.concatenate([over_y(early), over_y(late)], axis=1)
    up_total, _ = lax.optimization_barrier((up_total, down_part))
    up_part = over_z(up_total)
    up_got = swap(up_part, "x")

    d_middle, d_branch, d_branch_rel, d_att, sums_two = run_kernel(
        middle_back_kernel,
        [spot] + in_vmem(d_upper, tokens, grad_out, branch, mods) + in_place(ups + firsts),
        [
            ((rows, width), F32),
            ((rows, width), BF16),
            ((2, 8, span, rows), BF16),
            ((16, span, rows), BF16),
            ((8, width), F32),
        ],
        [
            vmem(FF, width),
            vmem(16, span, width),
            vmem(rows, width, dtype=F32),
            vmem(width, rows, dtype=F32),
        ]
        + [vmem(8, width, dtype=F32)] * 3
        + [sems(64)],
    )
    merge_keep, merge_send = pair_grads(d_branch_rel.reshape(2, 8 * span, rows), attended)
    shape = (2, 4, span, width)
    merge_keep = merge_keep.reshape(shape)
    merge_got = swap(merge_send.reshape(shape), "c")
    merge_total = over_y([add_low(merge_keep[i], merge_got[i]) for i in range(2)])

    d_qkv, d_qkv_rel = run_kernel(
        attend_back_kernel,
        [spot] + in_vmem(qkv, d_att),
        [((rows, 3 * width), BF16), ((2, 8, 3, span, rows), BF16)],
        [vmem(16, span, rows, dtype=F32)] * 3,
    )
    attend_keep, attend_send = pair_grads(d_qkv_rel.reshape(2, 24 * span, rows), h1)
    cut_attend = lambda v: (v[:, :, 0], v[:, :, 1], v[:, :, 2])
    shape = (2, 4, 3, span, width)
    early, late = split_sum(attend_keep.reshape(shape), attend_send.reshape(shape), cut_attend, x)
    first_total = jnp.concatenate([over_y(early), merge_total, over_y(late)], axis=2)
    first_total, _ = lax.optimization_barrier((first_total, up_part))
    first_part = over_z(first_total).reshape(span, 3, width).transpose(1, 0, 2)
    first_got = swap(first_part, "x")

    input_grad, sums_one = run_kernel(
        input_back_kernel,
        [spot] + in_vmem(d_qkv, tokens, d_middle, mods) + in_place(firsts),
        [((rows, width), BF16), ((8, width), F32)],
        [vmem(48, span, width), vmem(rows, width, dtype=F32)]
        + [vmem(8, width, dtype=F32)] * 2
        + [sems(48)],
    )
    block_out, sums_out = run_kernel(
        output_kernel,
        [spot] + in_vmem(act, tokens, branch, grad_out, mods) + in_place(downs),
        [((rows, width), BF16), ((8, width), F32)],
        [
            vmem(16, span, FF),
            vmem(rows, width, dtype=F32),
            vmem(8, width, dtype=F32),
            sems(48),
        ],
    )

    d_vector = jnp.concatenate([sums_one[:2], sums_two[:3], sums_out[:1]]).reshape(6 * width)
    clip_pick = (jnp.arange(clips) == clip_index).astype(F32)
    d_mod = sum_all(clip_pick[:, None] * d_vector[None, :])
    d_mod = lax.dynamic_slice_in_dim(d_mod, block * mod_span, mod_span, 1)
    grad_mod = contract_rows(d_mod, cond_act.astype(F32), HIGHEST)
    d_cond_part = jnp.dot(
        d_mod, own_low[2].astype(F32), precision=HIGHEST, preferred_element_type=F32
    )
    d_cond_act = sum_all(jnp.where(own[2], d_cond_part, 0.0))
    d_cond = silu_back(d_cond_act)[0]
    d_time_pre = jax.vjp(jax.nn.silu, time_pre)[1](d_cond)[0]
    d_cond_block = lax.dynamic_slice_in_dim(d_cond, block * span, span, 1)
    d_time_block = lax.dynamic_slice_in_dim(d_time_pre, block * span, span, 1)
    grad_table = contract_rows(d_cond_block, one_hot.astype(F32), HIGHEST)
    grad_time = contract_rows(d_time_block, features.astype(F32), HIGHEST)

    def joined(early, part, got, axis):
        first = x == 0
        halves = [jnp.where(first, part, got), jnp.where(first, got, part)]
        return jnp.concatenate([early.astype(BF16)] + halves, axis=axis).astype(F32)

    def both(part, got):
        return part.astype(F32) + got.astype(F32)

    grads = (
        grad_time,
        grad_table,
        grad_mod,
        jnp.concatenate(
            [
                both(first_part[0], first_got[0]),
                jnp.where(x == 0, first_part[2], first_got[2]).astype(F32),
                jnp.where(x == 0, first_got[2], first_part[2]).astype(F32),
            ]
        ),
        both(first_part[1], first_got[1]),
        jnp.concatenate(
            [
                both(up_part[:UP_E], up_got[:UP_E]),
                jnp.where(x == 0, up_part[UP_E:], up_got[UP_E:]).astype(F32),
                jnp.where(x == 0, up_got[UP_E:], up_part[UP_E:]).astype(F32),
            ]
        ),
        jnp.concatenate(
            [
                both(down_part[:, :DOWN_E], down_got[:, :DOWN_E]),
                jnp.where(x == 0, down_part[:, DOWN_E:], down_got[:, DOWN_E:]).astype(F32),
                jnp.where(x == 0, down_got[:, DOWN_E:], down_part[:, DOWN_E:]).astype(F32),
            ],
            axis=1,
        ),
    )
    rates = [
        0.5 * FREQ ** (-0.5),
        0.5,
        0.5 * D ** (-0.5),
        0.5 * D ** (-0.5),
        D ** (-0.5),
        0.5 * D ** (-0.5),
        0.5 * FF ** (-0.5),
    ]
    new_list, first_list, second_list, copy_list = ([], [], [], [])
    for number in range(7):
        fresh, mean, square = adamw_step(
            masters[number][0].T,
            means[number][0].T,
            squares[number][0].T,
            grads[number],
            rates[number],
        )
        fresh = jnp.where(own[number], fresh, 0.0).T[None]
        new_list.append(fresh)
        first_list.append(jnp.where(own[number], mean, 0.0).T[None])
        second_list.append(jnp.where(own[number], square, 0.0).T[None])
        copy_list.append(fresh.astype(BF16))
    return (
        block_out.reshape(inputs.shape),
        input_grad.reshape(inputs.shape),
        *new_list,
        *first_list,
        *second_list,
        *copy_list,
    )


def on_device(
    inputs,
    out_grad,
    frame_counts,
    timesteps,
    labels,
    owners,
    w_time,
    w_table,
    w_modulate,
    w_attend,
    w_merge,
    w_up,
    w_down,
    mean_time,
    mean_table,
    mean_modulate,
    mean_attend,
    mean_merge,
    mean_up,
    mean_down,
    square_time,
    square_table,
    square_modulate,
    square_attend,
    square_merge,
    square_up,
    square_down,
):
    masters = (w_time, w_table, w_modulate, w_attend, w_merge, w_up, w_down)
    means = (mean_time, mean_table, mean_modulate, mean_attend, mean_merge, mean_up, mean_down)
    squares = (
        square_time,
        square_table,
        square_modulate,
        square_attend,
        square_merge,
        square_up,
        square_down,
    )
    n_dp = lax.axis_size("dp")
    n_cond = lax.axis_size("cond")
    cond_index = lax.axis_index("cond")
    dp_index = lax.axis_index("dp")
    device = dp_index * n_cond + cond_index
    positions, frames, width = inputs.shape
    clips = timesteps.shape[0]
    clip_index = device * positions // PATCHES
    frame_count = lax.dynamic_index_in_dim(frame_counts, clip_index, 0, keepdims=False)
    both = (
        lax.all_gather(w_time.astype(jnp.bfloat16), "cond", axis=0, tiled=True),
        lax.all_gather(w_table.astype(jnp.bfloat16), "cond", axis=0, tiled=True),
        lax.all_gather(w_modulate.astype(jnp.bfloat16), "cond", axis=0, tiled=True),
        lax.all_gather(w_attend.astype(jnp.bfloat16), "cond", axis=0, tiled=True),
        lax.all_gather(w_merge.astype(jnp.bfloat16), "cond", axis=0, tiled=True),
        lax.all_gather(w_up.astype(jnp.bfloat16), "cond", axis=0, tiled=True),
        lax.all_gather(w_down.astype(jnp.bfloat16), "cond", axis=0, tiled=True),
    )
    owned = [
        lax.dynamic_index_in_dim(pair, owners[number], 0, keepdims=False)
        for number, pair in enumerate(both)
    ]
    time_w, table_w, attend_w, merge_w, up_w, down_w = (
        lax.all_gather(owned[0], "dp", axis=1, tiled=True),
        lax.all_gather(owned[1], "dp", axis=1, tiled=True),
        lax.all_gather(owned[3], "dp", axis=1, tiled=True),
        lax.all_gather(owned[4], "dp", axis=1, tiled=True),
        lax.all_gather(owned[5], "dp", axis=1, tiled=True),
        lax.all_gather(owned[6], "dp", axis=1, tiled=True),
    )
    half_width = owned[2].shape[1] // n_cond
    modulate_half = lax.dynamic_slice_in_dim(owned[2], cond_index * half_width, half_width, 1)
    features = timestep_features(timesteps).astype(jnp.bfloat16)
    time_pre = jnp.dot(features, time_w, preferred_element_type=jnp.float32)
    one_hot = (labels[:, None] == jnp.arange(LABELS)[None, :]).astype(jnp.bfloat16)
    cond_vec = jnp.dot(one_hot, table_w, preferred_element_type=jnp.float32) + jax.nn.silu(time_pre)
    cond_act, silu_back = jax.vjp(jax.nn.silu, cond_vec)
    cond_act = cond_act.astype(jnp.bfloat16)
    mod_part = jnp.dot(cond_act, modulate_half, preferred_element_type=jnp.float32)
    modulation = lax.all_gather(mod_part, ("dp", "cond"), axis=1, tiled=True)
    mod_row = lax.dynamic_index_in_dim(modulation, clip_index, 0, keepdims=False)
    shift_one, scale_one, gate_one, shift_two, scale_two, gate_two = [
        mod_row[part * width : (part + 1) * width] for part in range(6)
    ]
    rows = positions * frames
    tokens = inputs.reshape(rows, width).astype(jnp.float32)
    frame_ids = jnp.tile(jnp.arange(frames), positions)
    row_mask = (frame_ids < frame_count).astype(jnp.float32)[:, None]
    key_valid = jnp.arange(frames) < frame_count
    inv_scale = 1.0 / math.sqrt(HEAD)
    norm_one, rstd_one = normalize(tokens)
    hidden_one = (norm_one * (1.0 + scale_one) + shift_one).astype(jnp.bfloat16)
    qkv = jnp.dot(hidden_one, attend_w, preferred_element_type=jnp.float32).astype(jnp.bfloat16)
    queries = qkv[:, :width].reshape(positions, frames, HEADS, HEAD)
    key_rows = qkv[:, width : 2 * width].reshape(positions, frames, HEADS, HEAD)
    value_rows = qkv[:, 2 * width :].reshape(positions, frames, HEADS, HEAD)
    scores = (
        jnp.einsum("pfhe,pghe->phfg", queries, key_rows, preferred_element_type=jnp.float32)
        * inv_scale
    )
    scores = jnp.where(key_valid[None, None, None, :], scores, -1e30)
    top = jnp.max(scores, axis=-1, keepdims=True)
    expo = jnp.exp(scores - top)
    probs = expo / jnp.sum(expo, axis=-1, keepdims=True)
    probs_low = probs.astype(jnp.bfloat16)
    attended = jnp.einsum(
        "phfg,pghe->pfhe", probs_low, value_rows, preferred_element_type=jnp.float32
    )
    attended = attended.reshape(rows, width).astype(jnp.bfloat16)
    branch = jnp.dot(attended, merge_w, preferred_element_type=jnp.float32)
    middle = tokens + gate_one * branch
    norm_two, rstd_two = normalize(middle)
    hidden_two = (norm_two * (1.0 + scale_two) + shift_two).astype(jnp.bfloat16)
    upper = jnp.dot(hidden_two, up_w, preferred_element_type=jnp.float32)
    activ, gelu_back = jax.vjp(partial(jax.nn.gelu, approximate=True), upper)
    activ = activ.astype(jnp.bfloat16)
    mlp_out = jnp.dot(activ, down_w, preferred_element_type=jnp.float32)
    block_out = (
        (row_mask * (middle + gate_two * mlp_out))
        .reshape(positions, frames, width)
        .astype(jnp.bfloat16)
    )
    attend_b, merge_b, up_b, down_b = (
        lax.all_gather(owned[3], "dp", axis=1, tiled=True),
        lax.all_gather(owned[4], "dp", axis=1, tiled=True),
        lax.all_gather(owned[5], "dp", axis=1, tiled=True),
        lax.all_gather(owned[6], "dp", axis=1, tiled=True),
    )
    grad_out = out_grad.reshape(rows, width).astype(jnp.float32) * row_mask
    d_mlp = (grad_out * gate_two).astype(jnp.bfloat16)
    grad_down = contract_rows(activ, d_mlp)
    d_activ = contract_cols(d_mlp, down_b)
    d_upper = gelu_back(d_activ)[0].astype(jnp.bfloat16)
    grad_up = contract_rows(hidden_two, d_upper)
    d_hidden_two = contract_cols(d_upper, up_b)
    d_middle = grad_out + normalize_back(d_hidden_two * (1.0 + scale_two), norm_two, rstd_two)
    d_branch = (d_middle * gate_one).astype(jnp.bfloat16)
    grad_merge = contract_rows(attended, d_branch)
    d_attended = (
        contract_cols(d_branch, merge_b)
        .astype(jnp.bfloat16)
        .reshape(positions, frames, HEADS, HEAD)
    )
    d_probs = jnp.einsum(
        "pfhe,pghe->phfg", d_attended, value_rows, preferred_element_type=jnp.float32
    )
    d_values = jnp.einsum(
        "phfg,pfhe->pghe", probs_low, d_attended, preferred_element_type=jnp.float32
    )
    d_scores = (probs * (d_probs - jnp.sum(probs * d_probs, axis=-1, keepdims=True))).astype(
        jnp.bfloat16
    )
    d_queries = (
        jnp.einsum("phfg,pghe->pfhe", d_scores, key_rows, preferred_element_type=jnp.float32)
        * inv_scale
    )
    d_keys = (
        jnp.einsum("phfg,pfhe->pghe", d_scores, queries, preferred_element_type=jnp.float32)
        * inv_scale
    )
    d_qkv = jnp.concatenate(
        [
            d_queries.reshape(rows, width),
            d_keys.reshape(rows, width),
            d_values.reshape(rows, width),
        ],
        axis=1,
    ).astype(jnp.bfloat16)
    grad_attend = contract_rows(hidden_one, d_qkv)
    d_hidden_one = contract_cols(d_qkv, attend_b)
    d_tokens = d_middle + normalize_back(d_hidden_one * (1.0 + scale_one), norm_one, rstd_one)
    input_grad = d_tokens.reshape(positions, frames, width).astype(jnp.bfloat16)
    d_vector = jnp.concatenate(
        [
            jnp.sum(d_hidden_one, axis=0),
            jnp.sum(d_hidden_one * norm_one, axis=0),
            jnp.sum(d_middle * branch, axis=0),
            jnp.sum(d_hidden_two, axis=0),
            jnp.sum(d_hidden_two * norm_two, axis=0),
            jnp.sum(grad_out * mlp_out, axis=0),
        ]
    )
    clip_pick = (jnp.arange(clips) == clip_index).astype(jnp.float32)
    d_mod_local = clip_pick[:, None] * d_vector[None, :]
    d_mod_half = lax.psum_scatter(d_mod_local, ("dp", "cond"), scatter_dimension=1, tiled=True)
    grad_mod_half = contract_rows(cond_act.astype(jnp.float32), d_mod_half, HIGHEST)
    d_cond_part = contract_cols(d_mod_half, modulate_half.astype(jnp.float32), HIGHEST)
    d_cond_act = lax.psum(d_cond_part, ("dp", "cond"))
    d_cond = silu_back(d_cond_act)[0]
    grad_table = contract_rows(one_hot.astype(jnp.float32), d_cond, HIGHEST)
    d_time_pre = jax.vjp(jax.nn.silu, time_pre)[1](d_cond)[0]
    grad_time = contract_rows(features.astype(jnp.float32), d_time_pre, HIGHEST)
    span = width // n_dp
    grad_time_block = lax.dynamic_slice_in_dim(grad_time, dp_index * span, span, 1)
    grad_table_block = lax.dynamic_slice_in_dim(grad_table, dp_index * span, span, 1)
    blocks = (
        lax.psum_scatter(grad_attend, "dp", scatter_dimension=1, tiled=True),
        lax.psum_scatter(grad_merge, "dp", scatter_dimension=1, tiled=True),
        lax.psum_scatter(grad_up, "dp", scatter_dimension=1, tiled=True),
        lax.psum_scatter(grad_down, "dp", scatter_dimension=1, tiled=True),
    )
    placed = lax.dynamic_update_slice_in_dim(
        jnp.zeros((width, half_width * n_cond), jnp.float32),
        grad_mod_half,
        cond_index * half_width,
        1,
    )
    row_halves = (
        lax.psum_scatter(
            blocks[0].astype(jnp.bfloat16), "cond", scatter_dimension=0, tiled=True
        ).astype(jnp.float32),
        lax.psum_scatter(
            blocks[1].astype(jnp.bfloat16), "cond", scatter_dimension=0, tiled=True
        ).astype(jnp.float32),
        lax.psum_scatter(
            blocks[2].astype(jnp.bfloat16), "cond", scatter_dimension=0, tiled=True
        ).astype(jnp.float32),
        lax.psum_scatter(
            blocks[3].astype(jnp.bfloat16), "cond", scatter_dimension=0, tiled=True
        ).astype(jnp.float32),
        lax.psum_scatter(
            placed.astype(jnp.bfloat16), "cond", scatter_dimension=0, tiled=True
        ).astype(jnp.float32),
    )
    joined = (
        lax.all_gather(row_halves[0].astype(jnp.bfloat16), "cond", axis=0, tiled=True).astype(
            jnp.float32
        ),
        lax.all_gather(row_halves[1].astype(jnp.bfloat16), "cond", axis=0, tiled=True).astype(
            jnp.float32
        ),
        lax.all_gather(row_halves[2].astype(jnp.bfloat16), "cond", axis=0, tiled=True).astype(
            jnp.float32
        ),
        lax.all_gather(row_halves[3].astype(jnp.bfloat16), "cond", axis=0, tiled=True).astype(
            jnp.float32
        ),
        lax.all_gather(row_halves[4].astype(jnp.bfloat16), "cond", axis=0, tiled=True).astype(
            jnp.float32
        ),
    )
    grads = (
        grad_time_block,
        grad_table_block,
        joined[4],
        joined[0],
        joined[1],
        joined[2],
        joined[3],
    )
    rates = [
        0.5 * FREQ ** (-0.5),
        0.5,
        0.5 * D ** (-0.5),
        0.5 * D ** (-0.5),
        D ** (-0.5),
        0.5 * D ** (-0.5),
        0.5 * FF ** (-0.5),
    ]
    new_list, first_list, second_list, copy_list = ([], [], [], [])
    for number in range(7):
        fresh, first, second = adamw_step(
            masters[number][0], means[number][0], squares[number][0], grads[number], rates[number]
        )
        is_owner = cond_index == owners[number]
        fresh = jnp.where(is_owner, fresh, 0.0)[None]
        new_list.append(fresh)
        first_list.append(jnp.where(is_owner, first, 0.0)[None])
        second_list.append(jnp.where(is_owner, second, 0.0)[None])
        copy_list.append(fresh.astype(jnp.bfloat16))
    return (block_out, input_grad, *new_list, *first_list, *second_list, *copy_list)


def solution(mesh):
    n_dp, n_cond = mesh.shape["dp"], mesh.shape["cond"]
    if (n_dp, n_cond) == (16, 2):
        token_spec = P(("z", "y", "c", "x"), None, None)
        matrix_spec = P("x", None, ("z", "y", "c"))
        return jax.shard_map(
            on_grid,
            mesh=flat_mesh(mesh),
            in_specs=(token_spec,) * 2 + (P(),) * 4 + (matrix_spec,) * 21,
            out_specs=(token_spec,) * 2 + (matrix_spec,) * 28,
            check_vma=False,
        )
    token_spec = P(("dp", "cond"), None, None)
    matrix_spec = P("cond", None, "dp")
    return jax.shard_map(
        on_device,
        mesh=mesh,
        in_specs=(token_spec,) * 2 + (P(),) * 4 + (matrix_spec,) * 21,
        out_specs=(token_spec,) * 2 + (matrix_spec,) * 28,
        check_vma=False,
    )
```

```python
from functools import partial
import math

import jax
import jax.numpy as jnp
from jax import lax
from jax.experimental import pallas as pl
from jax.experimental.pallas import tpu as pltpu
from jax.sharding import Mesh, PartitionSpec as P

D = 1152
HEADS = 16
HEAD = 72
FF = 4608
FREQ = 256
LABELS = 101
FRAMES = 16
PATCHES = 256
STEP = 5


HIGHEST = lax.Precision.HIGHEST
EPSILON = 1e-06


def contract_rows(left, right, precision=None):
    return lax.dot_general(
        left,
        right,
        (((0,), (0,)), ((), ())),
        precision=precision,
        preferred_element_type=jnp.float32,
    )


def contract_cols(left, right, precision=None):
    return lax.dot_general(
        left,
        right,
        (((1,), (1,)), ((), ())),
        precision=precision,
        preferred_element_type=jnp.float32,
    )


def normalize(values):
    centre = values - jnp.mean(values, axis=-1, keepdims=True)
    spread = lax.rsqrt(jnp.mean(centre * centre, axis=-1, keepdims=True) + EPSILON)
    return (centre * spread, spread)


def normalize_back(upstream, normed, spread):
    return spread * (
        upstream
        - jnp.mean(upstream, axis=-1, keepdims=True)
        - normed * jnp.mean(upstream * normed, axis=-1, keepdims=True)
    )


def timestep_features(timesteps):
    half_count = FREQ // 2
    freqs = jnp.exp(-math.log(10000.0) * jnp.arange(half_count, dtype=jnp.float32) / half_count)
    angles = timesteps.astype(jnp.float32)[:, None] * freqs[None, :]
    return jnp.concatenate([jnp.cos(angles), jnp.sin(angles)], axis=1)


def adamw_step(master, first, second, grad, rate):
    first_new = 0.5 * first + 0.5 * grad
    second_new = 0.5 * second + 0.5 * grad * grad
    correct = 1.0 - 0.5**STEP
    update = first_new / correct / (jnp.sqrt(second_new / correct) + 1e-08)
    return (master - rate * (update + 0.01 * master), first_new, second_new)


BF16, F32 = jnp.bfloat16, jnp.float32
SLAB = 16
COST_FLOPS, COST_BYTES = 6e9, 18e6
GROUP = 128
WIDE = 256


def vmem(*shape, dtype=BF16):
    return pltpu.VMEM(shape, dtype)


def any_spec():
    return pl.BlockSpec(memory_space=pl.ANY)


def smem_spec():
    return pl.BlockSpec(memory_space=pltpu.SMEM)


def vmem_spec():
    return pl.BlockSpec(memory_space=pltpu.VMEM)


def dot_nn(left, right):
    return lax.dot_general(left, right, (((1,), (0,)), ((), ())), preferred_element_type=F32)


def dot_nt(left, right):
    return lax.dot_general(left, right, (((1,), (1,)), ((), ())), preferred_element_type=F32)


def cost(us):
    return pl.CostEstimate(flops=int(us * COST_FLOPS), bytes_accessed=int(us * COST_BYTES), transcendentals=0)


def run_kernel(body, operands, outs, scratch, us, ordered_after=(), mib=56, **kw):
    arrays = [array for array, _ in operands] + list(ordered_after)
    specs = [spec for _, spec in operands] + [any_spec() for _ in ordered_after]
    n_in, n_dep = len(operands), len(ordered_after)

    def kernel(*refs):
        body(*refs[:n_in], *refs[n_in + n_dep :])

    return pl.pallas_call(
        kernel,
        out_shape=[jax.ShapeDtypeStruct(shape, dtype) for shape, dtype in outs],
        in_specs=specs,
        out_specs=[vmem_spec() for _ in outs],
        scratch_shapes=scratch,
        compiler_params=pltpu.CompilerParams(vmem_limit_bytes=mib * 2**20),
        cost_estimate=cost(us),
        **kw,
    )(*arrays)


PIECES = 8


def block_order(place):
    y, c = place[1], place[2]
    for dc in range(2):
        for dy in range(2):
            yy = y if dy == 0 else 1 - y
            cc = c if dc == 0 else 1 - c
            for zz in range(4):
                yield dc * 4 + dy * 2, zz, (zz * 2 + yy) * 2 + cc


def start_all(copies, sems):
    made = [pltpu.make_async_copy(src, dst, sems.at[i]) for i, (src, dst) in enumerate(copies)]
    for copy in made:
        copy.start()
    return made


def attend_copies(pieces, place, wide):
    x = place[3]
    for at, zz, b in block_order(place):
        main, other = pieces[at : at + 2]
        yield main.at[zz, 0], wide.at[b * 3]
        yield main.at[zz, 2], wide.at[b * 3 + 1 + x]
        yield other.at[zz], wide.at[b * 3 + 2 - x]


def merge_copies(pieces, place, wide):
    for at, zz, b in block_order(place):
        yield pieces[at].at[zz, 1], wide.at[b]


UP_E, UP_L = 128, 80


def up_copies(pieces, place, wide):
    x = place[3]
    size = UP_E + 2 * UP_L
    for at, zz, b in block_order(place):
        main, other = pieces[at : at + 2]
        row = pl.multiple_of(b * size, 16)
        near_row = pl.multiple_of(b * size + UP_E + UP_L * x, 16)
        other_row = pl.multiple_of(b * size + UP_E + UP_L - UP_L * x, 16)
        yield main.at[zz, pl.ds(0, UP_E)], wide.at[pl.ds(row, UP_E)]
        yield main.at[zz, pl.ds(UP_E, UP_L)], wide.at[pl.ds(near_row, UP_L)]
        yield other.at[zz], wide.at[pl.ds(other_row, UP_L)]


DOWN_E, DOWN_L = 2048, 1280


def down_copies(pieces, place, wide):
    x = place[3]
    near_col = pl.multiple_of(DOWN_E + DOWN_L * x, 128)
    other_col = pl.multiple_of(DOWN_E + DOWN_L - DOWN_L * x, 128)
    for at, zz, b in block_order(place):
        main, other = pieces[at : at + 2]
        yield main.at[zz, :, pl.ds(0, DOWN_E)], wide.at[b, :, pl.ds(0, DOWN_E)]
        yield main.at[zz, :, pl.ds(DOWN_E, DOWN_L)], wide.at[b, :, pl.ds(near_col, DOWN_L)]
        yield other.at[zz], wide.at[b, :, pl.ds(other_col, DOWN_L)]


def rows_of(wide, first, count, cols=None):
    value = wide[pl.ds(first, count)] if cols is None else wide[pl.ds(first, count), :, cols]
    return value.astype(F32).reshape(count * HEAD, value.shape[-1]).astype(BF16)


def norm_slab(values):
    mean = jnp.sum(values, axis=1, keepdims=True) * (1.0 / D)
    centre = values - mean
    spread = lax.rsqrt(jnp.sum(centre * centre, axis=1, keepdims=True) * (1.0 / D) + EPSILON)
    return centre * spread, spread


def back_slab(upstream, normed, spread):
    first = jnp.sum(upstream, axis=1, keepdims=True) * (1.0 / D)
    second = jnp.sum(upstream * normed, axis=1, keepdims=True) * (1.0 / D)
    return spread * (upstream - first - normed * second)


def slabs(rows, size, body):
    @pl.loop(0, rows // size)
    def _(i):
        body(pl.ds(pl.multiple_of(i * size, size), size))


def fold(ref, value):
    ref[...] += jnp.sum(value.reshape(value.shape[0] // 8, 8, value.shape[1]), axis=0)


def turn(src, dst):
    @pl.loop(0, src.shape[0] // GROUP)
    def _(i):
        at = pl.ds(pl.multiple_of(i * GROUP, GROUP), GROUP)
        dst[:, at] = src[at].astype(F32).T


def store_relative(ref, turned, y, c):
    for b in range(16):
        zz, yy, cc = b // 4, (b // 2) % 2, b % 2
        dy = y if yy == 0 else 1 - y
        dc = c if cc == 0 else 1 - c
        ref[dc, dy * 4 + zz] = turned[b * HEAD : (b + 1) * HEAD].astype(BF16)


def frame_mask(count):
    keys = lax.broadcasted_iota(jnp.int32, (GROUP, GROUP), 0)
    asks = lax.broadcasted_iota(jnp.int32, (GROUP, GROUP), 1)
    return (keys // FRAMES == asks // FRAMES) & (keys % FRAMES < count)


def probs_of(key, query, mask):
    scores = dot_nn(key.astype(F32).T.astype(BF16), query) * (1.0 / math.sqrt(HEAD))
    scores = jnp.where(mask, scores, -1e30)
    top = jnp.max(scores, axis=0, keepdims=True)
    expo = jnp.where(mask, jnp.exp(scores - top), 0.0)
    return expo / jnp.sum(expo, axis=0, keepdims=True)


def qkv_kernel(place, tokens, mods, *rest):
    pieces, rest = rest[:PIECES], rest[PIECES:]
    h1, qkv, wide, sems = rest
    copies = start_all(list(attend_copies(pieces, place, wide)), sems)

    def norm_one(at):
        normed, _ = norm_slab(tokens[at].astype(F32))
        h1[at] = (normed * (1.0 + mods[1:2]) + mods[0:1]).astype(BF16)

    slabs(tokens.shape[0], SLAB, norm_one)
    for copy in copies:
        copy.wait()

    @pl.loop(0, 12)
    def _(i):
        value = dot_nt(rows_of(wide, i * 4, 4), h1[...])
        for j in range(4):
            qkv[i * 4 + j] = value[j * HEAD : (j + 1) * HEAD].astype(BF16)


def attend_kernel(place, qkv, tokens, mods, *rest):
    pieces, rest = rest[:PIECES], rest[PIECES:]
    attended, branch, h2, merge, turned, sems = rest
    copies = start_all(list(merge_copies(pieces, place, merge)), sems)
    rows = tokens.shape[0]
    mask = frame_mask(place[4])

    @pl.loop(0, HEADS)
    def _(head):
        for group in range(rows // GROUP):
            at = pl.ds(group * GROUP, GROUP)
            probs = probs_of(qkv[HEADS + head, :, at], qkv[head, :, at], mask)
            turned[head, :, at] = dot_nn(qkv[2 * HEADS + head, :, at], probs.astype(BF16))

    for group in range(rows // GROUP):
        at = pl.ds(group * GROUP, GROUP)
        attended[at] = turned[:, :, at].reshape(D, GROUP).T.astype(BF16)
    for copy in copies:
        copy.wait()
    branch[...] = dot_nt(attended[...], rows_of(merge, 0, 16))

    def norm_two(at):
        middle = tokens[at].astype(F32) + mods[2:3] * branch[at]
        normed, _ = norm_slab(middle)
        h2[at] = (normed * (1.0 + mods[4:5]) + mods[3:4]).astype(BF16)

    slabs(rows, SLAB, norm_two)


def up_kernel(place, h2, *rest):
    pieces, rest = rest[:PIECES], rest[PIECES:]
    act, slope, wide, upper, sems = rest
    for copy in start_all(list(up_copies(pieces, place, wide)), sems):
        copy.wait()
    rows = h2.shape[0]
    root = math.sqrt(2.0 / math.pi)

    @pl.loop(0, FF // WIDE)
    def _(i):
        cols = pl.ds(pl.multiple_of(i * WIDE, WIDE), WIDE)
        upper[...] = dot_nt(h2[...], wide[cols])

        def gelu(at):
            u = upper[at]
            square = u * u
            bent = jnp.tanh(root * u * (1.0 + 0.044715 * square))
            half = 0.5 * (1.0 + bent)
            act[at, cols] = (u * half).astype(BF16)
            rise = root * (1.0 + 3.0 * 0.044715 * square)
            slope[at, cols] = (half + 0.5 * u * (1.0 - bent * bent) * rise).astype(BF16)

        slabs(rows, 32, gelu)


def start_back_kernel(place, out_grad, mods, d_mlp, relative, turned):
    rows = out_grad.shape[0]

    def scale(at):
        frame = lax.broadcasted_iota(jnp.int32, (SLAB, 1), 0) % FRAMES
        dy = jnp.where(frame < place[4], out_grad[at].astype(F32), 0.0)
        d_mlp[at] = (dy * mods[5:6]).astype(BF16)

    slabs(rows, SLAB, scale)
    turn(d_mlp, turned)
    store_relative(relative, turned, place[1], place[2])


def d_upper_kernel(place, d_mlp, slope, *rest):
    pieces, rest = rest[:PIECES], rest[PIECES:]
    d_upper, d_upper_t, wide, value, sems = rest
    for copy in start_all(list(down_copies(pieces, place, wide)), sems):
        copy.wait()
    rows = d_mlp.shape[0]

    @pl.loop(0, FF // WIDE)
    def _(i):
        cols = pl.ds(pl.multiple_of(i * WIDE, WIDE), WIDE)
        value[...] = dot_nn(d_mlp[...], rows_of(wide, 0, 16, cols))

        @pl.loop(0, rows // GROUP)
        def _(j):
            at = pl.ds(pl.multiple_of(j * GROUP, GROUP), GROUP)
            part = value[at] * slope[at, cols].astype(F32)
            d_upper[at, cols] = part.astype(BF16)
            d_upper_t[cols, at] = part.T.astype(BF16)


def middle_back_kernel(place, d_upper, tokens, out_grad, branch, mods, *rest):
    ups, firsts, rest = rest[:PIECES], rest[PIECES : 2 * PIECES], rest[2 * PIECES :]
    d_middle, d_branch, relative, d_att, sums, wide, merge, value, turned, fold_a, fold_b, fold_c, sems = rest
    copies = list(up_copies(ups, place, wide)) + list(merge_copies(firsts, place, merge))
    copies = start_all(copies, sems)
    for copy in copies:
        copy.wait()
    rows = tokens.shape[0]
    value[...] = dot_nn(d_upper[...], wide[...])
    for ref in (fold_a, fold_b, fold_c):
        ref[...] = jnp.zeros_like(ref)

    def back(at):
        d_h2 = value[at]
        arm = branch[at]
        normed, spread = norm_slab(tokens[at].astype(F32) + mods[2:3] * arm)
        frame = lax.broadcasted_iota(jnp.int32, (SLAB, 1), 0) % FRAMES
        dy = jnp.where(frame < place[4], out_grad[at].astype(F32), 0.0)
        d_mid = dy + back_slab(d_h2 * (1.0 + mods[4:5]), normed, spread)
        d_middle[at] = d_mid
        d_branch[at] = (d_mid * mods[2:3]).astype(BF16)
        fold(fold_a, d_mid * arm)
        fold(fold_b, d_h2)
        fold(fold_c, d_h2 * normed)

    slabs(rows, SLAB, back)
    sums[...] = jnp.zeros_like(sums)
    sums[0:1] = jnp.sum(fold_a[...], axis=0, keepdims=True)
    sums[1:2] = jnp.sum(fold_b[...], axis=0, keepdims=True)
    sums[2:3] = jnp.sum(fold_c[...], axis=0, keepdims=True)
    turn(d_branch, turned)
    store_relative(relative, turned, place[1], place[2])
    value[...] = dot_nn(d_branch[...], rows_of(merge, 0, 16))
    turn(value, turned)
    for head in range(HEADS):
        d_att[head] = turned[head * HEAD : (head + 1) * HEAD].astype(BF16)


def attend_back_kernel(place, qkv, d_att, d_qkv, relative, d_q, d_k, d_v):
    rows = qkv.shape[2]
    y, c = place[1], place[2]
    mask = frame_mask(place[4])
    scale = 1.0 / math.sqrt(HEAD)

    @pl.loop(0, HEADS)
    def _(head):
        for group in range(rows // GROUP):
            at = pl.ds(group * GROUP, GROUP)
            query, key = qkv[head, :, at], qkv[HEADS + head, :, at]
            val, grad = qkv[2 * HEADS + head, :, at], d_att[head, :, at]
            probs = probs_of(key, query, mask)
            d_probs = dot_nn(val.astype(F32).T.astype(BF16), grad)
            d_v[head, :, at] = dot_nt(grad, probs.astype(BF16))
            inner = jnp.sum(probs * d_probs, axis=0, keepdims=True)
            d_scores = (probs * (d_probs - inner)).astype(BF16)
            d_q[head, :, at] = dot_nn(key, d_scores) * scale
            d_k[head, :, at] = dot_nt(query, d_scores) * scale

    for part, ref in enumerate((d_q, d_k, d_v)):
        for group in range(rows // GROUP):
            at = pl.ds(group * GROUP, GROUP)
            d_qkv[at, part * D : (part + 1) * D] = ref[:, :, at].reshape(D, GROUP).T.astype(BF16)
        for head in range(HEADS):
            number = part * HEADS + head
            b, tile = number // 3, number % 3
            zz, yy, cc = b // 4, (b // 2) % 2, b % 2
            dy = y if yy == 0 else 1 - y
            dc = c if cc == 0 else 1 - c
            relative[dc, dy * 4 + zz, tile] = ref[head].astype(BF16)


def input_back_kernel(place, d_qkv, tokens, d_middle, mods, *rest):
    pieces, rest = rest[:PIECES], rest[PIECES:]
    input_grad, sums, wide, value, fold_a, fold_b, sems = rest
    for copy in start_all(list(attend_copies(pieces, place, wide)), sems):
        copy.wait()
    rows = tokens.shape[0]
    for part in range(3):
        add = dot_nn(d_qkv[:, part * D : (part + 1) * D], rows_of(wide, part * 16, 16))
        if part == 0:
            value[...] = add
        else:
            value[...] += add
    for ref in (fold_a, fold_b):
        ref[...] = jnp.zeros_like(ref)

    def back(at):
        d_h1 = value[at]
        normed, spread = norm_slab(tokens[at].astype(F32))
        d_token = d_middle[at] + back_slab(d_h1 * (1.0 + mods[1:2]), normed, spread)
        input_grad[at] = d_token.astype(BF16)
        fold(fold_a, d_h1)
        fold(fold_b, d_h1 * normed)

    slabs(rows, SLAB, back)
    sums[...] = jnp.zeros_like(sums)
    sums[0:1] = jnp.sum(fold_a[...], axis=0, keepdims=True)
    sums[1:2] = jnp.sum(fold_b[...], axis=0, keepdims=True)


def output_kernel(place, act, tokens, branch, out_grad, mods, *rest):
    pieces, rest = rest[:PIECES], rest[PIECES:]
    block_out, sums, wide, value, fold_a, sems = rest
    for copy in start_all(list(down_copies(pieces, place, wide)), sems):
        copy.wait()
    rows = tokens.shape[0]
    value[...] = jnp.zeros_like(value)

    @pl.loop(0, FF // WIDE)
    def _(i):
        cols = pl.ds(pl.multiple_of(i * WIDE, WIDE), WIDE)
        value[...] += dot_nt(act[:, cols], rows_of(wide, 0, 16, cols))

    fold_a[...] = jnp.zeros_like(fold_a)

    def finish(at):
        mlp = value[at]
        frame = lax.broadcasted_iota(jnp.int32, (SLAB, 1), 0) % FRAMES
        keep = frame < place[4]
        middle = tokens[at].astype(F32) + mods[2:3] * branch[at]
        block_out[at] = jnp.where(keep, middle + mods[5:6] * mlp, 0.0).astype(BF16)
        fold(fold_a, jnp.where(keep, out_grad[at].astype(F32), 0.0) * mlp)

    slabs(rows, SLAB, finish)
    sums[...] = jnp.zeros_like(sums)
    sums[0:1] = jnp.sum(fold_a[...], axis=0, keepdims=True)


def pair_grads(left, right, ordered_after=(), row_block=288):
    _, rows, depth = left.shape
    cols = right.shape[1]
    n_dep = len(ordered_after)

    def kernel(keep_l, send_l, right_ref, *rest):
        keep, send = rest[n_dep:]
        send[...] = dot_nn(send_l[0], right_ref[...]).astype(BF16)
        keep[...] = dot_nn(keep_l[0], right_ref[...]).astype(BF16)

    col_block = WIDE * 5 if cols > D else cols
    col_block = cols // 4 if cols > D else cols
    grid = (cols // col_block, rows // row_block)
    return pl.pallas_call(
        kernel,
        grid=grid,
        out_shape=[jax.ShapeDtypeStruct((rows, cols), BF16)] * 2,
        in_specs=[
            pl.BlockSpec((1, row_block, depth), lambda j, i: (0, i, 0)),
            pl.BlockSpec((1, row_block, depth), lambda j, i: (1, i, 0)),
            pl.BlockSpec((depth, col_block), lambda j, i: (0, j)),
        ]
        + [any_spec()] * n_dep,
        out_specs=[pl.BlockSpec((row_block, col_block), lambda j, i: (i, j))] * 2,
        compiler_params=pltpu.CompilerParams(vmem_limit_bytes=40 * 2**20),
        cost_estimate=cost(rows * cols * depth / 3e8),
    )(left, left, right, *ordered_after)


def up_grads(place, left, right, ordered_after=()):
    depth, cols = right.shape
    size = left.shape[0] // 16
    n_dep = len(ordered_after)

    def kernel(place_ref, keep_l, send_l, right_ref, *rest):
        keep, send = rest[n_dep:]
        send[0] = dot_nn(send_l[...], right_ref[...]).astype(BF16)
        keep[0] = dot_nn(keep_l[...], right_ref[...]).astype(BF16)

    def index(dc):
        def block(i, place_ref):
            yy = (place_ref[1] + i // 4) % 2
            return ((i % 4 * 2 + yy) * 2 + (place_ref[2] + dc) % 2, 0)

        return block

    return pl.pallas_call(
        kernel,
        out_shape=[jax.ShapeDtypeStruct((8, size, cols), BF16)] * 2,
        grid_spec=pltpu.PrefetchScalarGridSpec(
            num_scalar_prefetch=1,
            grid=(8,),
            in_specs=[
                pl.BlockSpec((size, depth), index(0)),
                pl.BlockSpec((size, depth), index(1)),
                pl.BlockSpec((depth, cols), lambda i, place_ref: (0, 0)),
            ]
            + [any_spec()] * n_dep,
            out_specs=[pl.BlockSpec((1, size, cols), lambda i, place_ref: (i, 0, 0))] * 2,
        ),
        compiler_params=pltpu.CompilerParams(vmem_limit_bytes=40 * 2**20),
        cost_estimate=cost(9),
    )(place, left, left, right, *ordered_after)


def flat_mesh(mesh):
    n_dp, n_cond = mesh.shape["dp"], mesh.shape["cond"]
    return Mesh(mesh.devices.reshape(n_dp // 4, 2, 2, n_cond), ("z", "y", "c", "x"))


def swap(value, axis):
    return lax.ppermute(value, axis, [(0, 1), (1, 0)])


def sum_plane(value):
    for axis in ("c", "x", "y"):
        value = value + swap(value, axis)
    return value


def sum_all(value):
    value = sum_plane(value)
    for step in (1, 2):
        value = value + lax.ppermute(value, "z", [(i, i ^ step) for i in range(4)])
    return value


def turn_z(value, z):
    out = jnp.zeros_like(value)
    own = lax.dynamic_slice_in_dim(value, z, 1, 0)
    out = lax.dynamic_update_slice_in_dim(out, own, z, 0)
    for step in (1, 2, 3):
        entry = lax.dynamic_slice_in_dim(value, (z + step) % 4, 1, 0)
        got = lax.ppermute(entry, "z", [(i, (i + step) % 4) for i in range(4)])
        out = lax.dynamic_update_slice_in_dim(out, got, (z + 4 - step) % 4, 0)
    return out


def add_low(*terms):
    total = terms[0].astype(F32)
    for term in terms[1:]:
        total = total + term.astype(F32)
    return total.astype(BF16)


def after(value, *others):
    return lax.optimization_barrier((value, *others))[0]


def own_block(early, late, flag_early, flag_late, axis, x, before):
    first = x == 0
    near_late, far_late = jnp.where(first, late[0], late[1]), jnp.where(first, late[1], late[0])
    flag = jnp.concatenate(
        [
            jnp.broadcast_to(flag_early, early.shape),
            jnp.broadcast_to(jnp.where(first, flag_late[0], flag_late[1]), near_late.shape),
        ],
        axis=axis,
    )
    got = swap(after(jnp.concatenate([early, far_late], axis=axis), *before), "x")
    return jnp.where(flag, jnp.concatenate([early, near_late], axis=axis), got)


def gather_near(mine):
    near = lax.all_gather(mine.reshape(-1, mine.shape[-1]), "z", axis=0, tiled=False)
    return near.reshape(near.shape[:1] + mine.shape)


def gather_pieces(near, cut, before_far, before_late):
    far = swap(after(near, *before_far), "y")
    late = swap(cut(after(far, *before_late)), "x")
    pieces = [near, swap(cut(near), "x"), far, late]
    return pieces + [swap(piece, "c") for piece in pieces]


def core_sum(keep, send, cut, x):
    got = swap(send, "c")
    first = x == 0
    (ke, k0, k1), (ge, g0, g1) = cut(keep), cut(got)
    early = [add_low(ke[i], ge[i]) for i in range(2)]
    late_send = add_low(jnp.where(first, k1, k0), jnp.where(first, g1, g0))
    late_keep = add_low(jnp.where(first, k0, k1), jnp.where(first, g0, g1))
    return early, late_keep, late_send


def late_sum(late_keep, late_send, before):
    got = after(swap(late_send, "x"), *before)
    return [add_low(late_keep[i], got[i]) for i in range(2)]


def over_y(halves):
    return add_low(halves[0], swap(halves[1], "y"))


def over_z(value):
    flat = value.reshape(value.shape[0] * value.shape[1], -1)
    part = lax.psum_scatter(flat, "z", scatter_dimension=0, tiled=True)
    return part.reshape(value.shape[1:])


def on_grid(inputs, out_grad, frame_counts, timesteps, labels, owners, *matrices):
    masters, means, squares = matrices[:7], matrices[7:14], matrices[14:]
    z, y, c, x = (lax.axis_index(axis) for axis in ("z", "y", "c", "x"))
    block = (z * 2 + y) * 2 + c
    device = block * 2 + x
    positions, frames, width = inputs.shape
    rows = positions * frames
    span = width // 16
    clips = timesteps.shape[0]
    clip_index = device * positions // PATCHES
    frame_count = lax.dynamic_index_in_dim(frame_counts, clip_index, 0, keepdims=False)
    place = jnp.stack([z, y, c, x, frame_count, z, z, z]).astype(jnp.int32)
    own = [owners[number] == x for number in range(7)]
    own_low = [master[0].T.astype(BF16) for master in masters]

    attend_t, merge_t, up_t, down_t = own_low[3:]
    tiles = attend_t.reshape(3, span, width)
    flags = jnp.stack([own[3], own[4]])[:, None, None]
    first_mine = own_block(
        jnp.stack([tiles[0], merge_t]),
        (tiles[1:2], tiles[2:3]),
        jnp.stack([own[3], own[4]])[:, None, None],
        (own[3], own[3]),
        0,
        x,
        (),
    )
    up_mine = own_block(
        up_t[:UP_E],
        (up_t[UP_E : UP_E + UP_L], up_t[UP_E + UP_L :]),
        own[5],
        (own[5], own[5]),
        0,
        x,
        (first_mine,),
    )
    down_mine = own_block(
        down_t[:, :DOWN_E],
        (down_t[:, DOWN_E : DOWN_E + DOWN_L], down_t[:, DOWN_E + DOWN_L :]),
        own[6],
        (own[6], own[6]),
        1,
        x,
        (up_mine,),
    )

    features = timestep_features(timesteps).astype(BF16)
    one_hot = (labels[:, None] == jnp.arange(LABELS)[None, :]).astype(BF16)
    time_part = jnp.where(own[0], contract_cols(features, own_low[0]), 0.0)
    table_part = jnp.where(own[1], contract_cols(one_hot, own_low[1]), 0.0)
    parts = lax.dynamic_update_slice_in_dim(
        jnp.zeros((2, clips, width), F32), jnp.stack([time_part, table_part]), block * span, 2
    )
    parts = sum_all(parts)
    time_pre = parts[0]
    cond_vec = parts[1] + jax.nn.silu(time_pre)
    cond_act, silu_back = jax.vjp(jax.nn.silu, cond_vec)
    cond_act = cond_act.astype(BF16)
    mod_part = jnp.where(own[2], contract_cols(cond_act, own_low[2]), 0.0)
    mod_span = mod_part.shape[1]
    mod_row = lax.dynamic_update_slice(
        jnp.zeros((4, 4, mod_span), F32), turn_z(mod_part, z)[:, None], (0, y * 2 + c, 0)
    )
    mod_row = sum_plane(mod_row)
    mods = jnp.concatenate([mod_row.reshape(6, width), jnp.zeros((2, width), F32)])

    first_near, up_near, down_near = (
        gather_near(mine) for mine in (first_mine, up_mine, down_mine)
    )
    firsts = gather_pieces(first_near, lambda main: main[:, 2], (mods,), ())
    ups = gather_pieces(up_near, lambda main: main[:, UP_E:], firsts[:1], ())

    tokens = inputs.reshape(rows, width)
    grad_out = out_grad.reshape(rows, width)
    spot = (place, smem_spec())
    whole = vmem_spec()
    in_vmem = lambda *arrays: [(array, whole) for array in arrays]
    in_place = lambda arrays: [(array, any_spec()) for array in arrays]
    sems = lambda count: pltpu.SemaphoreType.DMA((count,))
    d_mlp, d_mlp_rel = run_kernel(
        start_back_kernel,
        [spot] + in_vmem(grad_out, mods),
        [((rows, width), BF16), ((2, 8, span, rows), BF16)],
        [vmem(width, rows, dtype=F32)],
        us=4,
    )
    h1, qkv = run_kernel(
        qkv_kernel,
        [spot] + in_vmem(tokens, mods) + in_place(firsts),
        [((rows, width), BF16), ((48, span, rows), BF16)],
        [vmem(48, span, width), sems(48)],
        us=18,
        ordered_after=[down_near],
    )
    attended, branch, h2 = run_kernel(
        attend_kernel,
        [spot] + in_vmem(qkv, tokens, mods) + in_place(firsts),
        [((rows, width), BF16), ((rows, width), F32), ((rows, width), BF16)],
        [vmem(16, span, width), vmem(16, span, rows, dtype=F32), sems(16)],
        us=20,
    )
    downs = gather_pieces(down_near, lambda main: main[:, :, DOWN_E:], ups[:1], (h2,))
    act, slope = run_kernel(
        up_kernel,
        [spot] + in_vmem(h2) + in_place(ups),
        [((rows, FF), BF16)] * 2,
        [vmem(FF, width), vmem(rows, WIDE, dtype=F32), sems(48)],
        us=27,
    )
    down_keep, down_send = pair_grads(d_mlp_rel.reshape(2, 8 * span, rows), act, downs[3:4])
    cut_down = lambda v: (
        v[..., :DOWN_E],
        v[..., DOWN_E : DOWN_E + DOWN_L],
        v[..., DOWN_E + DOWN_L :],
    )
    shape = (2, 4, span, FF)
    down_early, *down_late = core_sum(down_keep.reshape(shape), down_send.reshape(shape), cut_down, x)

    d_upper, d_upper_t = run_kernel(
        d_upper_kernel,
        [spot] + in_vmem(d_mlp, slope) + in_place(downs),
        [((rows, FF), BF16), ((FF, rows), BF16)],
        [vmem(16, span, FF), vmem(rows, WIDE, dtype=F32), sems(48)],
        us=28,
        ordered_after=[down_early[1], down_late[1]],
    )
    up_keep, up_send = up_grads(place, d_upper_t, h2)
    cut_up = lambda v: (v[:, :, :UP_E], v[:, :, UP_E : UP_E + UP_L], v[:, :, UP_E + UP_L :])
    shape = (2, 4, 4 * span, width)
    up_early, *up_late = core_sum(up_keep.reshape(shape), up_send.reshape(shape), cut_up, x)

    down_late = late_sum(*down_late, (up_keep,))
    d_middle, d_branch, d_branch_rel, d_att, sums_two = run_kernel(
        middle_back_kernel,
        [spot] + in_vmem(d_upper, tokens, grad_out, branch, mods) + in_place(ups + firsts),
        [
            ((rows, width), F32),
            ((rows, width), BF16),
            ((2, 8, span, rows), BF16),
            ((16, span, rows), BF16),
            ((8, width), F32),
        ],
        [
            vmem(FF, width),
            vmem(16, span, width),
            vmem(rows, width, dtype=F32),
            vmem(width, rows, dtype=F32),
        ]
        + [vmem(8, width, dtype=F32)] * 3
        + [sems(64)],
        ordered_after=[down_late[1]],
        us=33,
    )
    merge_keep, merge_send = pair_grads(d_branch_rel.reshape(2, 8 * span, rows), attended)
    shape = (2, 4, span, width)
    merge_keep = merge_keep.reshape(shape)
    merge_got = swap(merge_send.reshape(shape), "c")
    merge_total = over_y([add_low(merge_keep[i], merge_got[i]) for i in range(2)])

    down_total = jnp.concatenate(
        [over_y(down_early), after(over_y(down_late), d_middle)], axis=-1
    )
    d_qkv, d_qkv_rel = run_kernel(
        attend_back_kernel,
        [spot] + in_vmem(qkv, d_att),
        [((rows, 3 * width), BF16), ((2, 8, 3, span, rows), BF16)],
        [vmem(16, span, rows, dtype=F32)] * 3,
        ordered_after=[up_early[1], up_late[1], down_total],
        us=26,
    )
    up_late = late_sum(*up_late, (d_qkv,))
    attend_keep, attend_send = pair_grads(
        d_qkv_rel.reshape(2, 24 * span, rows), h1, [up_late[1]]
    )
    cut_attend = lambda v: (v[:, :, 0], v[:, :, 1], v[:, :, 2])
    shape = (2, 4, 3, span, width)
    first_early, *first_late = core_sum(
        attend_keep.reshape(shape), attend_send.reshape(shape), cut_attend, x
    )
    down_part = over_z(down_total)

    input_grad, sums_one = run_kernel(
        input_back_kernel,
        [spot] + in_vmem(d_qkv, tokens, d_middle, mods) + in_place(firsts),
        [((rows, width), BF16), ((8, width), F32)],
        [vmem(48, span, width), vmem(rows, width, dtype=F32)]
        + [vmem(8, width, dtype=F32)] * 2
        + [sems(48)],
        ordered_after=[attend_keep],
        us=22,
    )
    up_total = jnp.concatenate([over_y(up_early), after(over_y(up_late), input_grad)], axis=1)
    block_out, sums_out = run_kernel(
        output_kernel,
        [spot] + in_vmem(act, tokens, branch, grad_out, mods) + in_place(downs),
        [((rows, width), BF16), ((8, width), F32)],
        [
            vmem(16, span, FF),
            vmem(rows, width, dtype=F32),
            vmem(8, width, dtype=F32),
            sems(48),
        ],
        ordered_after=[up_total, first_early[1], first_late[1], down_part],
        us=21,
    )
    first_late = late_sum(*first_late, (block_out,))
    up_part = over_z(after(up_total, down_part))
    first_total = jnp.concatenate([over_y(first_early), merge_total, over_y(first_late)], axis=2)
    first_part = over_z(after(first_total, up_part))
    first_part = first_part.reshape(span, 3, width).transpose(1, 0, 2)
    down_got, up_got, first_got = swap(down_part, "x"), swap(up_part, "x"), swap(first_part, "x")

    d_vector = jnp.concatenate([sums_one[:2], sums_two[:3], sums_out[:1]]).reshape(6 * width)
    d_mod = sum_plane(after(d_vector, up_part).reshape(4, 4, mod_span))
    d_mod = lax.dynamic_index_in_dim(d_mod, y * 2 + c, 1, keepdims=False)
    d_mod = turn_z(d_mod, z)
    grad_mod = contract_rows(d_mod, cond_act.astype(F32), HIGHEST)
    d_cond_part = jnp.dot(
        d_mod, own_low[2].astype(F32), precision=HIGHEST, preferred_element_type=F32
    )
    d_cond_act = sum_all(jnp.where(own[2], d_cond_part, 0.0))
    d_cond = silu_back(d_cond_act)[0]
    d_time_pre = jax.vjp(jax.nn.silu, time_pre)[1](d_cond)[0]
    d_cond_block = lax.dynamic_slice_in_dim(d_cond, block * span, span, 1)
    d_time_block = lax.dynamic_slice_in_dim(d_time_pre, block * span, span, 1)
    grad_table = contract_rows(d_cond_block, one_hot.astype(F32), HIGHEST)
    grad_time = contract_rows(d_time_block, features.astype(F32), HIGHEST)

    def joined(early, part, got, axis):
        first = x == 0
        halves = [jnp.where(first, part, got), jnp.where(first, got, part)]
        return jnp.concatenate([early.astype(BF16)] + halves, axis=axis).astype(F32)

    def both(part, got):
        return part.astype(F32) + got.astype(F32)

    grads = (
        grad_time,
        grad_table,
        grad_mod,
        jnp.concatenate(
            [
                both(first_part[0], first_got[0]),
                jnp.where(x == 0, first_part[2], first_got[2]).astype(F32),
                jnp.where(x == 0, first_got[2], first_part[2]).astype(F32),
            ]
        ),
        both(first_part[1], first_got[1]),
        jnp.concatenate(
            [
                both(up_part[:UP_E], up_got[:UP_E]),
                jnp.where(x == 0, up_part[UP_E:], up_got[UP_E:]).astype(F32),
                jnp.where(x == 0, up_got[UP_E:], up_part[UP_E:]).astype(F32),
            ]
        ),
        jnp.concatenate(
            [
                both(down_part[:, :DOWN_E], down_got[:, :DOWN_E]),
                jnp.where(x == 0, down_part[:, DOWN_E:], down_got[:, DOWN_E:]).astype(F32),
                jnp.where(x == 0, down_got[:, DOWN_E:], down_part[:, DOWN_E:]).astype(F32),
            ],
            axis=1,
        ),
    )
    rates = [
        0.5 * FREQ ** (-0.5),
        0.5,
        0.5 * D ** (-0.5),
        0.5 * D ** (-0.5),
        D ** (-0.5),
        0.5 * D ** (-0.5),
        0.5 * FF ** (-0.5),
    ]
    new_list, first_list, second_list, copy_list = ([], [], [], [])
    for number in range(7):
        fresh, mean, square = adamw_step(
            masters[number][0].T,
            means[number][0].T,
            squares[number][0].T,
            grads[number],
            rates[number],
        )
        fresh = jnp.where(own[number], fresh, 0.0).T[None]
        new_list.append(fresh)
        first_list.append(jnp.where(own[number], mean, 0.0).T[None])
        second_list.append(jnp.where(own[number], square, 0.0).T[None])
        copy_list.append(fresh.astype(BF16))
    return (
        block_out.reshape(inputs.shape),
        input_grad.reshape(inputs.shape),
        *new_list,
        *first_list,
        *second_list,
        *copy_list,
    )


def on_device(
    inputs,
    out_grad,
    frame_counts,
    timesteps,
    labels,
    owners,
    w_time,
    w_table,
    w_modulate,
    w_attend,
    w_merge,
    w_up,
    w_down,
    mean_time,
    mean_table,
    mean_modulate,
    mean_attend,
    mean_merge,
    mean_up,
    mean_down,
    square_time,
    square_table,
    square_modulate,
    square_attend,
    square_merge,
    square_up,
    square_down,
):
    masters = (w_time, w_table, w_modulate, w_attend, w_merge, w_up, w_down)
    means = (mean_time, mean_table, mean_modulate, mean_attend, mean_merge, mean_up, mean_down)
    squares = (
        square_time,
        square_table,
        square_modulate,
        square_attend,
        square_merge,
        square_up,
        square_down,
    )
    n_dp = lax.axis_size("dp")
    n_cond = lax.axis_size("cond")
    cond_index = lax.axis_index("cond")
    dp_index = lax.axis_index("dp")
    device = dp_index * n_cond + cond_index
    positions, frames, width = inputs.shape
    clips = timesteps.shape[0]
    clip_index = device * positions // PATCHES
    frame_count = lax.dynamic_index_in_dim(frame_counts, clip_index, 0, keepdims=False)
    both = (
        lax.all_gather(w_time.astype(jnp.bfloat16), "cond", axis=0, tiled=True),
        lax.all_gather(w_table.astype(jnp.bfloat16), "cond", axis=0, tiled=True),
        lax.all_gather(w_modulate.astype(jnp.bfloat16), "cond", axis=0, tiled=True),
        lax.all_gather(w_attend.astype(jnp.bfloat16), "cond", axis=0, tiled=True),
        lax.all_gather(w_merge.astype(jnp.bfloat16), "cond", axis=0, tiled=True),
        lax.all_gather(w_up.astype(jnp.bfloat16), "cond", axis=0, tiled=True),
        lax.all_gather(w_down.astype(jnp.bfloat16), "cond", axis=0, tiled=True),
    )
    owned = [
        lax.dynamic_index_in_dim(pair, owners[number], 0, keepdims=False)
        for number, pair in enumerate(both)
    ]
    time_w, table_w, attend_w, merge_w, up_w, down_w = (
        lax.all_gather(owned[0], "dp", axis=1, tiled=True),
        lax.all_gather(owned[1], "dp", axis=1, tiled=True),
        lax.all_gather(owned[3], "dp", axis=1, tiled=True),
        lax.all_gather(owned[4], "dp", axis=1, tiled=True),
        lax.all_gather(owned[5], "dp", axis=1, tiled=True),
        lax.all_gather(owned[6], "dp", axis=1, tiled=True),
    )
    half_width = owned[2].shape[1] // n_cond
    modulate_half = lax.dynamic_slice_in_dim(owned[2], cond_index * half_width, half_width, 1)
    features = timestep_features(timesteps).astype(jnp.bfloat16)
    time_pre = jnp.dot(features, time_w, preferred_element_type=jnp.float32)
    one_hot = (labels[:, None] == jnp.arange(LABELS)[None, :]).astype(jnp.bfloat16)
    cond_vec = jnp.dot(one_hot, table_w, preferred_element_type=jnp.float32) + jax.nn.silu(time_pre)
    cond_act, silu_back = jax.vjp(jax.nn.silu, cond_vec)
    cond_act = cond_act.astype(jnp.bfloat16)
    mod_part = jnp.dot(cond_act, modulate_half, preferred_element_type=jnp.float32)
    modulation = lax.all_gather(mod_part, ("dp", "cond"), axis=1, tiled=True)
    mod_row = lax.dynamic_index_in_dim(modulation, clip_index, 0, keepdims=False)
    shift_one, scale_one, gate_one, shift_two, scale_two, gate_two = [
        mod_row[part * width : (part + 1) * width] for part in range(6)
    ]
    rows = positions * frames
    tokens = inputs.reshape(rows, width).astype(jnp.float32)
    frame_ids = jnp.tile(jnp.arange(frames), positions)
    row_mask = (frame_ids < frame_count).astype(jnp.float32)[:, None]
    key_valid = jnp.arange(frames) < frame_count
    inv_scale = 1.0 / math.sqrt(HEAD)
    norm_one, rstd_one = normalize(tokens)
    hidden_one = (norm_one * (1.0 + scale_one) + shift_one).astype(jnp.bfloat16)
    qkv = jnp.dot(hidden_one, attend_w, preferred_element_type=jnp.float32).astype(jnp.bfloat16)
    queries = qkv[:, :width].reshape(positions, frames, HEADS, HEAD)
    key_rows = qkv[:, width : 2 * width].reshape(positions, frames, HEADS, HEAD)
    value_rows = qkv[:, 2 * width :].reshape(positions, frames, HEADS, HEAD)
    scores = (
        jnp.einsum("pfhe,pghe->phfg", queries, key_rows, preferred_element_type=jnp.float32)
        * inv_scale
    )
    scores = jnp.where(key_valid[None, None, None, :], scores, -1e30)
    top = jnp.max(scores, axis=-1, keepdims=True)
    expo = jnp.exp(scores - top)
    probs = expo / jnp.sum(expo, axis=-1, keepdims=True)
    probs_low = probs.astype(jnp.bfloat16)
    attended = jnp.einsum(
        "phfg,pghe->pfhe", probs_low, value_rows, preferred_element_type=jnp.float32
    )
    attended = attended.reshape(rows, width).astype(jnp.bfloat16)
    branch = jnp.dot(attended, merge_w, preferred_element_type=jnp.float32)
    middle = tokens + gate_one * branch
    norm_two, rstd_two = normalize(middle)
    hidden_two = (norm_two * (1.0 + scale_two) + shift_two).astype(jnp.bfloat16)
    upper = jnp.dot(hidden_two, up_w, preferred_element_type=jnp.float32)
    activ, gelu_back = jax.vjp(partial(jax.nn.gelu, approximate=True), upper)
    activ = activ.astype(jnp.bfloat16)
    mlp_out = jnp.dot(activ, down_w, preferred_element_type=jnp.float32)
    block_out = (
        (row_mask * (middle + gate_two * mlp_out))
        .reshape(positions, frames, width)
        .astype(jnp.bfloat16)
    )
    attend_b, merge_b, up_b, down_b = (
        lax.all_gather(owned[3], "dp", axis=1, tiled=True),
        lax.all_gather(owned[4], "dp", axis=1, tiled=True),
        lax.all_gather(owned[5], "dp", axis=1, tiled=True),
        lax.all_gather(owned[6], "dp", axis=1, tiled=True),
    )
    grad_out = out_grad.reshape(rows, width).astype(jnp.float32) * row_mask
    d_mlp = (grad_out * gate_two).astype(jnp.bfloat16)
    grad_down = contract_rows(activ, d_mlp)
    d_activ = contract_cols(d_mlp, down_b)
    d_upper = gelu_back(d_activ)[0].astype(jnp.bfloat16)
    grad_up = contract_rows(hidden_two, d_upper)
    d_hidden_two = contract_cols(d_upper, up_b)
    d_middle = grad_out + normalize_back(d_hidden_two * (1.0 + scale_two), norm_two, rstd_two)
    d_branch = (d_middle * gate_one).astype(jnp.bfloat16)
    grad_merge = contract_rows(attended, d_branch)
    d_attended = (
        contract_cols(d_branch, merge_b)
        .astype(jnp.bfloat16)
        .reshape(positions, frames, HEADS, HEAD)
    )
    d_probs = jnp.einsum(
        "pfhe,pghe->phfg", d_attended, value_rows, preferred_element_type=jnp.float32
    )
    d_values = jnp.einsum(
        "phfg,pfhe->pghe", probs_low, d_attended, preferred_element_type=jnp.float32
    )
    d_scores = (probs * (d_probs - jnp.sum(probs * d_probs, axis=-1, keepdims=True))).astype(
        jnp.bfloat16
    )
    d_queries = (
        jnp.einsum("phfg,pghe->pfhe", d_scores, key_rows, preferred_element_type=jnp.float32)
        * inv_scale
    )
    d_keys = (
        jnp.einsum("phfg,pfhe->pghe", d_scores, queries, preferred_element_type=jnp.float32)
        * inv_scale
    )
    d_qkv = jnp.concatenate(
        [
            d_queries.reshape(rows, width),
            d_keys.reshape(rows, width),
            d_values.reshape(rows, width),
        ],
        axis=1,
    ).astype(jnp.bfloat16)
    grad_attend = contract_rows(hidden_one, d_qkv)
    d_hidden_one = contract_cols(d_qkv, attend_b)
    d_tokens = d_middle + normalize_back(d_hidden_one * (1.0 + scale_one), norm_one, rstd_one)
    input_grad = d_tokens.reshape(positions, frames, width).astype(jnp.bfloat16)
    d_vector = jnp.concatenate(
        [
            jnp.sum(d_hidden_one, axis=0),
            jnp.sum(d_hidden_one * norm_one, axis=0),
            jnp.sum(d_middle * branch, axis=0),
            jnp.sum(d_hidden_two, axis=0),
            jnp.sum(d_hidden_two * norm_two, axis=0),
            jnp.sum(grad_out * mlp_out, axis=0),
        ]
    )
    clip_pick = (jnp.arange(clips) == clip_index).astype(jnp.float32)
    d_mod_local = clip_pick[:, None] * d_vector[None, :]
    d_mod_half = lax.psum_scatter(d_mod_local, ("dp", "cond"), scatter_dimension=1, tiled=True)
    grad_mod_half = contract_rows(cond_act.astype(jnp.float32), d_mod_half, HIGHEST)
    d_cond_part = contract_cols(d_mod_half, modulate_half.astype(jnp.float32), HIGHEST)
    d_cond_act = lax.psum(d_cond_part, ("dp", "cond"))
    d_cond = silu_back(d_cond_act)[0]
    grad_table = contract_rows(one_hot.astype(jnp.float32), d_cond, HIGHEST)
    d_time_pre = jax.vjp(jax.nn.silu, time_pre)[1](d_cond)[0]
    grad_time = contract_rows(features.astype(jnp.float32), d_time_pre, HIGHEST)
    span = width // n_dp
    grad_time_block = lax.dynamic_slice_in_dim(grad_time, dp_index * span, span, 1)
    grad_table_block = lax.dynamic_slice_in_dim(grad_table, dp_index * span, span, 1)
    blocks = (
        lax.psum_scatter(grad_attend, "dp", scatter_dimension=1, tiled=True),
        lax.psum_scatter(grad_merge, "dp", scatter_dimension=1, tiled=True),
        lax.psum_scatter(grad_up, "dp", scatter_dimension=1, tiled=True),
        lax.psum_scatter(grad_down, "dp", scatter_dimension=1, tiled=True),
    )
    placed = lax.dynamic_update_slice_in_dim(
        jnp.zeros((width, half_width * n_cond), jnp.float32),
        grad_mod_half,
        cond_index * half_width,
        1,
    )
    row_halves = (
        lax.psum_scatter(
            blocks[0].astype(jnp.bfloat16), "cond", scatter_dimension=0, tiled=True
        ).astype(jnp.float32),
        lax.psum_scatter(
            blocks[1].astype(jnp.bfloat16), "cond", scatter_dimension=0, tiled=True
        ).astype(jnp.float32),
        lax.psum_scatter(
            blocks[2].astype(jnp.bfloat16), "cond", scatter_dimension=0, tiled=True
        ).astype(jnp.float32),
        lax.psum_scatter(
            blocks[3].astype(jnp.bfloat16), "cond", scatter_dimension=0, tiled=True
        ).astype(jnp.float32),
        lax.psum_scatter(
            placed.astype(jnp.bfloat16), "cond", scatter_dimension=0, tiled=True
        ).astype(jnp.float32),
    )
    joined = (
        lax.all_gather(row_halves[0].astype(jnp.bfloat16), "cond", axis=0, tiled=True).astype(
            jnp.float32
        ),
        lax.all_gather(row_halves[1].astype(jnp.bfloat16), "cond", axis=0, tiled=True).astype(
            jnp.float32
        ),
        lax.all_gather(row_halves[2].astype(jnp.bfloat16), "cond", axis=0, tiled=True).astype(
            jnp.float32
        ),
        lax.all_gather(row_halves[3].astype(jnp.bfloat16), "cond", axis=0, tiled=True).astype(
            jnp.float32
        ),
        lax.all_gather(row_halves[4].astype(jnp.bfloat16), "cond", axis=0, tiled=True).astype(
            jnp.float32
        ),
    )
    grads = (
        grad_time_block,
        grad_table_block,
        joined[4],
        joined[0],
        joined[1],
        joined[2],
        joined[3],
    )
    rates = [
        0.5 * FREQ ** (-0.5),
        0.5,
        0.5 * D ** (-0.5),
        0.5 * D ** (-0.5),
        D ** (-0.5),
        0.5 * D ** (-0.5),
        0.5 * FF ** (-0.5),
    ]
    new_list, first_list, second_list, copy_list = ([], [], [], [])
    for number in range(7):
        fresh, first, second = adamw_step(
            masters[number][0], means[number][0], squares[number][0], grads[number], rates[number]
        )
        is_owner = cond_index == owners[number]
        fresh = jnp.where(is_owner, fresh, 0.0)[None]
        new_list.append(fresh)
        first_list.append(jnp.where(is_owner, first, 0.0)[None])
        second_list.append(jnp.where(is_owner, second, 0.0)[None])
        copy_list.append(fresh.astype(jnp.bfloat16))
    return (block_out, input_grad, *new_list, *first_list, *second_list, *copy_list)


def solution(mesh):
    n_dp, n_cond = mesh.shape["dp"], mesh.shape["cond"]
    if (n_dp, n_cond) == (16, 2):
        token_spec = P(("z", "y", "c", "x"), None, None)
        matrix_spec = P("x", None, ("z", "y", "c"))
        return jax.shard_map(
            on_grid,
            mesh=flat_mesh(mesh),
            in_specs=(token_spec,) * 2 + (P(),) * 4 + (matrix_spec,) * 21,
            out_specs=(token_spec,) * 2 + (matrix_spec,) * 28,
            check_vma=False,
        )
    token_spec = P(("dp", "cond"), None, None)
    matrix_spec = P("cond", None, "dp")
    return jax.shard_map(
        on_device,
        mesh=mesh,
        in_specs=(token_spec,) * 2 + (P(),) * 4 + (matrix_spec,) * 21,
        out_specs=(token_spec,) * 2 + (matrix_spec,) * 28,
        check_vma=False,
    )
```

```python
from functools import partial
import math

import jax
import jax.numpy as jnp
from jax import lax
from jax.experimental import pallas as pl
from jax.experimental.pallas import tpu as pltpu
from jax.sharding import Mesh, PartitionSpec as P

D = 1152
HEADS = 16
HEAD = 72
FF = 4608
FREQ = 256
LABELS = 101
FRAMES = 16
PATCHES = 256
STEP = 5


HIGHEST = lax.Precision.HIGHEST
EPSILON = 1e-06


def contract_rows(left, right, precision=None):
    return lax.dot_general(
        left,
        right,
        (((0,), (0,)), ((), ())),
        precision=precision,
        preferred_element_type=jnp.float32,
    )


def contract_cols(left, right, precision=None):
    return lax.dot_general(
        left,
        right,
        (((1,), (1,)), ((), ())),
        precision=precision,
        preferred_element_type=jnp.float32,
    )


def normalize(values):
    centre = values - jnp.mean(values, axis=-1, keepdims=True)
    spread = lax.rsqrt(jnp.mean(centre * centre, axis=-1, keepdims=True) + EPSILON)
    return (centre * spread, spread)


def normalize_back(upstream, normed, spread):
    return spread * (
        upstream
        - jnp.mean(upstream, axis=-1, keepdims=True)
        - normed * jnp.mean(upstream * normed, axis=-1, keepdims=True)
    )


def timestep_features(timesteps):
    half_count = FREQ // 2
    freqs = jnp.exp(-math.log(10000.0) * jnp.arange(half_count, dtype=jnp.float32) / half_count)
    angles = timesteps.astype(jnp.float32)[:, None] * freqs[None, :]
    return jnp.concatenate([jnp.cos(angles), jnp.sin(angles)], axis=1)


def adamw_step(master, first, second, grad, rate):
    first_new = 0.5 * first + 0.5 * grad
    second_new = 0.5 * second + 0.5 * grad * grad
    correct = 1.0 - 0.5**STEP
    update = first_new / correct / (jnp.sqrt(second_new / correct) + 1e-08)
    return (master - rate * (update + 0.01 * master), first_new, second_new)


BF16, F32 = jnp.bfloat16, jnp.float32
SLAB = 128
COST_FLOPS, COST_BYTES = 6e9, 18e6
GROUP = 128
WIDE = 256


def vmem(*shape, dtype=BF16):
    return pltpu.VMEM(shape, dtype)


def any_spec():
    return pl.BlockSpec(memory_space=pl.ANY)


def smem_spec():
    return pl.BlockSpec(memory_space=pltpu.SMEM)


def vmem_spec():
    return pl.BlockSpec(memory_space=pltpu.VMEM)


def dot_nn(left, right):
    return lax.dot_general(left, right, (((1,), (0,)), ((), ())), preferred_element_type=F32)


def dot_nt(left, right):
    return lax.dot_general(left, right, (((1,), (1,)), ((), ())), preferred_element_type=F32)


def cost(us):
    return pl.CostEstimate(flops=int(us * COST_FLOPS), bytes_accessed=int(us * COST_BYTES), transcendentals=0)


def run_kernel(body, operands, outs, scratch, us, ordered_after=(), mib=56, steps=None):
    arrays = [array for array, _ in operands] + list(ordered_after)
    specs = [spec for _, spec in operands] + [any_spec() for _ in ordered_after]
    n_in, n_dep = len(operands), len(ordered_after)

    def kernel(*refs):
        body(*refs[:n_in], *refs[n_in + n_dep :])

    return pl.pallas_call(
        kernel,
        grid=() if steps is None else (steps,),
        out_shape=[jax.ShapeDtypeStruct(*out[:2]) for out in outs],
        in_specs=specs,
        out_specs=[out[2] if len(out) > 2 else vmem_spec() for out in outs],
        scratch_shapes=scratch,
        compiler_params=pltpu.CompilerParams(vmem_limit_bytes=mib * 2**20),
        cost_estimate=cost(us),
    )(*arrays)


PIECES = 8


def block_order(place, zz=None):
    y, c = place[1], place[2]
    for z in range(4) if zz is None else (zz,):
        for dc in range(2):
            for dy in range(2):
                yy = y if dy == 0 else 1 - y
                cc = c if dc == 0 else 1 - c
                yield dc * 4 + dy * 2, z, (z * 2 + yy) * 2 + cc


def start_all(copies, sems):
    made = [pltpu.make_async_copy(src, dst, sems.at[i]) for i, (src, dst) in enumerate(copies)]
    for copy in made:
        copy.start()
    return made


def attend_copies(pieces, place, wide):
    x = place[3]
    for at, zz, b in block_order(place):
        main, other = pieces[at : at + 2]
        yield main.at[zz, :, pl.ds(0, D)], wide.at[b * 3]
        yield main.at[zz, :, pl.ds(2 * D, D)], wide.at[b * 3 + 1 + x]
        yield other.at[zz], wide.at[b * 3 + 2 - x]


def merge_copies(pieces, place, wide):
    for at, zz, b in block_order(place):
        yield pieces[at].at[zz, :, pl.ds(D, D)], wide.at[b]


UP_E, UP_L = 128, 80


def up_copies(pieces, place, wide, z=None):
    x = place[3]
    size = UP_E + 2 * UP_L
    for at, zz, b in block_order(place, z):
        main, other = pieces[at : at + 2]
        row = pl.multiple_of(b * size, 16)
        near_row = pl.multiple_of(b * size + UP_E + UP_L * x, 16)
        other_row = pl.multiple_of(b * size + UP_E + UP_L - UP_L * x, 16)
        yield main.at[zz, pl.ds(0, UP_E)], wide.at[pl.ds(row, UP_E)]
        yield main.at[zz, pl.ds(UP_E, UP_L)], wide.at[pl.ds(near_row, UP_L)]
        yield other.at[zz], wide.at[pl.ds(other_row, UP_L)]


DOWN_E, DOWN_L = 2048, 1280


def down_copies(pieces, place, wide):
    x = place[3]
    near_col = pl.multiple_of(DOWN_E + DOWN_L * x, 128)
    other_col = pl.multiple_of(DOWN_E + DOWN_L - DOWN_L * x, 128)
    for at, zz, b in block_order(place):
        yield pieces[at].at[zz, :, pl.ds(0, DOWN_E)], wide.at[b, :, pl.ds(0, DOWN_E)]
    for at, zz, b in block_order(place):
        main, other = pieces[at : at + 2]
        yield main.at[zz, :, pl.ds(DOWN_E, DOWN_L)], wide.at[b, :, pl.ds(near_col, DOWN_L)]
        yield other.at[zz], wide.at[b, :, pl.ds(other_col, DOWN_L)]


def rows_of(wide, first, count, cols=None):
    value = wide[pl.ds(first, count)] if cols is None else wide[pl.ds(first, count), :, cols]
    return value.astype(F32).reshape(count * HEAD, value.shape[-1]).astype(BF16)


def norm_slab(values):
    mean = jnp.sum(values, axis=1, keepdims=True) * (1.0 / D)
    centre = values - mean
    spread = lax.rsqrt(jnp.sum(centre * centre, axis=1, keepdims=True) * (1.0 / D) + EPSILON)
    return centre * spread, spread


def back_slab(upstream, normed, spread):
    first = jnp.sum(upstream, axis=1, keepdims=True) * (1.0 / D)
    second = jnp.sum(upstream * normed, axis=1, keepdims=True) * (1.0 / D)
    return spread * (upstream - first - normed * second)


def slabs(rows, size, body):
    @pl.loop(0, rows // size)
    def _(i):
        body(pl.ds(pl.multiple_of(i * size, size), size))


def fold(ref, value):
    ref[...] += jnp.sum(value.reshape(value.shape[0] // 8, 8, value.shape[1]), axis=0)


def turn(src, dst):
    @pl.loop(0, src.shape[0] // GROUP)
    def _(i):
        at = pl.ds(pl.multiple_of(i * GROUP, GROUP), GROUP)
        dst[:, at] = src[at].astype(F32).T


def store_relative(ref, turned, y, c):
    for b in range(16):
        zz, yy, cc = b // 4, (b // 2) % 2, b % 2
        dy = y if yy == 0 else 1 - y
        dc = c if cc == 0 else 1 - c
        ref[dc, dy * 4 + zz] = turned[b * HEAD : (b + 1) * HEAD].astype(BF16)


def frame_mask(count):
    keys = lax.broadcasted_iota(jnp.int32, (GROUP, GROUP), 0)
    asks = lax.broadcasted_iota(jnp.int32, (GROUP, GROUP), 1)
    return (keys // FRAMES == asks // FRAMES) & (keys % FRAMES < count)


def probs_of(key, query, mask):
    scores = dot_nn(key.astype(F32).T.astype(BF16), query) * (1.0 / math.sqrt(HEAD))
    scores = jnp.where(mask, scores, -1e30)
    top = jnp.max(scores, axis=0, keepdims=True)
    expo = jnp.exp(scores - top)
    return expo * (1.0 / jnp.sum(expo, axis=0, keepdims=True))


def qkv_kernel(place, tokens, mods, *rest):
    pieces, rest = rest[:PIECES], rest[PIECES:]
    h1, qkv, wide, sems = rest
    copies = start_all(list(attend_copies(pieces, place, wide)), sems)

    def norm_one(at):
        normed, _ = norm_slab(tokens[at].astype(F32))
        h1[at] = (normed * (1.0 + mods[1:2]) + mods[0:1]).astype(BF16)

    slabs(tokens.shape[0], SLAB, norm_one)
    for copy in copies:
        copy.wait()

    @pl.loop(0, 12)
    def _(i):
        value = dot_nt(rows_of(wide, i * 4, 4), h1[...])
        for j in range(4):
            qkv[i * 4 + j] = value[j * HEAD : (j + 1) * HEAD].astype(BF16)


def attend_kernel(place, qkv, tokens, mods, *rest):
    pieces, rest = rest[:PIECES], rest[PIECES:]
    attended, branch, h2, merge, turned, sems = rest
    copies = start_all(list(merge_copies(pieces, place, merge)), sems)
    rows = tokens.shape[0]
    mask = frame_mask(place[4])

    @pl.loop(0, HEADS)
    def _(head):
        for group in range(rows // GROUP):
            at = pl.ds(group * GROUP, GROUP)
            probs = probs_of(qkv[HEADS + head, :, at], qkv[head, :, at], mask)
            turned[head, :, at] = dot_nn(qkv[2 * HEADS + head, :, at], probs.astype(BF16))

    for group in range(rows // GROUP):
        at = pl.ds(group * GROUP, GROUP)
        attended[at] = turned[:, :, at].reshape(D, GROUP).T.astype(BF16)
    for copy in copies:
        copy.wait()
    branch[...] = dot_nt(attended[...], rows_of(merge, 0, 16))

    def norm_two(at):
        middle = tokens[at].astype(F32) + mods[2:3] * branch[at]
        normed, _ = norm_slab(middle)
        h2[at] = (normed * (1.0 + mods[4:5]) + mods[3:4]).astype(BF16)

    slabs(rows, SLAB, norm_two)


def gelu_parts(u):
    root = math.sqrt(2.0 / math.pi)
    square = u * u
    bent = jnp.tanh(u * (root + (root * 0.044715) * square))
    half = 0.5 + 0.5 * bent
    rise = root + (root * 3.0 * 0.044715) * square
    return u * half, half + (0.5 * u) * (1.0 - bent * bent) * rise


def up_kernel(place, h2, *rest):
    pieces, rest = rest[:PIECES], rest[PIECES:]
    act, slope, wide, even, odd, sems = rest
    step = pl.program_id(0)

    @pl.when(step == 0)
    def _():
        start_all(list(up_copies(pieces, place, wide)), sems)

    for i, (src, dst) in enumerate(up_copies(pieces, place, wide, step)):
        pltpu.make_async_copy(src, dst, sems.at[step * 12 + i]).wait()
    rows = h2.shape[0]
    ends = [(at, min(WIDE, D - at)) for at in range(0, D, WIDE)]

    def finish(upper, first, width):
        for row in range(0, rows, 32):
            at = pl.ds(row, 32)
            value, rise = gelu_parts(upper[at, :width])
            act[at, pl.ds(first, width)] = value.astype(BF16)
            slope[at, pl.ds(first, width)] = rise.astype(BF16)

    for number, (first, width) in enumerate(ends):
        upper, before = (even, odd) if number % 2 == 0 else (odd, even)
        at = pl.ds(pl.multiple_of(step * D + first, 128), width)
        upper[:, :width] = dot_nt(h2[...], wide[at])
        if number:
            finish(before, *ends[number - 1])
    finish(even if len(ends) % 2 else odd, *ends[-1])


def start_back_kernel(place, out_grad, mods, d_mlp, relative, turned):
    rows = out_grad.shape[0]

    def scale(at):
        frame = lax.broadcasted_iota(jnp.int32, (SLAB, 1), 0) % FRAMES
        dy = jnp.where(frame < place[4], out_grad[at].astype(F32), 0.0)
        d_mlp[at] = (dy * mods[5:6]).astype(BF16)

    slabs(rows, SLAB, scale)
    turn(d_mlp, turned)
    store_relative(relative, turned, place[1], place[2])


def d_upper_kernel(place, d_mlp, slope, *rest):
    pieces, rest = rest[:PIECES], rest[PIECES:]
    d_upper, d_upper_t, wide, even, odd, sems = rest
    step = pl.program_id(0)

    @pl.when(step == 0)
    def _():
        for copy in start_all(list(down_copies(pieces, place, wide)), sems)[:16]:
            copy.wait()

    @pl.when(step == DOWN_E // (2 * WIDE))
    def _():
        for i, (src, dst) in enumerate(down_copies(pieces, place, wide)):
            if i >= 16:
                pltpu.make_async_copy(src, dst, sems.at[i]).wait()

    rows = d_mlp.shape[0]

    def finish(value, first):
        cols = pl.ds(first, WIDE)
        for row in range(0, rows, GROUP):
            at = pl.ds(row, GROUP)
            part = value[at] * slope[at, cols].astype(F32)
            d_upper[at, cols] = part.astype(BF16)
            d_upper_t[cols, at] = part.T.astype(BF16)

    base = pl.multiple_of(step * 2 * WIDE, 2 * WIDE)
    even[...] = dot_nn(d_mlp[...], rows_of(wide, 0, 16, pl.ds(base, WIDE)))
    odd[...] = dot_nn(d_mlp[...], rows_of(wide, 0, 16, pl.ds(base + WIDE, WIDE)))
    finish(even, 0)
    finish(odd, WIDE)


def middle_back_kernel(place, d_upper, tokens, out_grad, branch, mods, *rest):
    ups, firsts, rest = rest[:PIECES], rest[PIECES : 2 * PIECES], rest[2 * PIECES :]
    d_middle, d_branch, relative, d_att, sums, wide, merge, value, turned, fold_a, fold_b, fold_c, sems = rest
    copies = list(up_copies(ups, place, wide)) + list(merge_copies(firsts, place, merge))
    copies = start_all(copies, sems)
    rows = tokens.shape[0]
    for z in range(4):
        for copy in copies[z * 12 : (z + 1) * 12]:
            copy.wait()
        add = dot_nn(d_upper[:, z * D : (z + 1) * D], wide[z * D : (z + 1) * D])
        if z == 0:
            value[...] = add
        else:
            value[...] += add
    for copy in copies[48:]:
        copy.wait()
    for ref in (fold_a, fold_b, fold_c):
        ref[...] = jnp.zeros_like(ref)

    def back(at):
        d_h2 = value[at]
        arm = branch[at]
        normed, spread = norm_slab(tokens[at].astype(F32) + mods[2:3] * arm)
        frame = lax.broadcasted_iota(jnp.int32, (SLAB, 1), 0) % FRAMES
        dy = jnp.where(frame < place[4], out_grad[at].astype(F32), 0.0)
        d_mid = dy + back_slab(d_h2 * (1.0 + mods[4:5]), normed, spread)
        d_middle[at] = d_mid
        d_branch[at] = (d_mid * mods[2:3]).astype(BF16)
        fold(fold_a, d_mid * arm)
        fold(fold_b, d_h2)
        fold(fold_c, d_h2 * normed)

    slabs(rows, SLAB, back)
    sums[...] = jnp.zeros_like(sums)
    sums[0:1] = jnp.sum(fold_a[...], axis=0, keepdims=True)
    sums[1:2] = jnp.sum(fold_b[...], axis=0, keepdims=True)
    sums[2:3] = jnp.sum(fold_c[...], axis=0, keepdims=True)
    turn(d_branch, turned)
    store_relative(relative, turned, place[1], place[2])
    value[...] = dot_nn(d_branch[...], rows_of(merge, 0, 16))
    turn(value, turned)
    for head in range(HEADS):
        d_att[head] = turned[head * HEAD : (head + 1) * HEAD].astype(BF16)


def attend_back_kernel(place, qkv, d_att, d_qkv, relative, d_q, d_k, d_v):
    rows = qkv.shape[2]
    y, c = place[1], place[2]
    mask = frame_mask(place[4])
    scale = 1.0 / math.sqrt(HEAD)

    @pl.loop(0, HEADS // 2)
    def _(pair):
        for number in range(2 * rows // GROUP):
            head = pair * 2 + number % 2
            at = pl.ds(number // 2 * GROUP, GROUP)
            query, key = qkv[head, :, at], qkv[HEADS + head, :, at]
            val, grad = qkv[2 * HEADS + head, :, at], d_att[head, :, at]
            probs = probs_of(key, query, mask)
            d_probs = dot_nn(val.astype(F32).T.astype(BF16), grad)
            d_v[head, :, at] = dot_nt(grad, probs.astype(BF16))
            inner = jnp.sum(probs * d_probs, axis=0, keepdims=True)
            d_scores = (probs * (d_probs - inner)).astype(BF16)
            d_q[head, :, at] = dot_nn(key, d_scores) * scale
            d_k[head, :, at] = dot_nt(query, d_scores) * scale

    for part, ref in enumerate((d_q, d_k, d_v)):
        for group in range(rows // GROUP):
            at = pl.ds(group * GROUP, GROUP)
            d_qkv[at, part * D : (part + 1) * D] = ref[:, :, at].reshape(D, GROUP).T.astype(BF16)
        for head in range(HEADS):
            number = part * HEADS + head
            b, tile = number // 3, number % 3
            zz, yy, cc = b // 4, (b // 2) % 2, b % 2
            dy = y if yy == 0 else 1 - y
            dc = c if cc == 0 else 1 - c
            relative[dc, tile, dy * 4 + zz] = ref[head].astype(BF16)


def input_back_kernel(place, d_qkv, tokens, d_middle, mods, *rest):
    pieces, rest = rest[:PIECES], rest[PIECES:]
    input_grad, sums, wide, value, fold_a, fold_b, sems = rest
    for copy in start_all(list(attend_copies(pieces, place, wide)), sems):
        copy.wait()
    rows = tokens.shape[0]
    for part in range(3):
        add = dot_nn(d_qkv[:, part * D : (part + 1) * D], rows_of(wide, part * 16, 16))
        if part == 0:
            value[...] = add
        else:
            value[...] += add
    for ref in (fold_a, fold_b):
        ref[...] = jnp.zeros_like(ref)

    def back(at):
        d_h1 = value[at]
        normed, spread = norm_slab(tokens[at].astype(F32))
        d_token = d_middle[at] + back_slab(d_h1 * (1.0 + mods[1:2]), normed, spread)
        input_grad[at] = d_token.astype(BF16)
        fold(fold_a, d_h1)
        fold(fold_b, d_h1 * normed)

    slabs(rows, SLAB, back)
    sums[...] = jnp.zeros_like(sums)
    sums[0:1] = jnp.sum(fold_a[...], axis=0, keepdims=True)
    sums[1:2] = jnp.sum(fold_b[...], axis=0, keepdims=True)


def output_kernel(place, act, tokens, branch, out_grad, mods, *rest):
    pieces, rest = rest[:PIECES], rest[PIECES:]
    block_out, sums, wide, value, fold_a, sems = rest
    copies = start_all(list(down_copies(pieces, place, wide)), sems)
    rows = tokens.shape[0]
    for copy in copies[:16]:
        copy.wait()
    value[...] = dot_nt(act[:, :DOWN_E], rows_of(wide, 0, 16, pl.ds(0, DOWN_E)))
    for copy in copies[16:]:
        copy.wait()
    rest_cols = pl.ds(DOWN_E, FF - DOWN_E)
    value[...] += dot_nt(act[:, DOWN_E:], rows_of(wide, 0, 16, rest_cols))

    fold_a[...] = jnp.zeros_like(fold_a)

    def finish(at):
        mlp = value[at]
        frame = lax.broadcasted_iota(jnp.int32, (SLAB, 1), 0) % FRAMES
        keep = frame < place[4]
        middle = tokens[at].astype(F32) + mods[2:3] * branch[at]
        block_out[at] = jnp.where(keep, middle + mods[5:6] * mlp, 0.0).astype(BF16)
        fold(fold_a, jnp.where(keep, out_grad[at].astype(F32), 0.0) * mlp)

    slabs(rows, SLAB, finish)
    sums[...] = jnp.zeros_like(sums)
    sums[0:1] = jnp.sum(fold_a[...], axis=0, keepdims=True)


def pair_grads(left, right, ordered_after=(), row_block=288):
    _, rows, depth = left.shape
    cols = right.shape[1]
    n_dep = len(ordered_after)

    def kernel(keep_l, send_l, right_ref, *rest):
        keep, send = rest[n_dep:]
        send[...] = dot_nn(send_l[0], right_ref[...]).astype(BF16)
        keep[...] = dot_nn(keep_l[0], right_ref[...]).astype(BF16)

    col_block = WIDE * 5 if cols > D else cols
    col_block = cols // 4 if cols > D else cols
    grid = (cols // col_block, rows // row_block)
    return pl.pallas_call(
        kernel,
        grid=grid,
        out_shape=[jax.ShapeDtypeStruct((rows, cols), BF16)] * 2,
        in_specs=[
            pl.BlockSpec((1, row_block, depth), lambda j, i: (0, i, 0)),
            pl.BlockSpec((1, row_block, depth), lambda j, i: (1, i, 0)),
            pl.BlockSpec((depth, col_block), lambda j, i: (0, j)),
        ]
        + [any_spec()] * n_dep,
        out_specs=[pl.BlockSpec((row_block, col_block), lambda j, i: (i, j))] * 2,
        compiler_params=pltpu.CompilerParams(vmem_limit_bytes=40 * 2**20),
        cost_estimate=cost(rows * cols * depth / 3e8),
    )(left, left, right, *ordered_after)


def up_grads(place, left, right, ordered_after=()):
    depth, cols = right.shape
    size = left.shape[0] // 16
    n_dep = len(ordered_after)

    def kernel(place_ref, keep_l, send_l, right_ref, *rest):
        keep, send = rest[n_dep:]
        send[0] = dot_nn(send_l[...], right_ref[...]).astype(BF16)
        keep[0] = dot_nn(keep_l[...], right_ref[...]).astype(BF16)

    def index(dc):
        def block(i, place_ref):
            yy = (place_ref[1] + i // 4) % 2
            return ((i % 4 * 2 + yy) * 2 + (place_ref[2] + dc) % 2, 0)

        return block

    return pl.pallas_call(
        kernel,
        out_shape=[jax.ShapeDtypeStruct((8, size, cols), BF16)] * 2,
        grid_spec=pltpu.PrefetchScalarGridSpec(
            num_scalar_prefetch=1,
            grid=(8,),
            in_specs=[
                pl.BlockSpec((size, depth), index(0)),
                pl.BlockSpec((size, depth), index(1)),
                pl.BlockSpec((depth, cols), lambda i, place_ref: (0, 0)),
            ]
            + [any_spec()] * n_dep,
            out_specs=[pl.BlockSpec((1, size, cols), lambda i, place_ref: (i, 0, 0))] * 2,
        ),
        compiler_params=pltpu.CompilerParams(vmem_limit_bytes=40 * 2**20),
        cost_estimate=cost(9),
    )(place, left, left, right, *ordered_after)


def flat_mesh(mesh):
    n_dp, n_cond = mesh.shape["dp"], mesh.shape["cond"]
    return Mesh(mesh.devices.reshape(n_dp // 4, 2, 2, n_cond), ("z", "y", "c", "x"))


def swap(value, axis):
    return lax.ppermute(value, axis, [(0, 1), (1, 0)])


def sum_plane(value):
    for axis in ("c", "x", "y"):
        value = value + swap(value, axis)
    return value


def sum_all(value):
    value = sum_plane(value)
    for step in (1, 2):
        value = value + lax.ppermute(value, "z", [(i, i ^ step) for i in range(4)])
    return value


def turn_z(value, z):
    out = jnp.zeros_like(value)
    own = lax.dynamic_slice_in_dim(value, z, 1, 0)
    out = lax.dynamic_update_slice_in_dim(out, own, z, 0)
    for step in (1, 2, 3):
        entry = lax.dynamic_slice_in_dim(value, (z + step) % 4, 1, 0)
        got = lax.ppermute(entry, "z", [(i, (i + step) % 4) for i in range(4)])
        out = lax.dynamic_update_slice_in_dim(out, got, (z + 4 - step) % 4, 0)
    return out


def add_low(*terms):
    total = terms[0].astype(F32)
    for term in terms[1:]:
        total = total + term.astype(F32)
    return total.astype(BF16)


def after(value, *others):
    return lax.optimization_barrier((value, *others))[0]


def own_block(early, late, flag_early, flag_late, axis, x, before):
    first = x == 0
    near_late, far_late = jnp.where(first, late[0], late[1]), jnp.where(first, late[1], late[0])
    flag = jnp.concatenate(
        [
            jnp.broadcast_to(flag_early, early.shape),
            jnp.broadcast_to(jnp.where(first, flag_late[0], flag_late[1]), near_late.shape),
        ],
        axis=axis,
    )
    got = swap(after(jnp.concatenate([early, far_late], axis=axis), *before), "x")
    return jnp.where(flag, jnp.concatenate([early, near_late], axis=axis), got)


def gather_pieces(near, cut, before_far, before_near_late, before_late, before_core=()):
    far = swap(after(near, *before_far), "y")
    near_late = swap(cut(after(near, *before_near_late)), "x")
    far_late = swap(cut(after(far, near_late, *before_late)), "x")
    pieces = [near, near_late, far, far_late]
    return pieces + [swap(after(piece, *before_core), "c") for piece in pieces]


def core_sum(keep, send, cut, x):
    got = swap(send, "c")
    first = x == 0
    (ke, k0, k1), (ge, g0, g1) = cut(keep), cut(got)
    early = [add_low(ke[i], ge[i]) for i in range(2)]
    late_send = add_low(jnp.where(first, k1, k0), jnp.where(first, g1, g0))
    late_keep = add_low(jnp.where(first, k0, k1), jnp.where(first, g0, g1))
    return early, late_keep, late_send


def late_sum(late_keep, late_send, before):
    got = after(swap(late_send, "x"), *before)
    return [add_low(late_keep[i], got[i]) for i in range(2)]


def over_y(halves, before=()):
    return add_low(halves[0], after(swap(halves[1], "y"), *before))


def over_z(value):
    flat = value.reshape(value.shape[0] * value.shape[1], -1)
    part = lax.psum_scatter(flat, "z", scatter_dimension=0, tiled=True)
    return part.reshape(value.shape[1:])


def on_grid(inputs, out_grad, frame_counts, timesteps, labels, owners, *matrices):
    masters, means, squares = matrices[:7], matrices[7:14], matrices[14:]
    z, y, c, x = (lax.axis_index(axis) for axis in ("z", "y", "c", "x"))
    block = (z * 2 + y) * 2 + c
    device = block * 2 + x
    positions, frames, width = inputs.shape
    rows = positions * frames
    span = width // 16
    clips = timesteps.shape[0]
    clip_index = device * positions // PATCHES
    frame_count = lax.dynamic_index_in_dim(frame_counts, clip_index, 0, keepdims=False)
    place = jnp.stack([z, y, c, x, frame_count, z, z, z]).astype(jnp.int32)
    own = [owners[number] == x for number in range(7)]
    own_low = [master[0].T.astype(BF16) for master in masters]

    attend_t, merge_t, up_t, down_t = own_low[3:]
    tiles = attend_t.reshape(3, span, width)
    flags = jnp.stack([own[3], own[4]])[:, None, None]
    flag = jnp.where(jnp.arange(2 * width) < width, own[3], own[4])
    first_mine = own_block(
        jnp.concatenate([tiles[0], merge_t], axis=1),
        (tiles[1], tiles[2]),
        flag,
        (own[3], own[3]),
        1,
        x,
        (),
    )
    up_mine = own_block(
        up_t[:UP_E],
        (up_t[UP_E : UP_E + UP_L], up_t[UP_E + UP_L :]),
        own[5],
        (own[5], own[5]),
        0,
        x,
        (first_mine,),
    )
    down_mine = own_block(
        down_t[:, :DOWN_E],
        (down_t[:, DOWN_E : DOWN_E + DOWN_L], down_t[:, DOWN_E + DOWN_L :]),
        own[6],
        (own[6], own[6]),
        1,
        x,
        (up_mine,),
    )

    features = timestep_features(timesteps).astype(BF16)
    one_hot = (labels[:, None] == jnp.arange(LABELS)[None, :]).astype(BF16)
    time_part = jnp.where(own[0], contract_cols(features, own_low[0]), 0.0)
    table_part = jnp.where(own[1], contract_cols(one_hot, own_low[1]), 0.0)
    parts = lax.dynamic_update_slice_in_dim(
        jnp.zeros((2, clips, width), F32), jnp.stack([time_part, table_part]), block * span, 2
    )
    parts = sum_all(parts)
    time_pre = parts[0]
    cond_vec = parts[1] + jax.nn.silu(time_pre)
    cond_act, silu_back = jax.vjp(jax.nn.silu, cond_vec)
    cond_act = cond_act.astype(BF16)
    mod_part = jnp.where(own[2], contract_cols(cond_act, own_low[2]), 0.0)
    mod_span = mod_part.shape[1]
    mod_row = lax.dynamic_update_slice(
        jnp.zeros((4, 4, mod_span), F32), turn_z(mod_part, z)[:, None], (0, y * 2 + c, 0)
    )
    mod_row = sum_plane(mod_row)
    mods = jnp.concatenate([mod_row.reshape(6, width), jnp.zeros((2, width), F32)])

    first_near = lax.all_gather(first_mine, "z", axis=0, tiled=False)
    up_near = lax.all_gather(up_mine, "z", axis=0, tiled=False)
    down_near = lax.all_gather(down_mine, "z", axis=0, tiled=False)
    tokens = inputs.reshape(rows, width)
    grad_out = out_grad.reshape(rows, width)
    spot = (place, smem_spec())
    whole = vmem_spec()
    in_vmem = lambda *arrays: [(array, whole) for array in arrays]
    in_place = lambda arrays: [(array, any_spec()) for array in arrays]
    sems = lambda count: pltpu.SemaphoreType.DMA((count,))
    d_mlp, d_mlp_rel = run_kernel(
        start_back_kernel,
        [spot] + in_vmem(grad_out, mods),
        [((rows, width), BF16), ((2, 8, span, rows), BF16)],
        [vmem(width, rows, dtype=F32)],
        us=1,
    )
    firsts = gather_pieces(
        first_near, lambda main: main[:, :, 2 * width :], (mods,), (), ()
    )
    h1, qkv = run_kernel(
        qkv_kernel,
        [spot] + in_vmem(tokens, mods) + in_place(firsts),
        [((rows, width), BF16), ((48, span, rows), BF16)],
        [vmem(48, span, width), sems(48)],
        us=18,
        ordered_after=[d_mlp_rel],
    )
    attended, branch, h2 = run_kernel(
        attend_kernel,
        [spot] + in_vmem(qkv, tokens, mods) + in_place(firsts),
        [((rows, width), BF16), ((rows, width), F32), ((rows, width), BF16)],
        [vmem(16, span, width), vmem(16, span, rows, dtype=F32), sems(16)],
        us=20,
    )
    ups = gather_pieces(up_near, lambda main: main[:, UP_E:], firsts[:1], (), (h1,), (h2,))
    act, slope = run_kernel(
        up_kernel,
        [spot] + in_vmem(h2) + in_place(ups),
        [((rows, FF), BF16, pl.BlockSpec((rows, width), lambda i: (0, i)))] * 2,
        [vmem(FF, width)] + [vmem(rows, WIDE, dtype=F32)] * 2 + [sems(48)],
        steps=4,
        us=15,
    )
    down_keep, down_send = pair_grads(d_mlp_rel.reshape(2, 8 * span, rows), act)
    downs = gather_pieces(down_near, lambda main: main[:, :, DOWN_E:], (h1,), (h2,), (act,), (down_keep,))
    cut_down = lambda v: (
        v[..., :DOWN_E],
        v[..., DOWN_E : DOWN_E + DOWN_L],
        v[..., DOWN_E + DOWN_L :],
    )
    shape = (2, 4, span, FF)
    down_early, *down_late = core_sum(down_keep.reshape(shape), down_send.reshape(shape), cut_down, x)

    d_upper, d_upper_t = run_kernel(
        d_upper_kernel,
        [spot]
        + in_vmem(d_mlp)
        + [(slope, pl.BlockSpec((rows, 2 * WIDE), lambda i: (0, i)))]
        + in_place(downs),
        [
            ((rows, FF), BF16, pl.BlockSpec((rows, 2 * WIDE), lambda i: (0, i))),
            ((FF, rows), BF16, pl.BlockSpec((2 * WIDE, rows), lambda i: (i, 0))),
        ],
        [vmem(16, span, FF)] + [vmem(rows, WIDE, dtype=F32)] * 2 + [sems(48)],
        steps=FF // (2 * WIDE),
        us=16,
    )
    up_keep, up_send = up_grads(place, d_upper_t, h2, [down_early[1], down_late[1]])
    cut_up = lambda v: (v[:, :, :UP_E], v[:, :, UP_E : UP_E + UP_L], v[:, :, UP_E + UP_L :])
    shape = (2, 4, 4 * span, width)
    up_early, *up_late = core_sum(up_keep.reshape(shape), up_send.reshape(shape), cut_up, x)

    d_middle, d_branch, d_branch_rel, d_att, sums_two = run_kernel(
        middle_back_kernel,
        [spot] + in_vmem(d_upper, tokens, grad_out, branch, mods) + in_place(ups + firsts),
        [
            ((rows, width), F32),
            ((rows, width), BF16),
            ((2, 8, span, rows), BF16),
            ((16, span, rows), BF16),
            ((8, width), F32),
        ],
        [
            vmem(FF, width),
            vmem(16, span, width),
            vmem(rows, width, dtype=F32),
            vmem(width, rows, dtype=F32),
        ]
        + [vmem(8, width, dtype=F32)] * 3
        + [sems(64)],
        ordered_after=[up_keep],
        us=24,
    )
    merge_keep, merge_send = pair_grads(d_branch_rel.reshape(2, 8 * span, rows), attended)
    shape = (2, 4, span, width)
    merge_keep = merge_keep.reshape(shape)
    merge_got = swap(merge_send.reshape(shape), "c")
    merge_halves = [add_low(merge_keep[i], merge_got[i]) for i in range(2)]

    down_late = late_sum(*down_late, (d_middle,))
    d_qkv, d_qkv_rel = run_kernel(
        attend_back_kernel,
        [spot] + in_vmem(qkv, d_att),
        [((rows, 3 * width), BF16), ((2, 3, 8, span, rows), BF16)],
        [vmem(16, span, rows, dtype=F32)] * 3,
        ordered_after=[up_early[1], up_late[1], down_late[1]],
        us=25,
    )
    up_late = late_sum(*up_late, (d_qkv,))
    down_total = jnp.concatenate(
        [over_y(down_early, (d_qkv,)), over_y(down_late, (d_qkv,))], axis=-1
    )
    up_over = over_y(up_early)
    attend_keep, attend_send = pair_grads(
        d_qkv_rel.reshape(2, 24 * span, rows), h1, [down_total, up_late[1], up_over]
    )
    cut_attend = lambda v: (v[0], v[1], v[2])
    shape = (3, 2, 4, span, width)
    first_early, *first_late = core_sum(
        attend_keep.reshape(shape), attend_send.reshape(shape), cut_attend, x
    )
    down_part = over_z(down_total)

    input_grad, sums_one = run_kernel(
        input_back_kernel,
        [spot] + in_vmem(d_qkv, tokens, d_middle, mods) + in_place(firsts),
        [((rows, width), BF16), ((8, width), F32)],
        [vmem(48, span, width), vmem(rows, width, dtype=F32)]
        + [vmem(8, width, dtype=F32)] * 2
        + [sems(48)],
        ordered_after=[first_early[1], first_late[1]],
        us=16,
    )
    up_total = jnp.concatenate([up_over, over_y(up_late)], axis=1)
    early_total = jnp.concatenate(
        [over_y(halves, (input_grad,)) for halves in (first_early, merge_halves)], axis=2
    )
    block_out, sums_out = run_kernel(
        output_kernel,
        [spot] + in_vmem(act, tokens, branch, grad_out, mods) + in_place(downs),
        [((rows, width), BF16), ((8, width), F32)],
        [
            vmem(16, span, FF),
            vmem(rows, width, dtype=F32),
            vmem(8, width, dtype=F32),
            sems(48),
        ],
        ordered_after=[up_total, early_total],
        us=17,
    )
    up_part = over_z(after(up_total, down_part))
    first_late = late_sum(*first_late, (block_out,))
    early_part = over_z(after(early_total, up_part))
    late_part = over_z(after(over_y(first_late), up_part))
    down_got, up_got = swap(down_part, "x"), swap(up_part, "x")
    early_got, late_got = swap(early_part, "x"), swap(late_part, "x")

    d_vector = jnp.concatenate([sums_one[:2], sums_two[:3], sums_out[:1]]).reshape(6 * width)
    d_mod = sum_plane(after(d_vector, up_part, first_late[1]).reshape(4, 4, mod_span))
    d_mod = lax.dynamic_index_in_dim(d_mod, y * 2 + c, 1, keepdims=False)
    d_mod = turn_z(d_mod, z)
    grad_mod = contract_rows(d_mod, cond_act.astype(F32), HIGHEST)
    d_cond_part = jnp.dot(
        d_mod, own_low[2].astype(F32), precision=HIGHEST, preferred_element_type=F32
    )
    d_cond_act = sum_all(after(jnp.where(own[2], d_cond_part, 0.0), early_part))
    d_cond = silu_back(d_cond_act)[0]
    d_time_pre = jax.vjp(jax.nn.silu, time_pre)[1](d_cond)[0]
    d_cond_block = lax.dynamic_slice_in_dim(d_cond, block * span, span, 1)
    d_time_block = lax.dynamic_slice_in_dim(d_time_pre, block * span, span, 1)
    grad_table = contract_rows(d_cond_block, one_hot.astype(F32), HIGHEST)
    grad_time = contract_rows(d_time_block, features.astype(F32), HIGHEST)

    def joined(early, part, got, axis):
        first = x == 0
        halves = [jnp.where(first, part, got), jnp.where(first, got, part)]
        return jnp.concatenate([early.astype(BF16)] + halves, axis=axis).astype(F32)

    def both(part, got):
        return part.astype(F32) + got.astype(F32)

    grads = (
        grad_time,
        grad_table,
        grad_mod,
        jnp.concatenate(
            [
                both(early_part[:, :width], early_got[:, :width]),
                jnp.where(x == 0, late_part, late_got).astype(F32),
                jnp.where(x == 0, late_got, late_part).astype(F32),
            ]
        ),
        both(early_part[:, width:], early_got[:, width:]),
        jnp.concatenate(
            [
                both(up_part[:UP_E], up_got[:UP_E]),
                jnp.where(x == 0, up_part[UP_E:], up_got[UP_E:]).astype(F32),
                jnp.where(x == 0, up_got[UP_E:], up_part[UP_E:]).astype(F32),
            ]
        ),
        jnp.concatenate(
            [
                both(down_part[:, :DOWN_E], down_got[:, :DOWN_E]),
                jnp.where(x == 0, down_part[:, DOWN_E:], down_got[:, DOWN_E:]).astype(F32),
                jnp.where(x == 0, down_got[:, DOWN_E:], down_part[:, DOWN_E:]).astype(F32),
            ],
            axis=1,
        ),
    )
    rates = [
        0.5 * FREQ ** (-0.5),
        0.5,
        0.5 * D ** (-0.5),
        0.5 * D ** (-0.5),
        D ** (-0.5),
        0.5 * D ** (-0.5),
        0.5 * FF ** (-0.5),
    ]
    new_list, first_list, second_list, copy_list = ([], [], [], [])
    for number in range(7):
        fresh, mean, square = adamw_step(
            masters[number][0].T,
            means[number][0].T,
            squares[number][0].T,
            grads[number],
            rates[number],
        )
        fresh = jnp.where(own[number], fresh, 0.0).T[None]
        new_list.append(fresh)
        first_list.append(jnp.where(own[number], mean, 0.0).T[None])
        second_list.append(jnp.where(own[number], square, 0.0).T[None])
        copy_list.append(fresh.astype(BF16))
    return (
        block_out.reshape(inputs.shape),
        input_grad.reshape(inputs.shape),
        *new_list,
        *first_list,
        *second_list,
        *copy_list,
    )


def on_device(
    inputs,
    out_grad,
    frame_counts,
    timesteps,
    labels,
    owners,
    w_time,
    w_table,
    w_modulate,
    w_attend,
    w_merge,
    w_up,
    w_down,
    mean_time,
    mean_table,
    mean_modulate,
    mean_attend,
    mean_merge,
    mean_up,
    mean_down,
    square_time,
    square_table,
    square_modulate,
    square_attend,
    square_merge,
    square_up,
    square_down,
):
    masters = (w_time, w_table, w_modulate, w_attend, w_merge, w_up, w_down)
    means = (mean_time, mean_table, mean_modulate, mean_attend, mean_merge, mean_up, mean_down)
    squares = (
        square_time,
        square_table,
        square_modulate,
        square_attend,
        square_merge,
        square_up,
        square_down,
    )
    n_dp = lax.axis_size("dp")
    n_cond = lax.axis_size("cond")
    cond_index = lax.axis_index("cond")
    dp_index = lax.axis_index("dp")
    device = dp_index * n_cond + cond_index
    positions, frames, width = inputs.shape
    clips = timesteps.shape[0]
    clip_index = device * positions // PATCHES
    frame_count = lax.dynamic_index_in_dim(frame_counts, clip_index, 0, keepdims=False)
    both = (
        lax.all_gather(w_time.astype(jnp.bfloat16), "cond", axis=0, tiled=True),
        lax.all_gather(w_table.astype(jnp.bfloat16), "cond", axis=0, tiled=True),
        lax.all_gather(w_modulate.astype(jnp.bfloat16), "cond", axis=0, tiled=True),
        lax.all_gather(w_attend.astype(jnp.bfloat16), "cond", axis=0, tiled=True),
        lax.all_gather(w_merge.astype(jnp.bfloat16), "cond", axis=0, tiled=True),
        lax.all_gather(w_up.astype(jnp.bfloat16), "cond", axis=0, tiled=True),
        lax.all_gather(w_down.astype(jnp.bfloat16), "cond", axis=0, tiled=True),
    )
    owned = [
        lax.dynamic_index_in_dim(pair, owners[number], 0, keepdims=False)
        for number, pair in enumerate(both)
    ]
    time_w, table_w, attend_w, merge_w, up_w, down_w = (
        lax.all_gather(owned[0], "dp", axis=1, tiled=True),
        lax.all_gather(owned[1], "dp", axis=1, tiled=True),
        lax.all_gather(owned[3], "dp", axis=1, tiled=True),
        lax.all_gather(owned[4], "dp", axis=1, tiled=True),
        lax.all_gather(owned[5], "dp", axis=1, tiled=True),
        lax.all_gather(owned[6], "dp", axis=1, tiled=True),
    )
    half_width = owned[2].shape[1] // n_cond
    modulate_half = lax.dynamic_slice_in_dim(owned[2], cond_index * half_width, half_width, 1)
    features = timestep_features(timesteps).astype(jnp.bfloat16)
    time_pre = jnp.dot(features, time_w, preferred_element_type=jnp.float32)
    one_hot = (labels[:, None] == jnp.arange(LABELS)[None, :]).astype(jnp.bfloat16)
    cond_vec = jnp.dot(one_hot, table_w, preferred_element_type=jnp.float32) + jax.nn.silu(time_pre)
    cond_act, silu_back = jax.vjp(jax.nn.silu, cond_vec)
    cond_act = cond_act.astype(jnp.bfloat16)
    mod_part = jnp.dot(cond_act, modulate_half, preferred_element_type=jnp.float32)
    modulation = lax.all_gather(mod_part, ("dp", "cond"), axis=1, tiled=True)
    mod_row = lax.dynamic_index_in_dim(modulation, clip_index, 0, keepdims=False)
    shift_one, scale_one, gate_one, shift_two, scale_two, gate_two = [
        mod_row[part * width : (part + 1) * width] for part in range(6)
    ]
    rows = positions * frames
    tokens = inputs.reshape(rows, width).astype(jnp.float32)
    frame_ids = jnp.tile(jnp.arange(frames), positions)
    row_mask = (frame_ids < frame_count).astype(jnp.float32)[:, None]
    key_valid = jnp.arange(frames) < frame_count
    inv_scale = 1.0 / math.sqrt(HEAD)
    norm_one, rstd_one = normalize(tokens)
    hidden_one = (norm_one * (1.0 + scale_one) + shift_one).astype(jnp.bfloat16)
    qkv = jnp.dot(hidden_one, attend_w, preferred_element_type=jnp.float32).astype(jnp.bfloat16)
    queries = qkv[:, :width].reshape(positions, frames, HEADS, HEAD)
    key_rows = qkv[:, width : 2 * width].reshape(positions, frames, HEADS, HEAD)
    value_rows = qkv[:, 2 * width :].reshape(positions, frames, HEADS, HEAD)
    scores = (
        jnp.einsum("pfhe,pghe->phfg", queries, key_rows, preferred_element_type=jnp.float32)
        * inv_scale
    )
    scores = jnp.where(key_valid[None, None, None, :], scores, -1e30)
    top = jnp.max(scores, axis=-1, keepdims=True)
    expo = jnp.exp(scores - top)
    probs = expo / jnp.sum(expo, axis=-1, keepdims=True)
    probs_low = probs.astype(jnp.bfloat16)
    attended = jnp.einsum(
        "phfg,pghe->pfhe", probs_low, value_rows, preferred_element_type=jnp.float32
    )
    attended = attended.reshape(rows, width).astype(jnp.bfloat16)
    branch = jnp.dot(attended, merge_w, preferred_element_type=jnp.float32)
    middle = tokens + gate_one * branch
    norm_two, rstd_two = normalize(middle)
    hidden_two = (norm_two * (1.0 + scale_two) + shift_two).astype(jnp.bfloat16)
    upper = jnp.dot(hidden_two, up_w, preferred_element_type=jnp.float32)
    activ, gelu_back = jax.vjp(partial(jax.nn.gelu, approximate=True), upper)
    activ = activ.astype(jnp.bfloat16)
    mlp_out = jnp.dot(activ, down_w, preferred_element_type=jnp.float32)
    block_out = (
        (row_mask * (middle + gate_two * mlp_out))
        .reshape(positions, frames, width)
        .astype(jnp.bfloat16)
    )
    attend_b, merge_b, up_b, down_b = (
        lax.all_gather(owned[3], "dp", axis=1, tiled=True),
        lax.all_gather(owned[4], "dp", axis=1, tiled=True),
        lax.all_gather(owned[5], "dp", axis=1, tiled=True),
        lax.all_gather(owned[6], "dp", axis=1, tiled=True),
    )
    grad_out = out_grad.reshape(rows, width).astype(jnp.float32) * row_mask
    d_mlp = (grad_out * gate_two).astype(jnp.bfloat16)
    grad_down = contract_rows(activ, d_mlp)
    d_activ = contract_cols(d_mlp, down_b)
    d_upper = gelu_back(d_activ)[0].astype(jnp.bfloat16)
    grad_up = contract_rows(hidden_two, d_upper)
    d_hidden_two = contract_cols(d_upper, up_b)
    d_middle = grad_out + normalize_back(d_hidden_two * (1.0 + scale_two), norm_two, rstd_two)
    d_branch = (d_middle * gate_one).astype(jnp.bfloat16)
    grad_merge = contract_rows(attended, d_branch)
    d_attended = (
        contract_cols(d_branch, merge_b)
        .astype(jnp.bfloat16)
        .reshape(positions, frames, HEADS, HEAD)
    )
    d_probs = jnp.einsum(
        "pfhe,pghe->phfg", d_attended, value_rows, preferred_element_type=jnp.float32
    )
    d_values = jnp.einsum(
        "phfg,pfhe->pghe", probs_low, d_attended, preferred_element_type=jnp.float32
    )
    d_scores = (probs * (d_probs - jnp.sum(probs * d_probs, axis=-1, keepdims=True))).astype(
        jnp.bfloat16
    )
    d_queries = (
        jnp.einsum("phfg,pghe->pfhe", d_scores, key_rows, preferred_element_type=jnp.float32)
        * inv_scale
    )
    d_keys = (
        jnp.einsum("phfg,pfhe->pghe", d_scores, queries, preferred_element_type=jnp.float32)
        * inv_scale
    )
    d_qkv = jnp.concatenate(
        [
            d_queries.reshape(rows, width),
            d_keys.reshape(rows, width),
            d_values.reshape(rows, width),
        ],
        axis=1,
    ).astype(jnp.bfloat16)
    grad_attend = contract_rows(hidden_one, d_qkv)
    d_hidden_one = contract_cols(d_qkv, attend_b)
    d_tokens = d_middle + normalize_back(d_hidden_one * (1.0 + scale_one), norm_one, rstd_one)
    input_grad = d_tokens.reshape(positions, frames, width).astype(jnp.bfloat16)
    d_vector = jnp.concatenate(
        [
            jnp.sum(d_hidden_one, axis=0),
            jnp.sum(d_hidden_one * norm_one, axis=0),
            jnp.sum(d_middle * branch, axis=0),
            jnp.sum(d_hidden_two, axis=0),
            jnp.sum(d_hidden_two * norm_two, axis=0),
            jnp.sum(grad_out * mlp_out, axis=0),
        ]
    )
    clip_pick = (jnp.arange(clips) == clip_index).astype(jnp.float32)
    d_mod_local = clip_pick[:, None] * d_vector[None, :]
    d_mod_half = lax.psum_scatter(d_mod_local, ("dp", "cond"), scatter_dimension=1, tiled=True)
    grad_mod_half = contract_rows(cond_act.astype(jnp.float32), d_mod_half, HIGHEST)
    d_cond_part = contract_cols(d_mod_half, modulate_half.astype(jnp.float32), HIGHEST)
    d_cond_act = lax.psum(d_cond_part, ("dp", "cond"))
    d_cond = silu_back(d_cond_act)[0]
    grad_table = contract_rows(one_hot.astype(jnp.float32), d_cond, HIGHEST)
    d_time_pre = jax.vjp(jax.nn.silu, time_pre)[1](d_cond)[0]
    grad_time = contract_rows(features.astype(jnp.float32), d_time_pre, HIGHEST)
    span = width // n_dp
    grad_time_block = lax.dynamic_slice_in_dim(grad_time, dp_index * span, span, 1)
    grad_table_block = lax.dynamic_slice_in_dim(grad_table, dp_index * span, span, 1)
    blocks = (
        lax.psum_scatter(grad_attend, "dp", scatter_dimension=1, tiled=True),
        lax.psum_scatter(grad_merge, "dp", scatter_dimension=1, tiled=True),
        lax.psum_scatter(grad_up, "dp", scatter_dimension=1, tiled=True),
        lax.psum_scatter(grad_down, "dp", scatter_dimension=1, tiled=True),
    )
    placed = lax.dynamic_update_slice_in_dim(
        jnp.zeros((width, half_width * n_cond), jnp.float32),
        grad_mod_half,
        cond_index * half_width,
        1,
    )
    row_halves = (
        lax.psum_scatter(
            blocks[0].astype(jnp.bfloat16), "cond", scatter_dimension=0, tiled=True
        ).astype(jnp.float32),
        lax.psum_scatter(
            blocks[1].astype(jnp.bfloat16), "cond", scatter_dimension=0, tiled=True
        ).astype(jnp.float32),
        lax.psum_scatter(
            blocks[2].astype(jnp.bfloat16), "cond", scatter_dimension=0, tiled=True
        ).astype(jnp.float32),
        lax.psum_scatter(
            blocks[3].astype(jnp.bfloat16), "cond", scatter_dimension=0, tiled=True
        ).astype(jnp.float32),
        lax.psum_scatter(
            placed.astype(jnp.bfloat16), "cond", scatter_dimension=0, tiled=True
        ).astype(jnp.float32),
    )
    joined = (
        lax.all_gather(row_halves[0].astype(jnp.bfloat16), "cond", axis=0, tiled=True).astype(
            jnp.float32
        ),
        lax.all_gather(row_halves[1].astype(jnp.bfloat16), "cond", axis=0, tiled=True).astype(
            jnp.float32
        ),
        lax.all_gather(row_halves[2].astype(jnp.bfloat16), "cond", axis=0, tiled=True).astype(
            jnp.float32
        ),
        lax.all_gather(row_halves[3].astype(jnp.bfloat16), "cond", axis=0, tiled=True).astype(
            jnp.float32
        ),
        lax.all_gather(row_halves[4].astype(jnp.bfloat16), "cond", axis=0, tiled=True).astype(
            jnp.float32
        ),
    )
    grads = (
        grad_time_block,
        grad_table_block,
        joined[4],
        joined[0],
        joined[1],
        joined[2],
        joined[3],
    )
    rates = [
        0.5 * FREQ ** (-0.5),
        0.5,
        0.5 * D ** (-0.5),
        0.5 * D ** (-0.5),
        D ** (-0.5),
        0.5 * D ** (-0.5),
        0.5 * FF ** (-0.5),
    ]
    new_list, first_list, second_list, copy_list = ([], [], [], [])
    for number in range(7):
        fresh, first, second = adamw_step(
            masters[number][0], means[number][0], squares[number][0], grads[number], rates[number]
        )
        is_owner = cond_index == owners[number]
        fresh = jnp.where(is_owner, fresh, 0.0)[None]
        new_list.append(fresh)
        first_list.append(jnp.where(is_owner, first, 0.0)[None])
        second_list.append(jnp.where(is_owner, second, 0.0)[None])
        copy_list.append(fresh.astype(jnp.bfloat16))
    return (block_out, input_grad, *new_list, *first_list, *second_list, *copy_list)


def solution(mesh):
    n_dp, n_cond = mesh.shape["dp"], mesh.shape["cond"]
    if (n_dp, n_cond) == (16, 2):
        token_spec = P(("z", "y", "c", "x"), None, None)
        matrix_spec = P("x", None, ("z", "y", "c"))
        return jax.shard_map(
            on_grid,
            mesh=flat_mesh(mesh),
            in_specs=(token_spec,) * 2 + (P(),) * 4 + (matrix_spec,) * 21,
            out_specs=(token_spec,) * 2 + (matrix_spec,) * 28,
            check_vma=False,
        )
    token_spec = P(("dp", "cond"), None, None)
    matrix_spec = P("cond", None, "dp")
    return jax.shard_map(
        on_device,
        mesh=mesh,
        in_specs=(token_spec,) * 2 + (P(),) * 4 + (matrix_spec,) * 21,
        out_specs=(token_spec,) * 2 + (matrix_spec,) * 28,
        check_vma=False,
    )
```

```python
from functools import partial
import math

import jax
import jax.numpy as jnp
from jax import lax
from jax.experimental import pallas as pl
from jax.experimental.pallas import tpu as pltpu
from jax.sharding import Mesh, PartitionSpec as P

D = 1152
HEADS = 16
HEAD = 72
FF = 4608
FREQ = 256
LABELS = 101
FRAMES = 16
PATCHES = 256
STEP = 5


HIGHEST = lax.Precision.HIGHEST
EPSILON = 1e-06


def contract_rows(left, right, precision=None):
    return lax.dot_general(
        left,
        right,
        (((0,), (0,)), ((), ())),
        precision=precision,
        preferred_element_type=jnp.float32,
    )


def contract_cols(left, right, precision=None):
    return lax.dot_general(
        left,
        right,
        (((1,), (1,)), ((), ())),
        precision=precision,
        preferred_element_type=jnp.float32,
    )


def normalize(values):
    centre = values - jnp.mean(values, axis=-1, keepdims=True)
    spread = lax.rsqrt(jnp.mean(centre * centre, axis=-1, keepdims=True) + EPSILON)
    return (centre * spread, spread)


def normalize_back(upstream, normed, spread):
    return spread * (
        upstream
        - jnp.mean(upstream, axis=-1, keepdims=True)
        - normed * jnp.mean(upstream * normed, axis=-1, keepdims=True)
    )


def timestep_features(timesteps):
    half_count = FREQ // 2
    freqs = jnp.exp(-math.log(10000.0) * jnp.arange(half_count, dtype=jnp.float32) / half_count)
    angles = timesteps.astype(jnp.float32)[:, None] * freqs[None, :]
    return jnp.concatenate([jnp.cos(angles), jnp.sin(angles)], axis=1)


def adamw_step(master, first, second, grad, rate):
    first_new = 0.5 * first + 0.5 * grad
    second_new = 0.5 * second + 0.5 * grad * grad
    correct = 1.0 - 0.5**STEP
    update = first_new / correct / (jnp.sqrt(second_new / correct) + 1e-08)
    return (master - rate * (update + 0.01 * master), first_new, second_new)


BF16, F32 = jnp.bfloat16, jnp.float32
SLAB = 128
COST_FLOPS, COST_BYTES = 6e9, 18e6
GROUP = 128
WIDE = 256


def vmem(*shape, dtype=BF16):
    return pltpu.VMEM(shape, dtype)


def any_spec():
    return pl.BlockSpec(memory_space=pl.ANY)


def smem_spec():
    return pl.BlockSpec(memory_space=pltpu.SMEM)


def vmem_spec():
    return pl.BlockSpec(memory_space=pltpu.VMEM)


def dot_nn(left, right):
    return lax.dot_general(left, right, (((1,), (0,)), ((), ())), preferred_element_type=F32)


def dot_nt(left, right):
    return lax.dot_general(left, right, (((1,), (1,)), ((), ())), preferred_element_type=F32)


def cost(us):
    return pl.CostEstimate(flops=int(us * COST_FLOPS), bytes_accessed=int(us * COST_BYTES), transcendentals=0)


def run_kernel(body, operands, outs, scratch, us, ordered_after=(), mib=56, steps=None):
    arrays = [array for array, _ in operands] + list(ordered_after)
    specs = [spec for _, spec in operands] + [any_spec() for _ in ordered_after]
    n_in, n_dep = len(operands), len(ordered_after)

    def kernel(*refs):
        body(*refs[:n_in], *refs[n_in + n_dep :])

    return pl.pallas_call(
        kernel,
        grid=() if steps is None else (steps,),
        out_shape=[jax.ShapeDtypeStruct(*out[:2]) for out in outs],
        in_specs=specs,
        out_specs=[out[2] if len(out) > 2 else vmem_spec() for out in outs],
        scratch_shapes=scratch,
        compiler_params=pltpu.CompilerParams(vmem_limit_bytes=mib * 2**20),
        cost_estimate=cost(us),
    )(*arrays)


PIECES = 8


def block_order(place, zz=None):
    y, c = place[1], place[2]
    for z in range(4) if zz is None else (zz,):
        for dc in range(2):
            for dy in range(2):
                yy = y if dy == 0 else 1 - y
                cc = c if dc == 0 else 1 - c
                yield dc * 4 + dy * 2, z, (z * 2 + yy) * 2 + cc


def start_all(copies, sems):
    made = [pltpu.make_async_copy(src, dst, sems.at[i]) for i, (src, dst) in enumerate(copies)]
    for copy in made:
        copy.start()
    return made


def attend_copies(pieces, place, wide):
    x = place[3]
    for at, zz, b in block_order(place):
        main, other = pieces[at : at + 2]
        yield main.at[zz, :, pl.ds(0, D)], wide.at[b * 3]
        yield main.at[zz, :, pl.ds(2 * D, D)], wide.at[b * 3 + 1 + x]
        yield other.at[zz], wide.at[b * 3 + 2 - x]


def merge_copies(pieces, place, wide):
    for at, zz, b in block_order(place):
        yield pieces[at].at[zz, :, pl.ds(D, D)], wide.at[b]


UP_E, UP_L = 128, 80


def up_copies(pieces, place, wide, z=None):
    x = place[3]
    size = UP_E + 2 * UP_L
    for at, zz, b in block_order(place, z):
        main, other = pieces[at : at + 2]
        row = pl.multiple_of(b * size, 16)
        near_row = pl.multiple_of(b * size + UP_E + UP_L * x, 16)
        other_row = pl.multiple_of(b * size + UP_E + UP_L - UP_L * x, 16)
        yield main.at[zz, pl.ds(0, UP_E)], wide.at[pl.ds(row, UP_E)]
        yield main.at[zz, pl.ds(UP_E, UP_L)], wide.at[pl.ds(near_row, UP_L)]
        yield other.at[zz], wide.at[pl.ds(other_row, UP_L)]


DOWN_E, DOWN_L = 2048, 1280


def down_copies(pieces, place, wide):
    x = place[3]
    near_col = pl.multiple_of(DOWN_E + DOWN_L * x, 128)
    other_col = pl.multiple_of(DOWN_E + DOWN_L - DOWN_L * x, 128)
    for at, zz, b in block_order(place):
        yield pieces[at].at[zz, :, pl.ds(0, DOWN_E)], wide.at[b, :, pl.ds(0, DOWN_E)]
    for at, zz, b in block_order(place):
        main, other = pieces[at : at + 2]
        yield main.at[zz, :, pl.ds(DOWN_E, DOWN_L)], wide.at[b, :, pl.ds(near_col, DOWN_L)]
        yield other.at[zz], wide.at[b, :, pl.ds(other_col, DOWN_L)]


def rows_of(wide, first, count, cols=None):
    value = wide[pl.ds(first, count)] if cols is None else wide[pl.ds(first, count), :, cols]
    return value.astype(F32).reshape(count * HEAD, value.shape[-1]).astype(BF16)


def norm_slab(values):
    mean = jnp.sum(values, axis=1, keepdims=True) * (1.0 / D)
    centre = values - mean
    spread = lax.rsqrt(jnp.sum(centre * centre, axis=1, keepdims=True) * (1.0 / D) + EPSILON)
    return centre * spread, spread


def back_slab(upstream, normed, spread):
    first = jnp.sum(upstream, axis=1, keepdims=True) * (1.0 / D)
    second = jnp.sum(upstream * normed, axis=1, keepdims=True) * (1.0 / D)
    return spread * (upstream - first - normed * second)


def slabs(rows, size, body):
    @pl.loop(0, rows // size)
    def _(i):
        body(pl.ds(pl.multiple_of(i * size, size), size))


def fold(ref, value):
    ref[...] += jnp.sum(value.reshape(value.shape[0] // 8, 8, value.shape[1]), axis=0)


def turn(src, dst):
    @pl.loop(0, src.shape[0] // GROUP)
    def _(i):
        at = pl.ds(pl.multiple_of(i * GROUP, GROUP), GROUP)
        dst[:, at] = src[at].astype(F32).T


def store_relative(ref, turned, y, c):
    for b in range(16):
        zz, yy, cc = b // 4, (b // 2) % 2, b % 2
        dy = y if yy == 0 else 1 - y
        dc = c if cc == 0 else 1 - c
        ref[dc, dy * 4 + zz] = turned[b * HEAD : (b + 1) * HEAD].astype(BF16)


def frame_mask(count):
    keys = lax.broadcasted_iota(jnp.int32, (GROUP, GROUP), 0)
    asks = lax.broadcasted_iota(jnp.int32, (GROUP, GROUP), 1)
    return (keys // FRAMES == asks // FRAMES) & (keys % FRAMES < count)


def probs_of(key, query, mask):
    scores = dot_nn(key.astype(F32).T.astype(BF16), query) * (1.0 / math.sqrt(HEAD))
    scores = jnp.where(mask, scores, -1e30)
    top = jnp.max(scores, axis=0, keepdims=True)
    expo = jnp.exp(scores - top)
    return expo * (1.0 / jnp.sum(expo, axis=0, keepdims=True))


def qkv_kernel(place, tokens, mods, *rest):
    pieces, rest = rest[:PIECES], rest[PIECES:]
    h1, qkv, wide, sems = rest
    copies = start_all(list(attend_copies(pieces, place, wide)), sems)

    def norm_one(at):
        normed, _ = norm_slab(tokens[at].astype(F32))
        h1[at] = (normed * (1.0 + mods[1:2]) + mods[0:1]).astype(BF16)

    slabs(tokens.shape[0], SLAB, norm_one)
    for copy in copies:
        copy.wait()

    @pl.loop(0, 12)
    def _(i):
        value = dot_nt(rows_of(wide, i * 4, 4), h1[...])
        for j in range(4):
            qkv[i * 4 + j] = value[j * HEAD : (j + 1) * HEAD].astype(BF16)


def attend_kernel(place, qkv, tokens, mods, *rest):
    pieces, rest = rest[:PIECES], rest[PIECES:]
    attended, branch, h2, merge, turned, sems = rest
    copies = start_all(list(merge_copies(pieces, place, merge)), sems)
    rows = tokens.shape[0]
    mask = frame_mask(place[4])

    @pl.loop(0, HEADS)
    def _(head):
        for group in range(rows // GROUP):
            at = pl.ds(group * GROUP, GROUP)
            probs = probs_of(qkv[HEADS + head, :, at], qkv[head, :, at], mask)
            turned[head, :, at] = dot_nn(qkv[2 * HEADS + head, :, at], probs.astype(BF16))

    for group in range(rows // GROUP):
        at = pl.ds(group * GROUP, GROUP)
        attended[at] = turned[:, :, at].reshape(D, GROUP).T.astype(BF16)
    for copy in copies:
        copy.wait()
    branch[...] = dot_nt(attended[...], rows_of(merge, 0, 16))

    def norm_two(at):
        middle = tokens[at].astype(F32) + mods[2:3] * branch[at]
        normed, _ = norm_slab(middle)
        h2[at] = (normed * (1.0 + mods[4:5]) + mods[3:4]).astype(BF16)

    slabs(rows, SLAB, norm_two)


def gelu_parts(u):
    root = math.sqrt(2.0 / math.pi)
    square = u * u
    bent = jnp.tanh(u * (root + (root * 0.044715) * square))
    half = 0.5 + 0.5 * bent
    rise = root + (root * 3.0 * 0.044715) * square
    return u * half, half + (0.5 * u) * (1.0 - bent * bent) * rise


def up_kernel(place, h2, *rest):
    pieces, rest = rest[:PIECES], rest[PIECES:]
    act, slope, wide, even, odd, sems = rest
    step = pl.program_id(0)

    @pl.when(step == 0)
    def _():
        start_all(list(up_copies(pieces, place, wide)), sems)

    for i, (src, dst) in enumerate(up_copies(pieces, place, wide, step)):
        pltpu.make_async_copy(src, dst, sems.at[step * 12 + i]).wait()
    rows = h2.shape[0]
    ends = [(at, min(WIDE, D - at)) for at in range(0, D, WIDE)]

    def finish(upper, first, width):
        for row in range(0, rows, 32):
            at = pl.ds(row, 32)
            value, rise = gelu_parts(upper[at, :width])
            act[at, pl.ds(first, width)] = value.astype(BF16)
            slope[at, pl.ds(first, width)] = rise.astype(BF16)

    for number, (first, width) in enumerate(ends):
        upper, before = (even, odd) if number % 2 == 0 else (odd, even)
        at = pl.ds(pl.multiple_of(step * D + first, 128), width)
        upper[:, :width] = dot_nt(h2[...], wide[at])
        if number:
            finish(before, *ends[number - 1])
    finish(even if len(ends) % 2 else odd, *ends[-1])


def start_back_kernel(place, out_grad, mods, d_mlp, relative, turned):
    rows = out_grad.shape[0]

    def scale(at):
        frame = lax.broadcasted_iota(jnp.int32, (SLAB, 1), 0) % FRAMES
        dy = jnp.where(frame < place[4], out_grad[at].astype(F32), 0.0)
        d_mlp[at] = (dy * mods[5:6]).astype(BF16)

    slabs(rows, SLAB, scale)
    turn(d_mlp, turned)
    store_relative(relative, turned, place[1], place[2])


def d_upper_kernel(place, d_mlp, slope, *rest):
    pieces, rest = rest[:PIECES], rest[PIECES:]
    d_upper, d_upper_t, wide, even, odd, sems = rest
    step = pl.program_id(0)

    @pl.when(step == 0)
    def _():
        for copy in start_all(list(down_copies(pieces, place, wide)), sems)[:16]:
            copy.wait()

    @pl.when(step == DOWN_E // (2 * WIDE))
    def _():
        for i, (src, dst) in enumerate(down_copies(pieces, place, wide)):
            if i >= 16:
                pltpu.make_async_copy(src, dst, sems.at[i]).wait()

    rows = d_mlp.shape[0]

    def finish(value, first):
        cols = pl.ds(first, WIDE)
        for row in range(0, rows, GROUP):
            at = pl.ds(row, GROUP)
            part = value[at] * slope[at, cols].astype(F32)
            d_upper[at, cols] = part.astype(BF16)
            d_upper_t[cols, at] = part.T.astype(BF16)

    base = pl.multiple_of(step * 2 * WIDE, 2 * WIDE)
    even[...] = dot_nn(d_mlp[...], rows_of(wide, 0, 16, pl.ds(base, WIDE)))
    odd[...] = dot_nn(d_mlp[...], rows_of(wide, 0, 16, pl.ds(base + WIDE, WIDE)))
    finish(even, 0)
    finish(odd, WIDE)


def middle_back_kernel(place, d_upper, tokens, out_grad, branch, mods, *rest):
    ups, firsts, rest = rest[:PIECES], rest[PIECES : 2 * PIECES], rest[2 * PIECES :]
    d_middle, d_branch, relative, d_att, sums, wide, merge, value, turned, fold_a, fold_b, fold_c, sems = rest
    copies = list(up_copies(ups, place, wide)) + list(merge_copies(firsts, place, merge))
    copies = start_all(copies, sems)
    rows = tokens.shape[0]
    for z in range(4):
        for copy in copies[z * 12 : (z + 1) * 12]:
            copy.wait()
        add = dot_nn(d_upper[:, z * D : (z + 1) * D], wide[z * D : (z + 1) * D])
        if z == 0:
            value[...] = add
        else:
            value[...] += add
    for copy in copies[48:]:
        copy.wait()
    for ref in (fold_a, fold_b, fold_c):
        ref[...] = jnp.zeros_like(ref)

    def back(at):
        d_h2 = value[at]
        arm = branch[at]
        normed, spread = norm_slab(tokens[at].astype(F32) + mods[2:3] * arm)
        frame = lax.broadcasted_iota(jnp.int32, (SLAB, 1), 0) % FRAMES
        dy = jnp.where(frame < place[4], out_grad[at].astype(F32), 0.0)
        d_mid = dy + back_slab(d_h2 * (1.0 + mods[4:5]), normed, spread)
        d_middle[at] = d_mid
        d_branch[at] = (d_mid * mods[2:3]).astype(BF16)
        fold(fold_a, d_mid * arm)
        fold(fold_b, d_h2)
        fold(fold_c, d_h2 * normed)

    slabs(rows, SLAB, back)
    sums[...] = jnp.zeros_like(sums)
    sums[0:1] = jnp.sum(fold_a[...], axis=0, keepdims=True)
    sums[1:2] = jnp.sum(fold_b[...], axis=0, keepdims=True)
    sums[2:3] = jnp.sum(fold_c[...], axis=0, keepdims=True)
    turn(d_branch, turned)
    store_relative(relative, turned, place[1], place[2])
    value[...] = dot_nn(d_branch[...], rows_of(merge, 0, 16))
    turn(value, turned)
    for head in range(HEADS):
        d_att[head] = turned[head * HEAD : (head + 1) * HEAD].astype(BF16)


def attend_back_kernel(place, qkv, d_att, d_qkv, relative, d_q, d_k, d_v):
    rows = qkv.shape[2]
    y, c = place[1], place[2]
    mask = frame_mask(place[4])
    scale = 1.0 / math.sqrt(HEAD)

    @pl.loop(0, HEADS // 2)
    def _(pair):
        for number in range(2 * rows // GROUP):
            head = pair * 2 + number % 2
            at = pl.ds(number // 2 * GROUP, GROUP)
            query, key = qkv[head, :, at], qkv[HEADS + head, :, at]
            val, grad = qkv[2 * HEADS + head, :, at], d_att[head, :, at]
            probs = probs_of(key, query, mask)
            d_probs = dot_nn(val.astype(F32).T.astype(BF16), grad)
            d_v[head, :, at] = dot_nt(grad, probs.astype(BF16))
            inner = jnp.sum(probs * d_probs, axis=0, keepdims=True)
            d_scores = (probs * (d_probs - inner)).astype(BF16)
            d_q[head, :, at] = dot_nn(key, d_scores) * scale
            d_k[head, :, at] = dot_nt(query, d_scores) * scale

    for part, ref in enumerate((d_q, d_k, d_v)):
        for group in range(rows // GROUP):
            at = pl.ds(group * GROUP, GROUP)
            d_qkv[at, part * D : (part + 1) * D] = ref[:, :, at].reshape(D, GROUP).T.astype(BF16)
        for head in range(HEADS):
            number = part * HEADS + head
            b, tile = number // 3, number % 3
            zz, yy, cc = b // 4, (b // 2) % 2, b % 2
            dy = y if yy == 0 else 1 - y
            dc = c if cc == 0 else 1 - c
            relative[dc, tile, dy * 4 + zz] = ref[head].astype(BF16)


def input_back_kernel(place, d_qkv, tokens, d_middle, mods, *rest):
    pieces, rest = rest[:PIECES], rest[PIECES:]
    input_grad, sums, wide, value, fold_a, fold_b, sems = rest
    for copy in start_all(list(attend_copies(pieces, place, wide)), sems):
        copy.wait()
    rows = tokens.shape[0]
    for part in range(3):
        add = dot_nn(d_qkv[:, part * D : (part + 1) * D], rows_of(wide, part * 16, 16))
        if part == 0:
            value[...] = add
        else:
            value[...] += add
    for ref in (fold_a, fold_b):
        ref[...] = jnp.zeros_like(ref)

    def back(at):
        d_h1 = value[at]
        normed, spread = norm_slab(tokens[at].astype(F32))
        d_token = d_middle[at] + back_slab(d_h1 * (1.0 + mods[1:2]), normed, spread)
        input_grad[at] = d_token.astype(BF16)
        fold(fold_a, d_h1)
        fold(fold_b, d_h1 * normed)

    slabs(rows, SLAB, back)
    sums[...] = jnp.zeros_like(sums)
    sums[0:1] = jnp.sum(fold_a[...], axis=0, keepdims=True)
    sums[1:2] = jnp.sum(fold_b[...], axis=0, keepdims=True)


def output_kernel(place, act, tokens, branch, out_grad, mods, *rest):
    pieces, rest = rest[:PIECES], rest[PIECES:]
    block_out, sums, wide, value, fold_a, sems = rest
    copies = start_all(list(down_copies(pieces, place, wide)), sems)
    rows = tokens.shape[0]
    for copy in copies[:16]:
        copy.wait()
    value[...] = dot_nt(act[:, :DOWN_E], rows_of(wide, 0, 16, pl.ds(0, DOWN_E)))
    for copy in copies[16:]:
        copy.wait()
    rest_cols = pl.ds(DOWN_E, FF - DOWN_E)
    value[...] += dot_nt(act[:, DOWN_E:], rows_of(wide, 0, 16, rest_cols))

    fold_a[...] = jnp.zeros_like(fold_a)

    def finish(at):
        mlp = value[at]
        frame = lax.broadcasted_iota(jnp.int32, (SLAB, 1), 0) % FRAMES
        keep = frame < place[4]
        middle = tokens[at].astype(F32) + mods[2:3] * branch[at]
        block_out[at] = jnp.where(keep, middle + mods[5:6] * mlp, 0.0).astype(BF16)
        fold(fold_a, jnp.where(keep, out_grad[at].astype(F32), 0.0) * mlp)

    slabs(rows, SLAB, finish)
    sums[...] = jnp.zeros_like(sums)
    sums[0:1] = jnp.sum(fold_a[...], axis=0, keepdims=True)


def pair_grads(left, right, ordered_after=(), row_block=288):
    _, rows, depth = left.shape
    cols = right.shape[1]
    n_dep = len(ordered_after)

    def kernel(keep_l, send_l, right_ref, *rest):
        keep, send = rest[n_dep:]
        send[...] = dot_nn(send_l[0], right_ref[...]).astype(BF16)
        keep[...] = dot_nn(keep_l[0], right_ref[...]).astype(BF16)

    col_block = WIDE * 5 if cols > D else cols
    col_block = cols // 4 if cols > D else cols
    grid = (cols // col_block, rows // row_block)
    return pl.pallas_call(
        kernel,
        grid=grid,
        out_shape=[jax.ShapeDtypeStruct((rows, cols), BF16)] * 2,
        in_specs=[
            pl.BlockSpec((1, row_block, depth), lambda j, i: (0, i, 0)),
            pl.BlockSpec((1, row_block, depth), lambda j, i: (1, i, 0)),
            pl.BlockSpec((depth, col_block), lambda j, i: (0, j)),
        ]
        + [any_spec()] * n_dep,
        out_specs=[pl.BlockSpec((row_block, col_block), lambda j, i: (i, j))] * 2,
        compiler_params=pltpu.CompilerParams(vmem_limit_bytes=40 * 2**20),
        cost_estimate=cost(0.5),
    )(left, left, right, *ordered_after)


def up_grads(place, left, right, ordered_after=()):
    depth, cols = right.shape
    size = left.shape[0] // 16
    n_dep = len(ordered_after)

    def kernel(place_ref, keep_l, send_l, right_ref, *rest):
        keep, send = rest[n_dep:]
        send[0] = dot_nn(send_l[...], right_ref[...]).astype(BF16)
        keep[0] = dot_nn(keep_l[...], right_ref[...]).astype(BF16)

    def index(dc):
        def block(i, place_ref):
            yy = (place_ref[1] + i // 4) % 2
            return ((i % 4 * 2 + yy) * 2 + (place_ref[2] + dc) % 2, 0)

        return block

    return pl.pallas_call(
        kernel,
        out_shape=[jax.ShapeDtypeStruct((8, size, cols), BF16)] * 2,
        grid_spec=pltpu.PrefetchScalarGridSpec(
            num_scalar_prefetch=1,
            grid=(8,),
            in_specs=[
                pl.BlockSpec((size, depth), index(0)),
                pl.BlockSpec((size, depth), index(1)),
                pl.BlockSpec((depth, cols), lambda i, place_ref: (0, 0)),
            ]
            + [any_spec()] * n_dep,
            out_specs=[pl.BlockSpec((1, size, cols), lambda i, place_ref: (i, 0, 0))] * 2,
        ),
        compiler_params=pltpu.CompilerParams(vmem_limit_bytes=40 * 2**20),
        cost_estimate=cost(9),
    )(place, left, left, right, *ordered_after)


def flat_mesh(mesh):
    n_dp, n_cond = mesh.shape["dp"], mesh.shape["cond"]
    return Mesh(mesh.devices.reshape(n_dp // 4, 2, 2, n_cond), ("z", "y", "c", "x"))


def swap(value, axis):
    return lax.ppermute(value, axis, [(0, 1), (1, 0)])


def sum_plane(value):
    for axis in ("c", "x", "y"):
        value = value + swap(value, axis)
    return value


def sum_all(value):
    value = sum_plane(value)
    for step in (1, 2):
        value = value + lax.ppermute(value, "z", [(i, i ^ step) for i in range(4)])
    return value


def turn_z(value, z):
    out = jnp.zeros_like(value)
    own = lax.dynamic_slice_in_dim(value, z, 1, 0)
    out = lax.dynamic_update_slice_in_dim(out, own, z, 0)
    for step in (1, 2, 3):
        entry = lax.dynamic_slice_in_dim(value, (z + step) % 4, 1, 0)
        got = lax.ppermute(entry, "z", [(i, (i + step) % 4) for i in range(4)])
        out = lax.dynamic_update_slice_in_dim(out, got, (z + 4 - step) % 4, 0)
    return out


def add_low(*terms):
    total = terms[0].astype(F32)
    for term in terms[1:]:
        total = total + term.astype(F32)
    return total.astype(BF16)


def after(value, *others):
    return lax.optimization_barrier((value, *others))[0]


def own_block(early, late, flag_early, flag_late, axis, x, before):
    first = x == 0
    near_late, far_late = jnp.where(first, late[0], late[1]), jnp.where(first, late[1], late[0])
    flag = jnp.concatenate(
        [
            jnp.broadcast_to(flag_early, early.shape),
            jnp.broadcast_to(jnp.where(first, flag_late[0], flag_late[1]), near_late.shape),
        ],
        axis=axis,
    )
    got = swap(after(jnp.concatenate([early, far_late], axis=axis), *before), "x")
    return jnp.where(flag, jnp.concatenate([early, near_late], axis=axis), got)


def gather_pieces(near, cut, before_far, before_near_late, before_late, before_core=()):
    far = swap(after(near, *before_far), "y")
    near_late = swap(cut(after(near, *before_near_late)), "x")
    far_late = swap(cut(after(far, near_late, *before_late)), "x")
    pieces = [near, near_late, far, far_late]
    held = [(), before_late, before_late, before_core]
    return pieces + [swap(after(piece, *hold), "c") for piece, hold in zip(pieces, held)]


def core_sum(keep, send, cut, x):
    got = swap(send, "c")
    first = x == 0
    (ke, k0, k1), (ge, g0, g1) = cut(keep), cut(got)
    early = [add_low(ke[i], ge[i]) for i in range(2)]
    late_send = add_low(jnp.where(first, k1, k0), jnp.where(first, g1, g0))
    late_keep = add_low(jnp.where(first, k0, k1), jnp.where(first, g0, g1))
    return early, late_keep, late_send


def late_sum(late_keep, late_send, before):
    got = after(swap(late_send, "x"), *before)
    return [add_low(late_keep[i], got[i]) for i in range(2)]


def over_y(halves, before=()):
    return add_low(halves[0], after(swap(halves[1], "y"), *before))


def over_z(value):
    flat = value.reshape(value.shape[0] * value.shape[1], -1)
    part = lax.psum_scatter(flat, "z", scatter_dimension=0, tiled=True)
    return part.reshape(value.shape[1:])


def on_grid(inputs, out_grad, frame_counts, timesteps, labels, owners, *matrices):
    masters, means, squares = matrices[:7], matrices[7:14], matrices[14:]
    z, y, c, x = (lax.axis_index(axis) for axis in ("z", "y", "c", "x"))
    block = (z * 2 + y) * 2 + c
    device = block * 2 + x
    positions, frames, width = inputs.shape
    rows = positions * frames
    span = width // 16
    clips = timesteps.shape[0]
    clip_index = device * positions // PATCHES
    frame_count = lax.dynamic_index_in_dim(frame_counts, clip_index, 0, keepdims=False)
    place = jnp.stack([z, y, c, x, frame_count, z, z, z]).astype(jnp.int32)
    own = [owners[number] == x for number in range(7)]
    own_low = [master[0].T.astype(BF16) for master in masters]

    attend_t, merge_t, up_t, down_t = own_low[3:]
    tiles = attend_t.reshape(3, span, width)
    flags = jnp.stack([own[3], own[4]])[:, None, None]
    flag = jnp.where(jnp.arange(2 * width) < width, own[3], own[4])
    first_mine = own_block(
        jnp.concatenate([tiles[0], merge_t], axis=1),
        (tiles[1], tiles[2]),
        flag,
        (own[3], own[3]),
        1,
        x,
        (),
    )
    up_mine = own_block(
        up_t[:UP_E],
        (up_t[UP_E : UP_E + UP_L], up_t[UP_E + UP_L :]),
        own[5],
        (own[5], own[5]),
        0,
        x,
        (first_mine,),
    )
    down_mine = own_block(
        down_t[:, :DOWN_E],
        (down_t[:, DOWN_E : DOWN_E + DOWN_L], down_t[:, DOWN_E + DOWN_L :]),
        own[6],
        (own[6], own[6]),
        1,
        x,
        (up_mine,),
    )

    features = timestep_features(timesteps).astype(BF16)
    one_hot = (labels[:, None] == jnp.arange(LABELS)[None, :]).astype(BF16)
    time_part = jnp.where(own[0], contract_cols(features, own_low[0]), 0.0)
    table_part = jnp.where(own[1], contract_cols(one_hot, own_low[1]), 0.0)
    parts = lax.dynamic_update_slice_in_dim(
        jnp.zeros((2, clips, width), F32), jnp.stack([time_part, table_part]), block * span, 2
    )
    parts = sum_all(parts)
    time_pre = parts[0]
    cond_vec = parts[1] + jax.nn.silu(time_pre)
    cond_act, silu_back = jax.vjp(jax.nn.silu, cond_vec)
    cond_act = cond_act.astype(BF16)
    mod_part = jnp.where(own[2], contract_cols(cond_act, own_low[2]), 0.0)
    mod_span = mod_part.shape[1]
    mod_row = lax.dynamic_update_slice(
        jnp.zeros((4, 4, mod_span), F32), turn_z(mod_part, z)[:, None], (0, y * 2 + c, 0)
    )
    mod_row = sum_plane(mod_row)
    mods = jnp.concatenate([mod_row.reshape(6, width), jnp.zeros((2, width), F32)])

    first_near = lax.all_gather(first_mine, "z", axis=0, tiled=False)
    up_near = lax.all_gather(up_mine, "z", axis=0, tiled=False)
    down_near = lax.all_gather(down_mine, "z", axis=0, tiled=False)
    tokens = inputs.reshape(rows, width)
    grad_out = out_grad.reshape(rows, width)
    spot = (place, smem_spec())
    whole = vmem_spec()
    in_vmem = lambda *arrays: [(array, whole) for array in arrays]
    in_place = lambda arrays: [(array, any_spec()) for array in arrays]
    sems = lambda count: pltpu.SemaphoreType.DMA((count,))
    d_mlp, d_mlp_rel = run_kernel(
        start_back_kernel,
        [spot] + in_vmem(grad_out, mods),
        [((rows, width), BF16), ((2, 8, span, rows), BF16)],
        [vmem(width, rows, dtype=F32)],
        us=1,
    )
    firsts = gather_pieces(
        first_near, lambda main: main[:, :, 2 * width :], (d_mlp_rel,), (), (up_near,)
    )
    h1, qkv = run_kernel(
        qkv_kernel,
        [spot] + in_vmem(tokens, mods) + in_place(firsts),
        [((rows, width), BF16), ((48, span, rows), BF16)],
        [vmem(48, span, width), sems(48)],
        us=2,
        ordered_after=[d_mlp_rel, down_near],
    )
    attended, branch, h2 = run_kernel(
        attend_kernel,
        [spot] + in_vmem(qkv, tokens, mods) + in_place(firsts),
        [((rows, width), BF16), ((rows, width), F32), ((rows, width), BF16)],
        [vmem(16, span, width), vmem(16, span, rows, dtype=F32), sems(16)],
        us=2,
    )
    ups = gather_pieces(up_near, lambda main: main[:, UP_E:], firsts[:1], firsts[3:4], (h1,), (h2,))
    act, slope = run_kernel(
        up_kernel,
        [spot] + in_vmem(h2) + in_place(ups),
        [((rows, FF), BF16, pl.BlockSpec((rows, width), lambda i: (0, i)))] * 2,
        [vmem(FF, width)] + [vmem(rows, WIDE, dtype=F32)] * 2 + [sems(48)],
        steps=4,
        us=2,
    )
    down_keep, down_send = pair_grads(d_mlp_rel.reshape(2, 8 * span, rows), act)
    downs = gather_pieces(down_near, lambda main: main[:, :, DOWN_E:], (), (h2,), (act,), (down_keep,))
    cut_down = lambda v: (
        v[..., :DOWN_E],
        v[..., DOWN_E : DOWN_E + DOWN_L],
        v[..., DOWN_E + DOWN_L :],
    )
    shape = (2, 4, span, FF)
    down_early, *down_late = core_sum(down_keep.reshape(shape), down_send.reshape(shape), cut_down, x)

    d_upper, d_upper_t = run_kernel(
        d_upper_kernel,
        [spot]
        + in_vmem(d_mlp)
        + [(slope, pl.BlockSpec((rows, 2 * WIDE), lambda i: (0, i)))]
        + in_place(downs),
        [
            ((rows, FF), BF16, pl.BlockSpec((rows, 2 * WIDE), lambda i: (0, i))),
            ((FF, rows), BF16, pl.BlockSpec((2 * WIDE, rows), lambda i: (i, 0))),
        ],
        [vmem(16, span, FF)] + [vmem(rows, WIDE, dtype=F32)] * 2 + [sems(48)],
        steps=FF // (2 * WIDE),
        us=16,
    )
    up_keep, up_send = up_grads(place, d_upper_t, h2, [down_early[1], down_late[1]])
    cut_up = lambda v: (v[:, :, :UP_E], v[:, :, UP_E : UP_E + UP_L], v[:, :, UP_E + UP_L :])
    shape = (2, 4, 4 * span, width)
    up_early, *up_late = core_sum(up_keep.reshape(shape), up_send.reshape(shape), cut_up, x)

    d_middle, d_branch, d_branch_rel, d_att, sums_two = run_kernel(
        middle_back_kernel,
        [spot] + in_vmem(d_upper, tokens, grad_out, branch, mods) + in_place(ups + firsts),
        [
            ((rows, width), F32),
            ((rows, width), BF16),
            ((2, 8, span, rows), BF16),
            ((16, span, rows), BF16),
            ((8, width), F32),
        ],
        [
            vmem(FF, width),
            vmem(16, span, width),
            vmem(rows, width, dtype=F32),
            vmem(width, rows, dtype=F32),
        ]
        + [vmem(8, width, dtype=F32)] * 3
        + [sems(64)],
        ordered_after=[up_keep],
        us=24,
    )
    merge_keep, merge_send = pair_grads(d_branch_rel.reshape(2, 8 * span, rows), attended)
    shape = (2, 4, span, width)
    merge_keep = merge_keep.reshape(shape)
    merge_got = swap(merge_send.reshape(shape), "c")
    merge_halves = [add_low(merge_keep[i], merge_got[i]) for i in range(2)]

    down_late = late_sum(*down_late, (d_middle,))
    down_over_early = over_y(down_early)
    down_part = over_z(down_over_early)
    d_qkv, d_qkv_rel = run_kernel(
        attend_back_kernel,
        [spot] + in_vmem(qkv, d_att),
        [((rows, 3 * width), BF16), ((2, 3, 8, span, rows), BF16)],
        [vmem(16, span, rows, dtype=F32)] * 3,
        ordered_after=[up_early[1], up_late[1], down_late[1], down_over_early],
        us=25,
    )
    up_late = late_sum(*up_late, (d_qkv,))
    down_over = over_y(down_late, (d_qkv,))
    up_over = over_y(up_early)
    attend_keep, attend_send = pair_grads(
        d_qkv_rel.reshape(2, 24 * span, rows), h1, [down_over, up_late[1], up_over]
    )
    cut_attend = lambda v: (v[0], v[1], v[2])
    shape = (3, 2, 4, span, width)
    first_early, *first_late = core_sum(
        attend_keep.reshape(shape), attend_send.reshape(shape), cut_attend, x
    )
    down_late_part = over_z(after(down_over, down_part))
    up_part = over_z(after(up_over, down_late_part))

    input_grad, sums_one = run_kernel(
        input_back_kernel,
        [spot] + in_vmem(d_qkv, tokens, d_middle, mods) + in_place(firsts),
        [((rows, width), BF16), ((8, width), F32)],
        [vmem(48, span, width), vmem(rows, width, dtype=F32)]
        + [vmem(8, width, dtype=F32)] * 2
        + [sems(48)],
        ordered_after=[first_early[1], first_late[1]],
        us=3,
    )
    up_late_over = over_y(up_late, (input_grad,))
    early_total = jnp.concatenate(
        [over_y(halves, (input_grad,)) for halves in (first_early, merge_halves)], axis=2
    )
    block_out, sums_out = run_kernel(
        output_kernel,
        [spot] + in_vmem(act, tokens, branch, grad_out, mods) + in_place(downs),
        [((rows, width), BF16), ((8, width), F32)],
        [
            vmem(16, span, FF),
            vmem(rows, width, dtype=F32),
            vmem(8, width, dtype=F32),
            sems(48),
        ],
        ordered_after=[up_late_over, early_total],
        us=3,
    )
    up_late_part = over_z(after(up_late_over, up_part))
    first_late = late_sum(*first_late, (block_out,))
    early_part = over_z(after(early_total, up_late_part))
    first_late_over = over_y(first_late)
    late_part = over_z(after(first_late_over, early_part))

    def ends(part, late):
        early = part.astype(F32) + swap(part, "x").astype(F32)
        other = swap(late, "x")
        first = x == 0
        return early, jnp.where(first, late, other), jnp.where(first, other, late)

    down_ends = ends(down_part, down_late_part)
    up_ends = ends(up_part, up_late_part)
    first_ends = ends(early_part, late_part)

    d_vector = jnp.concatenate([sums_one[:2], sums_two[:3], sums_out[:1]]).reshape(6 * width)
    d_mod = sum_plane(after(d_vector, first_late_over).reshape(4, 4, mod_span))
    d_mod = lax.dynamic_index_in_dim(d_mod, y * 2 + c, 1, keepdims=False)
    d_mod = turn_z(d_mod, z)
    grad_mod = contract_rows(d_mod, cond_act.astype(F32), HIGHEST)
    d_cond_part = jnp.dot(
        d_mod, own_low[2].astype(F32), precision=HIGHEST, preferred_element_type=F32
    )
    d_cond_act = sum_all(after(jnp.where(own[2], d_cond_part, 0.0), late_part))
    d_cond = silu_back(d_cond_act)[0]
    d_time_pre = jax.vjp(jax.nn.silu, time_pre)[1](d_cond)[0]
    d_cond_block = lax.dynamic_slice_in_dim(d_cond, block * span, span, 1)
    d_time_block = lax.dynamic_slice_in_dim(d_time_pre, block * span, span, 1)
    grad_table = contract_rows(d_cond_block, one_hot.astype(F32), HIGHEST)
    grad_time = contract_rows(d_time_block, features.astype(F32), HIGHEST)

    grads = (
        grad_time,
        grad_table,
        grad_mod,
        jnp.concatenate([first_ends[0][:, :width], *first_ends[1:]]),
        first_ends[0][:, width:],
        jnp.concatenate(up_ends),
        jnp.concatenate(down_ends, axis=1),
    )
    rates = [
        0.5 * FREQ ** (-0.5),
        0.5,
        0.5 * D ** (-0.5),
        0.5 * D ** (-0.5),
        D ** (-0.5),
        0.5 * D ** (-0.5),
        0.5 * FF ** (-0.5),
    ]
    new_list, first_list, second_list, copy_list = ([], [], [], [])
    for number in range(7):
        fresh, mean, square = adamw_step(
            masters[number][0].T,
            means[number][0].T,
            squares[number][0].T,
            grads[number],
            rates[number],
        )
        fresh = jnp.where(own[number], fresh, 0.0).T[None]
        new_list.append(fresh)
        first_list.append(jnp.where(own[number], mean, 0.0).T[None])
        second_list.append(jnp.where(own[number], square, 0.0).T[None])
        copy_list.append(fresh.astype(BF16))
    return (
        block_out.reshape(inputs.shape),
        input_grad.reshape(inputs.shape),
        *new_list,
        *first_list,
        *second_list,
        *copy_list,
    )


def on_device(
    inputs,
    out_grad,
    frame_counts,
    timesteps,
    labels,
    owners,
    w_time,
    w_table,
    w_modulate,
    w_attend,
    w_merge,
    w_up,
    w_down,
    mean_time,
    mean_table,
    mean_modulate,
    mean_attend,
    mean_merge,
    mean_up,
    mean_down,
    square_time,
    square_table,
    square_modulate,
    square_attend,
    square_merge,
    square_up,
    square_down,
):
    masters = (w_time, w_table, w_modulate, w_attend, w_merge, w_up, w_down)
    means = (mean_time, mean_table, mean_modulate, mean_attend, mean_merge, mean_up, mean_down)
    squares = (
        square_time,
        square_table,
        square_modulate,
        square_attend,
        square_merge,
        square_up,
        square_down,
    )
    n_dp = lax.axis_size("dp")
    n_cond = lax.axis_size("cond")
    cond_index = lax.axis_index("cond")
    dp_index = lax.axis_index("dp")
    device = dp_index * n_cond + cond_index
    positions, frames, width = inputs.shape
    clips = timesteps.shape[0]
    clip_index = device * positions // PATCHES
    frame_count = lax.dynamic_index_in_dim(frame_counts, clip_index, 0, keepdims=False)
    both = (
        lax.all_gather(w_time.astype(jnp.bfloat16), "cond", axis=0, tiled=True),
        lax.all_gather(w_table.astype(jnp.bfloat16), "cond", axis=0, tiled=True),
        lax.all_gather(w_modulate.astype(jnp.bfloat16), "cond", axis=0, tiled=True),
        lax.all_gather(w_attend.astype(jnp.bfloat16), "cond", axis=0, tiled=True),
        lax.all_gather(w_merge.astype(jnp.bfloat16), "cond", axis=0, tiled=True),
        lax.all_gather(w_up.astype(jnp.bfloat16), "cond", axis=0, tiled=True),
        lax.all_gather(w_down.astype(jnp.bfloat16), "cond", axis=0, tiled=True),
    )
    owned = [
        lax.dynamic_index_in_dim(pair, owners[number], 0, keepdims=False)
        for number, pair in enumerate(both)
    ]
    time_w, table_w, attend_w, merge_w, up_w, down_w = (
        lax.all_gather(owned[0], "dp", axis=1, tiled=True),
        lax.all_gather(owned[1], "dp", axis=1, tiled=True),
        lax.all_gather(owned[3], "dp", axis=1, tiled=True),
        lax.all_gather(owned[4], "dp", axis=1, tiled=True),
        lax.all_gather(owned[5], "dp", axis=1, tiled=True),
        lax.all_gather(owned[6], "dp", axis=1, tiled=True),
    )
    half_width = owned[2].shape[1] // n_cond
    modulate_half = lax.dynamic_slice_in_dim(owned[2], cond_index * half_width, half_width, 1)
    features = timestep_features(timesteps).astype(jnp.bfloat16)
    time_pre = jnp.dot(features, time_w, preferred_element_type=jnp.float32)
    one_hot = (labels[:, None] == jnp.arange(LABELS)[None, :]).astype(jnp.bfloat16)
    cond_vec = jnp.dot(one_hot, table_w, preferred_element_type=jnp.float32) + jax.nn.silu(time_pre)
    cond_act, silu_back = jax.vjp(jax.nn.silu, cond_vec)
    cond_act = cond_act.astype(jnp.bfloat16)
    mod_part = jnp.dot(cond_act, modulate_half, preferred_element_type=jnp.float32)
    modulation = lax.all_gather(mod_part, ("dp", "cond"), axis=1, tiled=True)
    mod_row = lax.dynamic_index_in_dim(modulation, clip_index, 0, keepdims=False)
    shift_one, scale_one, gate_one, shift_two, scale_two, gate_two = [
        mod_row[part * width : (part + 1) * width] for part in range(6)
    ]
    rows = positions * frames
    tokens = inputs.reshape(rows, width).astype(jnp.float32)
    frame_ids = jnp.tile(jnp.arange(frames), positions)
    row_mask = (frame_ids < frame_count).astype(jnp.float32)[:, None]
    key_valid = jnp.arange(frames) < frame_count
    inv_scale = 1.0 / math.sqrt(HEAD)
    norm_one, rstd_one = normalize(tokens)
    hidden_one = (norm_one * (1.0 + scale_one) + shift_one).astype(jnp.bfloat16)
    qkv = jnp.dot(hidden_one, attend_w, preferred_element_type=jnp.float32).astype(jnp.bfloat16)
    queries = qkv[:, :width].reshape(positions, frames, HEADS, HEAD)
    key_rows = qkv[:, width : 2 * width].reshape(positions, frames, HEADS, HEAD)
    value_rows = qkv[:, 2 * width :].reshape(positions, frames, HEADS, HEAD)
    scores = (
        jnp.einsum("pfhe,pghe->phfg", queries, key_rows, preferred_element_type=jnp.float32)
        * inv_scale
    )
    scores = jnp.where(key_valid[None, None, None, :], scores, -1e30)
    top = jnp.max(scores, axis=-1, keepdims=True)
    expo = jnp.exp(scores - top)
    probs = expo / jnp.sum(expo, axis=-1, keepdims=True)
    probs_low = probs.astype(jnp.bfloat16)
    attended = jnp.einsum(
        "phfg,pghe->pfhe", probs_low, value_rows, preferred_element_type=jnp.float32
    )
    attended = attended.reshape(rows, width).astype(jnp.bfloat16)
    branch = jnp.dot(attended, merge_w, preferred_element_type=jnp.float32)
    middle = tokens + gate_one * branch
    norm_two, rstd_two = normalize(middle)
    hidden_two = (norm_two * (1.0 + scale_two) + shift_two).astype(jnp.bfloat16)
    upper = jnp.dot(hidden_two, up_w, preferred_element_type=jnp.float32)
    activ, gelu_back = jax.vjp(partial(jax.nn.gelu, approximate=True), upper)
    activ = activ.astype(jnp.bfloat16)
    mlp_out = jnp.dot(activ, down_w, preferred_element_type=jnp.float32)
    block_out = (
        (row_mask * (middle + gate_two * mlp_out))
        .reshape(positions, frames, width)
        .astype(jnp.bfloat16)
    )
    attend_b, merge_b, up_b, down_b = (
        lax.all_gather(owned[3], "dp", axis=1, tiled=True),
        lax.all_gather(owned[4], "dp", axis=1, tiled=True),
        lax.all_gather(owned[5], "dp", axis=1, tiled=True),
        lax.all_gather(owned[6], "dp", axis=1, tiled=True),
    )
    grad_out = out_grad.reshape(rows, width).astype(jnp.float32) * row_mask
    d_mlp = (grad_out * gate_two).astype(jnp.bfloat16)
    grad_down = contract_rows(activ, d_mlp)
    d_activ = contract_cols(d_mlp, down_b)
    d_upper = gelu_back(d_activ)[0].astype(jnp.bfloat16)
    grad_up = contract_rows(hidden_two, d_upper)
    d_hidden_two = contract_cols(d_upper, up_b)
    d_middle = grad_out + normalize_back(d_hidden_two * (1.0 + scale_two), norm_two, rstd_two)
    d_branch = (d_middle * gate_one).astype(jnp.bfloat16)
    grad_merge = contract_rows(attended, d_branch)
    d_attended = (
        contract_cols(d_branch, merge_b)
        .astype(jnp.bfloat16)
        .reshape(positions, frames, HEADS, HEAD)
    )
    d_probs = jnp.einsum(
        "pfhe,pghe->phfg", d_attended, value_rows, preferred_element_type=jnp.float32
    )
    d_values = jnp.einsum(
        "phfg,pfhe->pghe", probs_low, d_attended, preferred_element_type=jnp.float32
    )
    d_scores = (probs * (d_probs - jnp.sum(probs * d_probs, axis=-1, keepdims=True))).astype(
        jnp.bfloat16
    )
    d_queries = (
        jnp.einsum("phfg,pghe->pfhe", d_scores, key_rows, preferred_element_type=jnp.float32)
        * inv_scale
    )
    d_keys = (
        jnp.einsum("phfg,pfhe->pghe", d_scores, queries, preferred_element_type=jnp.float32)
        * inv_scale
    )
    d_qkv = jnp.concatenate(
        [
            d_queries.reshape(rows, width),
            d_keys.reshape(rows, width),
            d_values.reshape(rows, width),
        ],
        axis=1,
    ).astype(jnp.bfloat16)
    grad_attend = contract_rows(hidden_one, d_qkv)
    d_hidden_one = contract_cols(d_qkv, attend_b)
    d_tokens = d_middle + normalize_back(d_hidden_one * (1.0 + scale_one), norm_one, rstd_one)
    input_grad = d_tokens.reshape(positions, frames, width).astype(jnp.bfloat16)
    d_vector = jnp.concatenate(
        [
            jnp.sum(d_hidden_one, axis=0),
            jnp.sum(d_hidden_one * norm_one, axis=0),
            jnp.sum(d_middle * branch, axis=0),
            jnp.sum(d_hidden_two, axis=0),
            jnp.sum(d_hidden_two * norm_two, axis=0),
            jnp.sum(grad_out * mlp_out, axis=0),
        ]
    )
    clip_pick = (jnp.arange(clips) == clip_index).astype(jnp.float32)
    d_mod_local = clip_pick[:, None] * d_vector[None, :]
    d_mod_half = lax.psum_scatter(d_mod_local, ("dp", "cond"), scatter_dimension=1, tiled=True)
    grad_mod_half = contract_rows(cond_act.astype(jnp.float32), d_mod_half, HIGHEST)
    d_cond_part = contract_cols(d_mod_half, modulate_half.astype(jnp.float32), HIGHEST)
    d_cond_act = lax.psum(d_cond_part, ("dp", "cond"))
    d_cond = silu_back(d_cond_act)[0]
    grad_table = contract_rows(one_hot.astype(jnp.float32), d_cond, HIGHEST)
    d_time_pre = jax.vjp(jax.nn.silu, time_pre)[1](d_cond)[0]
    grad_time = contract_rows(features.astype(jnp.float32), d_time_pre, HIGHEST)
    span = width // n_dp
    grad_time_block = lax.dynamic_slice_in_dim(grad_time, dp_index * span, span, 1)
    grad_table_block = lax.dynamic_slice_in_dim(grad_table, dp_index * span, span, 1)
    blocks = (
        lax.psum_scatter(grad_attend, "dp", scatter_dimension=1, tiled=True),
        lax.psum_scatter(grad_merge, "dp", scatter_dimension=1, tiled=True),
        lax.psum_scatter(grad_up, "dp", scatter_dimension=1, tiled=True),
        lax.psum_scatter(grad_down, "dp", scatter_dimension=1, tiled=True),
    )
    placed = lax.dynamic_update_slice_in_dim(
        jnp.zeros((width, half_width * n_cond), jnp.float32),
        grad_mod_half,
        cond_index * half_width,
        1,
    )
    row_halves = (
        lax.psum_scatter(
            blocks[0].astype(jnp.bfloat16), "cond", scatter_dimension=0, tiled=True
        ).astype(jnp.float32),
        lax.psum_scatter(
            blocks[1].astype(jnp.bfloat16), "cond", scatter_dimension=0, tiled=True
        ).astype(jnp.float32),
        lax.psum_scatter(
            blocks[2].astype(jnp.bfloat16), "cond", scatter_dimension=0, tiled=True
        ).astype(jnp.float32),
        lax.psum_scatter(
            blocks[3].astype(jnp.bfloat16), "cond", scatter_dimension=0, tiled=True
        ).astype(jnp.float32),
        lax.psum_scatter(
            placed.astype(jnp.bfloat16), "cond", scatter_dimension=0, tiled=True
        ).astype(jnp.float32),
    )
    joined = (
        lax.all_gather(row_halves[0].astype(jnp.bfloat16), "cond", axis=0, tiled=True).astype(
            jnp.float32
        ),
        lax.all_gather(row_halves[1].astype(jnp.bfloat16), "cond", axis=0, tiled=True).astype(
            jnp.float32
        ),
        lax.all_gather(row_halves[2].astype(jnp.bfloat16), "cond", axis=0, tiled=True).astype(
            jnp.float32
        ),
        lax.all_gather(row_halves[3].astype(jnp.bfloat16), "cond", axis=0, tiled=True).astype(
            jnp.float32
        ),
        lax.all_gather(row_halves[4].astype(jnp.bfloat16), "cond", axis=0, tiled=True).astype(
            jnp.float32
        ),
    )
    grads = (
        grad_time_block,
        grad_table_block,
        joined[4],
        joined[0],
        joined[1],
        joined[2],
        joined[3],
    )
    rates = [
        0.5 * FREQ ** (-0.5),
        0.5,
        0.5 * D ** (-0.5),
        0.5 * D ** (-0.5),
        D ** (-0.5),
        0.5 * D ** (-0.5),
        0.5 * FF ** (-0.5),
    ]
    new_list, first_list, second_list, copy_list = ([], [], [], [])
    for number in range(7):
        fresh, first, second = adamw_step(
            masters[number][0], means[number][0], squares[number][0], grads[number], rates[number]
        )
        is_owner = cond_index == owners[number]
        fresh = jnp.where(is_owner, fresh, 0.0)[None]
        new_list.append(fresh)
        first_list.append(jnp.where(is_owner, first, 0.0)[None])
        second_list.append(jnp.where(is_owner, second, 0.0)[None])
        copy_list.append(fresh.astype(jnp.bfloat16))
    return (block_out, input_grad, *new_list, *first_list, *second_list, *copy_list)


def solution(mesh):
    n_dp, n_cond = mesh.shape["dp"], mesh.shape["cond"]
    if (n_dp, n_cond) == (16, 2):
        token_spec = P(("z", "y", "c", "x"), None, None)
        matrix_spec = P("x", None, ("z", "y", "c"))
        return jax.shard_map(
            on_grid,
            mesh=flat_mesh(mesh),
            in_specs=(token_spec,) * 2 + (P(),) * 4 + (matrix_spec,) * 21,
            out_specs=(token_spec,) * 2 + (matrix_spec,) * 28,
            check_vma=False,
        )
    token_spec = P(("dp", "cond"), None, None)
    matrix_spec = P("cond", None, "dp")
    return jax.shard_map(
        on_device,
        mesh=mesh,
        in_specs=(token_spec,) * 2 + (P(),) * 4 + (matrix_spec,) * 21,
        out_specs=(token_spec,) * 2 + (matrix_spec,) * 28,
        check_vma=False,
    )
```

```python
from functools import partial
import math

import jax
import jax.numpy as jnp
from jax import lax
from jax.experimental import pallas as pl
from jax.experimental.pallas import tpu as pltpu
from jax.sharding import Mesh, PartitionSpec as P

D = 1152
HEADS = 16
HEAD = 72
FF = 4608
FREQ = 256
LABELS = 101
FRAMES = 16
PATCHES = 256
STEP = 5


HIGHEST = lax.Precision.HIGHEST
EPSILON = 1e-06


def contract_rows(left, right, precision=None):
    return lax.dot_general(
        left,
        right,
        (((0,), (0,)), ((), ())),
        precision=precision,
        preferred_element_type=jnp.float32,
    )


def contract_cols(left, right, precision=None):
    return lax.dot_general(
        left,
        right,
        (((1,), (1,)), ((), ())),
        precision=precision,
        preferred_element_type=jnp.float32,
    )


def normalize(values):
    centre = values - jnp.mean(values, axis=-1, keepdims=True)
    spread = lax.rsqrt(jnp.mean(centre * centre, axis=-1, keepdims=True) + EPSILON)
    return (centre * spread, spread)


def normalize_back(upstream, normed, spread):
    return spread * (
        upstream
        - jnp.mean(upstream, axis=-1, keepdims=True)
        - normed * jnp.mean(upstream * normed, axis=-1, keepdims=True)
    )


def timestep_features(timesteps):
    half_count = FREQ // 2
    freqs = jnp.exp(-math.log(10000.0) * jnp.arange(half_count, dtype=jnp.float32) / half_count)
    angles = timesteps.astype(jnp.float32)[:, None] * freqs[None, :]
    return jnp.concatenate([jnp.cos(angles), jnp.sin(angles)], axis=1)


def adamw_step(master, first, second, grad, rate):
    first_new = 0.5 * first + 0.5 * grad
    second_new = 0.5 * second + 0.5 * grad * grad
    correct = 1.0 - 0.5**STEP
    update = first_new / correct / (jnp.sqrt(second_new / correct) + 1e-08)
    return (master - rate * (update + 0.01 * master), first_new, second_new)


BF16, F32 = jnp.bfloat16, jnp.float32
SLAB = 128
COST_FLOPS, COST_BYTES = 6e9, 18e6
GROUP = 128
WIDE = 256


def vmem(*shape, dtype=BF16):
    return pltpu.VMEM(shape, dtype)


def any_spec():
    return pl.BlockSpec(memory_space=pl.ANY)


def smem_spec():
    return pl.BlockSpec(memory_space=pltpu.SMEM)


def vmem_spec():
    return pl.BlockSpec(memory_space=pltpu.VMEM)


def dot_nn(left, right):
    return lax.dot_general(left, right, (((1,), (0,)), ((), ())), preferred_element_type=F32)


def dot_nt(left, right):
    return lax.dot_general(left, right, (((1,), (1,)), ((), ())), preferred_element_type=F32)


def cost(us):
    return pl.CostEstimate(flops=int(us * COST_FLOPS), bytes_accessed=int(us * COST_BYTES), transcendentals=0)


def run_kernel(body, operands, outs, scratch, us, ordered_after=(), mib=56, steps=None):
    arrays = [array for array, _ in operands] + list(ordered_after)
    specs = [spec for _, spec in operands] + [any_spec() for _ in ordered_after]
    n_in, n_dep = len(operands), len(ordered_after)

    def kernel(*refs):
        body(*refs[:n_in], *refs[n_in + n_dep :])

    return pl.pallas_call(
        kernel,
        grid=() if steps is None else (steps,),
        out_shape=[jax.ShapeDtypeStruct(*out[:2]) for out in outs],
        in_specs=specs,
        out_specs=[out[2] if len(out) > 2 else vmem_spec() for out in outs],
        scratch_shapes=scratch,
        compiler_params=pltpu.CompilerParams(vmem_limit_bytes=mib * 2**20),
        cost_estimate=cost(us),
    )(*arrays)


PIECES = 8


def block_order(place, zz=None):
    y, c = place[1], place[2]
    for z in range(4) if zz is None else (zz,):
        for dc in range(2):
            for dy in range(2):
                yy = y if dy == 0 else 1 - y
                cc = c if dc == 0 else 1 - c
                yield dc * 4 + dy * 2, z, (z * 2 + yy) * 2 + cc


def start_all(copies, sems):
    made = [pltpu.make_async_copy(src, dst, sems.at[i]) for i, (src, dst) in enumerate(copies)]
    for copy in made:
        copy.start()
    return made


def attend_copies(pieces, place, wide):
    x = place[3]
    for at, zz, b in block_order(place):
        main, other = pieces[at : at + 2]
        yield main.at[zz, :, pl.ds(0, D)], wide.at[b * 3]
        yield main.at[zz, :, pl.ds(2 * D, D)], wide.at[b * 3 + 1 + x]
        yield other.at[zz], wide.at[b * 3 + 2 - x]


def merge_copies(pieces, place, wide):
    for at, zz, b in block_order(place):
        yield pieces[at].at[zz, :, pl.ds(D, D)], wide.at[b]


UP_E, UP_L = 128, 80


def up_copies(pieces, place, wide, z=None):
    x = place[3]
    size = UP_E + 2 * UP_L
    for at, zz, b in block_order(place, z):
        main, other = pieces[at : at + 2]
        row = pl.multiple_of(b * size, 16)
        near_row = pl.multiple_of(b * size + UP_E + UP_L * x, 16)
        other_row = pl.multiple_of(b * size + UP_E + UP_L - UP_L * x, 16)
        yield main.at[zz, pl.ds(0, UP_E)], wide.at[pl.ds(row, UP_E)]
        yield main.at[zz, pl.ds(UP_E, UP_L)], wide.at[pl.ds(near_row, UP_L)]
        yield other.at[zz], wide.at[pl.ds(other_row, UP_L)]


DOWN_E, DOWN_L = 2048, 1280


def down_copies(pieces, place, wide):
    x = place[3]
    near_col = pl.multiple_of(DOWN_E + DOWN_L * x, 128)
    other_col = pl.multiple_of(DOWN_E + DOWN_L - DOWN_L * x, 128)
    for at, zz, b in block_order(place):
        yield pieces[at].at[zz, :, pl.ds(0, DOWN_E)], wide.at[b, :, pl.ds(0, DOWN_E)]
    for at, zz, b in block_order(place):
        main, other = pieces[at : at + 2]
        yield main.at[zz, :, pl.ds(DOWN_E, DOWN_L)], wide.at[b, :, pl.ds(near_col, DOWN_L)]
        yield other.at[zz], wide.at[b, :, pl.ds(other_col, DOWN_L)]


def rows_of(wide, first, count, cols=None):
    value = wide[pl.ds(first, count)] if cols is None else wide[pl.ds(first, count), :, cols]
    return value.astype(F32).reshape(count * HEAD, value.shape[-1]).astype(BF16)


def norm_slab(values):
    mean = jnp.sum(values, axis=1, keepdims=True) * (1.0 / D)
    centre = values - mean
    spread = lax.rsqrt(jnp.sum(centre * centre, axis=1, keepdims=True) * (1.0 / D) + EPSILON)
    return centre * spread, spread


def back_slab(upstream, normed, spread):
    first = jnp.sum(upstream, axis=1, keepdims=True) * (1.0 / D)
    second = jnp.sum(upstream * normed, axis=1, keepdims=True) * (1.0 / D)
    return spread * (upstream - first - normed * second)


def slabs(rows, size, body):
    @pl.loop(0, rows // size)
    def _(i):
        body(pl.ds(pl.multiple_of(i * size, size), size))


def fold(ref, value):
    ref[...] += jnp.sum(value.reshape(value.shape[0] // 8, 8, value.shape[1]), axis=0)


def turn(src, dst):
    @pl.loop(0, src.shape[0] // GROUP)
    def _(i):
        at = pl.ds(pl.multiple_of(i * GROUP, GROUP), GROUP)
        dst[:, at] = src[at].astype(F32).T


def store_relative(ref, turned, y, c):
    for b in range(16):
        zz, yy, cc = b // 4, (b // 2) % 2, b % 2
        dy = y if yy == 0 else 1 - y
        dc = c if cc == 0 else 1 - c
        ref[dc, dy * 4 + zz] = turned[b * HEAD : (b + 1) * HEAD].astype(BF16)


def frame_mask(count):
    keys = lax.broadcasted_iota(jnp.int32, (GROUP, GROUP), 0)
    asks = lax.broadcasted_iota(jnp.int32, (GROUP, GROUP), 1)
    return (keys // FRAMES == asks // FRAMES) & (keys % FRAMES < count)


def probs_of(key, query, mask):
    scores = dot_nn(key.astype(F32).T.astype(BF16), query) * (1.0 / math.sqrt(HEAD))
    scores = jnp.where(mask, scores, -1e30)
    top = jnp.max(scores, axis=0, keepdims=True)
    expo = jnp.exp(scores - top)
    return expo * (1.0 / jnp.sum(expo, axis=0, keepdims=True))


def qkv_kernel(place, tokens, mods, *rest):
    pieces, rest = rest[:PIECES], rest[PIECES:]
    h1, qkv, wide, sems = rest
    copies = start_all(list(attend_copies(pieces, place, wide)), sems)

    def norm_one(at):
        normed, _ = norm_slab(tokens[at].astype(F32))
        h1[at] = (normed * (1.0 + mods[1:2]) + mods[0:1]).astype(BF16)

    slabs(tokens.shape[0], SLAB, norm_one)
    for copy in copies:
        copy.wait()

    @pl.loop(0, 12)
    def _(i):
        value = dot_nt(rows_of(wide, i * 4, 4), h1[...])
        for j in range(4):
            qkv[i * 4 + j] = value[j * HEAD : (j + 1) * HEAD].astype(BF16)


def attend_kernel(place, qkv, tokens, mods, *rest):
    pieces, rest = rest[:PIECES], rest[PIECES:]
    attended, branch, h2, merge, turned, sems = rest
    copies = start_all(list(merge_copies(pieces, place, merge)), sems)
    rows = tokens.shape[0]
    mask = frame_mask(place[4])

    @pl.loop(0, HEADS)
    def _(head):
        for group in range(rows // GROUP):
            at = pl.ds(group * GROUP, GROUP)
            probs = probs_of(qkv[HEADS + head, :, at], qkv[head, :, at], mask)
            turned[head, :, at] = dot_nn(qkv[2 * HEADS + head, :, at], probs.astype(BF16))

    for group in range(rows // GROUP):
        at = pl.ds(group * GROUP, GROUP)
        attended[at] = turned[:, :, at].reshape(D, GROUP).T.astype(BF16)
    for copy in copies:
        copy.wait()
    branch[...] = dot_nt(attended[...], rows_of(merge, 0, 16))

    def norm_two(at):
        middle = tokens[at].astype(F32) + mods[2:3] * branch[at]
        normed, _ = norm_slab(middle)
        h2[at] = (normed * (1.0 + mods[4:5]) + mods[3:4]).astype(BF16)

    slabs(rows, SLAB, norm_two)


def gelu_parts(u):
    root = math.sqrt(2.0 / math.pi)
    square = u * u
    bent = jnp.tanh(u * (root + (root * 0.044715) * square))
    half = 0.5 + 0.5 * bent
    rise = root + (root * 3.0 * 0.044715) * square
    return u * half, half + (0.5 * u) * (1.0 - bent * bent) * rise


def up_kernel(place, h2, *rest):
    pieces, rest = rest[:PIECES], rest[PIECES:]
    act, slope, wide, even, odd, sems = rest
    step = pl.program_id(0)

    @pl.when(step == 0)
    def _():
        start_all(list(up_copies(pieces, place, wide)), sems)

    for i, (src, dst) in enumerate(up_copies(pieces, place, wide, step)):
        pltpu.make_async_copy(src, dst, sems.at[step * 12 + i]).wait()
    rows = h2.shape[0]
    ends = [(at, min(WIDE, D - at)) for at in range(0, D, WIDE)]

    def finish(upper, first, width):
        for row in range(0, rows, 32):
            at = pl.ds(row, 32)
            value, rise = gelu_parts(upper[at, :width])
            act[at, pl.ds(first, width)] = value.astype(BF16)
            slope[at, pl.ds(first, width)] = rise.astype(BF16)

    for number, (first, width) in enumerate(ends):
        upper, before = (even, odd) if number % 2 == 0 else (odd, even)
        at = pl.ds(pl.multiple_of(step * D + first, 128), width)
        upper[:, :width] = dot_nt(h2[...], wide[at])
        if number:
            finish(before, *ends[number - 1])
    finish(even if len(ends) % 2 else odd, *ends[-1])


def start_back_kernel(place, out_grad, mods, d_mlp, relative, turned):
    rows = out_grad.shape[0]

    def scale(at):
        frame = lax.broadcasted_iota(jnp.int32, (SLAB, 1), 0) % FRAMES
        dy = jnp.where(frame < place[4], out_grad[at].astype(F32), 0.0)
        d_mlp[at] = (dy * mods[5:6]).astype(BF16)

    slabs(rows, SLAB, scale)
    turn(d_mlp, turned)
    store_relative(relative, turned, place[1], place[2])


def d_upper_kernel(place, d_mlp, slope, *rest):
    pieces, rest = rest[:PIECES], rest[PIECES:]
    d_upper, d_upper_t, wide, even, odd, sems = rest
    step = pl.program_id(0)

    @pl.when(step == 0)
    def _():
        for copy in start_all(list(down_copies(pieces, place, wide)), sems)[:16]:
            copy.wait()

    @pl.when(step == DOWN_E // (2 * WIDE))
    def _():
        for i, (src, dst) in enumerate(down_copies(pieces, place, wide)):
            if i >= 16:
                pltpu.make_async_copy(src, dst, sems.at[i]).wait()

    rows = d_mlp.shape[0]

    def finish(value, first):
        cols = pl.ds(first, WIDE)
        for row in range(0, rows, GROUP):
            at = pl.ds(row, GROUP)
            part = value[at] * slope[at, cols].astype(F32)
            d_upper[at, cols] = part.astype(BF16)
            d_upper_t[cols, at] = part.T.astype(BF16)

    base = pl.multiple_of(step * 2 * WIDE, 2 * WIDE)
    even[...] = dot_nn(d_mlp[...], rows_of(wide, 0, 16, pl.ds(base, WIDE)))
    odd[...] = dot_nn(d_mlp[...], rows_of(wide, 0, 16, pl.ds(base + WIDE, WIDE)))
    finish(even, 0)
    finish(odd, WIDE)


def middle_back_kernel(place, d_upper, tokens, out_grad, branch, mods, *rest):
    ups, firsts, rest = rest[:PIECES], rest[PIECES : 2 * PIECES], rest[2 * PIECES :]
    d_middle, d_branch, relative, d_att, sums, wide, merge, value, turned, fold_a, fold_b, fold_c, sems = rest
    copies = list(up_copies(ups, place, wide)) + list(merge_copies(firsts, place, merge))
    copies = start_all(copies, sems)
    rows = tokens.shape[0]
    for z in range(4):
        for copy in copies[z * 12 : (z + 1) * 12]:
            copy.wait()
        add = dot_nn(d_upper[:, z * D : (z + 1) * D], wide[z * D : (z + 1) * D])
        if z == 0:
            value[...] = add
        else:
            value[...] += add
    for copy in copies[48:]:
        copy.wait()
    for ref in (fold_a, fold_b, fold_c):
        ref[...] = jnp.zeros_like(ref)

    def back(at):
        d_h2 = value[at]
        arm = branch[at]
        normed, spread = norm_slab(tokens[at].astype(F32) + mods[2:3] * arm)
        frame = lax.broadcasted_iota(jnp.int32, (SLAB, 1), 0) % FRAMES
        dy = jnp.where(frame < place[4], out_grad[at].astype(F32), 0.0)
        d_mid = dy + back_slab(d_h2 * (1.0 + mods[4:5]), normed, spread)
        d_middle[at] = d_mid
        d_branch[at] = (d_mid * mods[2:3]).astype(BF16)
        fold(fold_a, d_mid * arm)
        fold(fold_b, d_h2)
        fold(fold_c, d_h2 * normed)

    slabs(rows, SLAB, back)
    sums[...] = jnp.zeros_like(sums)
    sums[0:1] = jnp.sum(fold_a[...], axis=0, keepdims=True)
    sums[1:2] = jnp.sum(fold_b[...], axis=0, keepdims=True)
    sums[2:3] = jnp.sum(fold_c[...], axis=0, keepdims=True)
    turn(d_branch, turned)
    store_relative(relative, turned, place[1], place[2])
    value[...] = dot_nn(d_branch[...], rows_of(merge, 0, 16))
    turn(value, turned)
    for head in range(HEADS):
        d_att[head] = turned[head * HEAD : (head + 1) * HEAD].astype(BF16)


def attend_back_kernel(place, qkv, d_att, d_qkv, relative, d_q, d_k, d_v):
    rows = qkv.shape[2]
    y, c = place[1], place[2]
    mask = frame_mask(place[4])
    scale = 1.0 / math.sqrt(HEAD)

    @pl.loop(0, HEADS // 2)
    def _(pair):
        for number in range(2 * rows // GROUP):
            head = pair * 2 + number % 2
            at = pl.ds(number // 2 * GROUP, GROUP)
            query, key = qkv[head, :, at], qkv[HEADS + head, :, at]
            val, grad = qkv[2 * HEADS + head, :, at], d_att[head, :, at]
            probs = probs_of(key, query, mask)
            d_probs = dot_nn(val.astype(F32).T.astype(BF16), grad)
            d_v[head, :, at] = dot_nt(grad, probs.astype(BF16))
            inner = jnp.sum(probs * d_probs, axis=0, keepdims=True)
            d_scores = (probs * (d_probs - inner)).astype(BF16)
            d_q[head, :, at] = dot_nn(key, d_scores) * scale
            d_k[head, :, at] = dot_nt(query, d_scores) * scale

    for part, ref in enumerate((d_q, d_k, d_v)):
        for group in range(rows // GROUP):
            at = pl.ds(group * GROUP, GROUP)
            d_qkv[at, part * D : (part + 1) * D] = ref[:, :, at].reshape(D, GROUP).T.astype(BF16)
        for head in range(HEADS):
            number = part * HEADS + head
            b, tile = number // 3, number % 3
            zz, yy, cc = b // 4, (b // 2) % 2, b % 2
            dy = y if yy == 0 else 1 - y
            dc = c if cc == 0 else 1 - c
            relative[dc, tile, dy * 4 + zz] = ref[head].astype(BF16)


def input_back_kernel(place, d_qkv, tokens, d_middle, mods, *rest):
    pieces, rest = rest[:PIECES], rest[PIECES:]
    input_grad, sums, wide, value, fold_a, fold_b, sems = rest
    for copy in start_all(list(attend_copies(pieces, place, wide)), sems):
        copy.wait()
    rows = tokens.shape[0]
    for part in range(3):
        add = dot_nn(d_qkv[:, part * D : (part + 1) * D], rows_of(wide, part * 16, 16))
        if part == 0:
            value[...] = add
        else:
            value[...] += add
    for ref in (fold_a, fold_b):
        ref[...] = jnp.zeros_like(ref)

    def back(at):
        d_h1 = value[at]
        normed, spread = norm_slab(tokens[at].astype(F32))
        d_token = d_middle[at] + back_slab(d_h1 * (1.0 + mods[1:2]), normed, spread)
        input_grad[at] = d_token.astype(BF16)
        fold(fold_a, d_h1)
        fold(fold_b, d_h1 * normed)

    slabs(rows, SLAB, back)
    sums[...] = jnp.zeros_like(sums)
    sums[0:1] = jnp.sum(fold_a[...], axis=0, keepdims=True)
    sums[1:2] = jnp.sum(fold_b[...], axis=0, keepdims=True)


def output_kernel(place, act, tokens, branch, out_grad, mods, *rest):
    pieces, rest = rest[:PIECES], rest[PIECES:]
    block_out, sums, wide, value, fold_a, sems = rest
    copies = start_all(list(down_copies(pieces, place, wide)), sems)
    rows = tokens.shape[0]
    for copy in copies[:16]:
        copy.wait()
    value[...] = dot_nt(act[:, :DOWN_E], rows_of(wide, 0, 16, pl.ds(0, DOWN_E)))
    for copy in copies[16:]:
        copy.wait()
    rest_cols = pl.ds(DOWN_E, FF - DOWN_E)
    value[...] += dot_nt(act[:, DOWN_E:], rows_of(wide, 0, 16, rest_cols))

    fold_a[...] = jnp.zeros_like(fold_a)

    def finish(at):
        mlp = value[at]
        frame = lax.broadcasted_iota(jnp.int32, (SLAB, 1), 0) % FRAMES
        keep = frame < place[4]
        middle = tokens[at].astype(F32) + mods[2:3] * branch[at]
        block_out[at] = jnp.where(keep, middle + mods[5:6] * mlp, 0.0).astype(BF16)
        fold(fold_a, jnp.where(keep, out_grad[at].astype(F32), 0.0) * mlp)

    slabs(rows, SLAB, finish)
    sums[...] = jnp.zeros_like(sums)
    sums[0:1] = jnp.sum(fold_a[...], axis=0, keepdims=True)


def pair_grads(left, right, us, ordered_after=(), row_block=288):
    _, rows, depth = left.shape
    cols = right.shape[1]
    n_dep = len(ordered_after)

    def kernel(keep_l, send_l, right_ref, *rest):
        keep, send = rest[n_dep:]
        send[...] = dot_nn(send_l[0], right_ref[...]).astype(BF16)
        keep[...] = dot_nn(keep_l[0], right_ref[...]).astype(BF16)

    col_block = cols // 4 if cols > D else cols
    grid = (cols // col_block, rows // row_block)
    return pl.pallas_call(
        kernel,
        grid=grid,
        out_shape=[jax.ShapeDtypeStruct((rows, cols), BF16)] * 2,
        in_specs=[
            pl.BlockSpec((1, row_block, depth), lambda j, i: (0, i, 0)),
            pl.BlockSpec((1, row_block, depth), lambda j, i: (1, i, 0)),
            pl.BlockSpec((depth, col_block), lambda j, i: (0, j)),
        ]
        + [any_spec()] * n_dep,
        out_specs=[pl.BlockSpec((row_block, col_block), lambda j, i: (i, j))] * 2,
        compiler_params=pltpu.CompilerParams(vmem_limit_bytes=40 * 2**20),
        cost_estimate=cost(us),
    )(left, left, right, *ordered_after)


def up_grads(place, left, right, ordered_after=()):
    depth, cols = right.shape
    size = left.shape[0] // 16
    n_dep = len(ordered_after)

    def kernel(place_ref, keep_l, send_l, right_ref, *rest):
        keep, send = rest[n_dep:]
        send[0] = dot_nn(send_l[...], right_ref[...]).astype(BF16)
        keep[0] = dot_nn(keep_l[...], right_ref[...]).astype(BF16)

    def index(dc):
        def block(i, place_ref):
            yy = (place_ref[1] + i // 4) % 2
            return ((i % 4 * 2 + yy) * 2 + (place_ref[2] + dc) % 2, 0)

        return block

    return pl.pallas_call(
        kernel,
        out_shape=[jax.ShapeDtypeStruct((8, size, cols), BF16)] * 2,
        grid_spec=pltpu.PrefetchScalarGridSpec(
            num_scalar_prefetch=1,
            grid=(8,),
            in_specs=[
                pl.BlockSpec((size, depth), index(0)),
                pl.BlockSpec((size, depth), index(1)),
                pl.BlockSpec((depth, cols), lambda i, place_ref: (0, 0)),
            ]
            + [any_spec()] * n_dep,
            out_specs=[pl.BlockSpec((1, size, cols), lambda i, place_ref: (i, 0, 0))] * 2,
        ),
        compiler_params=pltpu.CompilerParams(vmem_limit_bytes=40 * 2**20),
        cost_estimate=cost(9),
    )(place, left, left, right, *ordered_after)


def flat_mesh(mesh):
    n_dp, n_cond = mesh.shape["dp"], mesh.shape["cond"]
    return Mesh(mesh.devices.reshape(n_dp // 4, 2, 2, n_cond), ("z", "y", "c", "x"))


def swap(value, axis):
    return lax.ppermute(value, axis, [(0, 1), (1, 0)])


def sum_plane(value):
    for axis in ("c", "x", "y"):
        value = value + swap(value, axis)
    return value


def sum_all(value):
    value = sum_plane(value)
    for step in (1, 2):
        value = value + lax.ppermute(value, "z", [(i, i ^ step) for i in range(4)])
    return value


def turn_z(value, z):
    out = jnp.zeros_like(value)
    own = lax.dynamic_slice_in_dim(value, z, 1, 0)
    out = lax.dynamic_update_slice_in_dim(out, own, z, 0)
    for step in (1, 2, 3):
        entry = lax.dynamic_slice_in_dim(value, (z + step) % 4, 1, 0)
        got = lax.ppermute(entry, "z", [(i, (i + step) % 4) for i in range(4)])
        out = lax.dynamic_update_slice_in_dim(out, got, (z + 4 - step) % 4, 0)
    return out


def add_low(*terms):
    total = terms[0].astype(F32)
    for term in terms[1:]:
        total = total + term.astype(F32)
    return total.astype(BF16)


def after(value, *others):
    return lax.optimization_barrier((value, *others))[0]


def own_block(early, late, flag_early, flag_late, axis, x, before):
    first = x == 0
    near_late, far_late = jnp.where(first, late[0], late[1]), jnp.where(first, late[1], late[0])
    flag = jnp.concatenate(
        [
            jnp.broadcast_to(flag_early, early.shape),
            jnp.broadcast_to(jnp.where(first, flag_late[0], flag_late[1]), near_late.shape),
        ],
        axis=axis,
    )
    got = swap(after(jnp.concatenate([early, far_late], axis=axis), *before), "x")
    return jnp.where(flag, jnp.concatenate([early, near_late], axis=axis), got)


def gather_pieces(near, cut, before_far, before_near_late, before_late, before_core=()):
    far = swap(after(near, *before_far), "y")
    near_late = swap(cut(after(near, *before_near_late)), "x")
    far_late = swap(cut(after(far, near_late, *before_late)), "x")
    pieces = [near, near_late, far, far_late]
    held = [(), before_late, before_late, before_core]
    return pieces + [swap(after(piece, *hold), "c") for piece, hold in zip(pieces, held)]


def core_sum(keep, send, cut, x):
    got = swap(send, "c")
    first = x == 0
    (ke, k0, k1), (ge, g0, g1) = cut(keep), cut(got)
    early = [add_low(ke[i], ge[i]) for i in range(2)]
    late_send = add_low(jnp.where(first, k1, k0), jnp.where(first, g1, g0))
    late_keep = add_low(jnp.where(first, k0, k1), jnp.where(first, g0, g1))
    return early, late_keep, late_send


def late_sum(late_keep, late_send, before):
    got = after(swap(late_send, "x"), *before)
    return [add_low(late_keep[i], got[i]) for i in range(2)]


def over_y(halves, before=()):
    return add_low(halves[0], after(swap(halves[1], "y"), *before))


def over_z(value):
    flat = value.reshape(value.shape[0] * value.shape[1], -1)
    part = lax.psum_scatter(flat, "z", scatter_dimension=0, tiled=True)
    return part.reshape(value.shape[1:])


def on_grid(inputs, out_grad, frame_counts, timesteps, labels, owners, *matrices):
    masters, means, squares = matrices[:7], matrices[7:14], matrices[14:]
    z, y, c, x = (lax.axis_index(axis) for axis in ("z", "y", "c", "x"))
    block = (z * 2 + y) * 2 + c
    device = block * 2 + x
    positions, frames, width = inputs.shape
    rows = positions * frames
    span = width // 16
    clips = timesteps.shape[0]
    clip_index = device * positions // PATCHES
    frame_count = lax.dynamic_index_in_dim(frame_counts, clip_index, 0, keepdims=False)
    place = jnp.stack([z, y, c, x, frame_count, z, z, z]).astype(jnp.int32)
    own = [owners[number] == x for number in range(7)]
    own_low = [master[0].T.astype(BF16) for master in masters]

    attend_t, merge_t, up_t, down_t = own_low[3:]
    tiles = attend_t.reshape(3, span, width)
    flags = jnp.stack([own[3], own[4]])[:, None, None]
    flag = jnp.where(jnp.arange(2 * width) < width, own[3], own[4])
    first_mine = own_block(
        jnp.concatenate([tiles[0], merge_t], axis=1),
        (tiles[1], tiles[2]),
        flag,
        (own[3], own[3]),
        1,
        x,
        (),
    )
    up_mine = own_block(
        up_t[:UP_E],
        (up_t[UP_E : UP_E + UP_L], up_t[UP_E + UP_L :]),
        own[5],
        (own[5], own[5]),
        0,
        x,
        (first_mine,),
    )
    down_mine = own_block(
        down_t[:, :DOWN_E],
        (down_t[:, DOWN_E : DOWN_E + DOWN_L], down_t[:, DOWN_E + DOWN_L :]),
        own[6],
        (own[6], own[6]),
        1,
        x,
        (up_mine,),
    )

    features = timestep_features(timesteps).astype(BF16)
    one_hot = (labels[:, None] == jnp.arange(LABELS)[None, :]).astype(BF16)
    time_part = jnp.where(own[0], contract_cols(features, own_low[0]), 0.0)
    table_part = jnp.where(own[1], contract_cols(one_hot, own_low[1]), 0.0)
    parts = lax.dynamic_update_slice_in_dim(
        jnp.zeros((2, clips, width), F32), jnp.stack([time_part, table_part]), block * span, 2
    )
    parts = sum_all(parts)
    time_pre = parts[0]
    cond_vec = parts[1] + jax.nn.silu(time_pre)
    cond_act = jax.nn.silu(cond_vec).astype(BF16)
    mod_part = jnp.where(own[2], contract_cols(cond_act, own_low[2]), 0.0)
    mod_span = mod_part.shape[1]
    mod_row = lax.dynamic_update_slice(
        jnp.zeros((4, 4, mod_span), F32), turn_z(mod_part, z)[:, None], (0, y * 2 + c, 0)
    )
    mod_row = sum_plane(mod_row)
    mods = jnp.concatenate([mod_row.reshape(6, width), jnp.zeros((2, width), F32)])

    first_near = lax.all_gather(first_mine, "z", axis=0, tiled=False)
    up_near = lax.all_gather(up_mine, "z", axis=0, tiled=False)
    down_near = lax.all_gather(down_mine, "z", axis=0, tiled=False)
    tokens = inputs.reshape(rows, width)
    grad_out = out_grad.reshape(rows, width)
    spot = (place, smem_spec())
    whole = vmem_spec()
    in_vmem = lambda *arrays: [(array, whole) for array in arrays]
    in_place = lambda arrays: [(array, any_spec()) for array in arrays]
    sems = lambda count: pltpu.SemaphoreType.DMA((count,))
    d_mlp, d_mlp_rel = run_kernel(
        start_back_kernel,
        [spot] + in_vmem(grad_out, mods),
        [((rows, width), BF16), ((2, 8, span, rows), BF16)],
        [vmem(width, rows, dtype=F32)],
        us=1,
    )
    firsts = gather_pieces(
        first_near, lambda main: main[:, :, 2 * width :], (d_mlp_rel,), (), (up_near,)
    )
    h1, qkv = run_kernel(
        qkv_kernel,
        [spot] + in_vmem(tokens, mods) + in_place(firsts),
        [((rows, width), BF16), ((48, span, rows), BF16)],
        [vmem(48, span, width), sems(48)],
        us=2,
        ordered_after=[d_mlp_rel, down_near],
    )
    attended, branch, h2 = run_kernel(
        attend_kernel,
        [spot] + in_vmem(qkv, tokens, mods) + in_place(firsts),
        [((rows, width), BF16), ((rows, width), F32), ((rows, width), BF16)],
        [vmem(16, span, width), vmem(16, span, rows, dtype=F32), sems(16)],
        us=2,
    )
    ups = gather_pieces(up_near, lambda main: main[:, UP_E:], firsts[:1], firsts[3:4], (h1,), (h2,))
    act, slope = run_kernel(
        up_kernel,
        [spot] + in_vmem(h2) + in_place(ups),
        [((rows, FF), BF16, pl.BlockSpec((rows, width), lambda i: (0, i)))] * 2,
        [vmem(FF, width)] + [vmem(rows, WIDE, dtype=F32)] * 2 + [sems(48)],
        steps=4,
        us=2,
    )
    down_keep, down_send = pair_grads(d_mlp_rel.reshape(2, 8 * span, rows), act, 0.5)
    downs = gather_pieces(down_near, lambda main: main[:, :, DOWN_E:], (), (h2,), (act,), (down_keep,))
    cut_down = lambda v: (
        v[..., :DOWN_E],
        v[..., DOWN_E : DOWN_E + DOWN_L],
        v[..., DOWN_E + DOWN_L :],
    )
    shape = (2, 4, span, FF)
    down_early, *down_late = core_sum(down_keep.reshape(shape), down_send.reshape(shape), cut_down, x)

    d_upper, d_upper_t = run_kernel(
        d_upper_kernel,
        [spot]
        + in_vmem(d_mlp)
        + [(slope, pl.BlockSpec((rows, 2 * WIDE), lambda i: (0, i)))]
        + in_place(downs),
        [
            ((rows, FF), BF16, pl.BlockSpec((rows, 2 * WIDE), lambda i: (0, i))),
            ((FF, rows), BF16, pl.BlockSpec((2 * WIDE, rows), lambda i: (i, 0))),
        ],
        [vmem(16, span, FF)] + [vmem(rows, WIDE, dtype=F32)] * 2 + [sems(48)],
        steps=FF // (2 * WIDE),
        us=16,
    )
    up_keep, up_send = up_grads(place, d_upper_t, h2, [down_early[1], down_late[1]])
    cut_up = lambda v: (v[:, :, :UP_E], v[:, :, UP_E : UP_E + UP_L], v[:, :, UP_E + UP_L :])
    shape = (2, 4, 4 * span, width)
    up_early, *up_late = core_sum(up_keep.reshape(shape), up_send.reshape(shape), cut_up, x)

    d_middle, d_branch, d_branch_rel, d_att, sums_two = run_kernel(
        middle_back_kernel,
        [spot] + in_vmem(d_upper, tokens, grad_out, branch, mods) + in_place(ups + firsts),
        [
            ((rows, width), F32),
            ((rows, width), BF16),
            ((2, 8, span, rows), BF16),
            ((16, span, rows), BF16),
            ((8, width), F32),
        ],
        [
            vmem(FF, width),
            vmem(16, span, width),
            vmem(rows, width, dtype=F32),
            vmem(width, rows, dtype=F32),
        ]
        + [vmem(8, width, dtype=F32)] * 3
        + [sems(64)],
        ordered_after=[up_keep],
        us=24,
    )
    merge_keep, merge_send = pair_grads(d_branch_rel.reshape(2, 8 * span, rows), attended, 0.02)
    shape = (2, 4, span, width)
    merge_keep = merge_keep.reshape(shape)
    merge_got = swap(merge_send.reshape(shape), "c")
    merge_halves = [add_low(merge_keep[i], merge_got[i]) for i in range(2)]

    down_late = late_sum(*down_late, (d_middle,))
    down_over_early = over_y(down_early)
    down_part = over_z(down_over_early)
    d_qkv, d_qkv_rel = run_kernel(
        attend_back_kernel,
        [spot] + in_vmem(qkv, d_att),
        [((rows, 3 * width), BF16), ((2, 3, 8, span, rows), BF16)],
        [vmem(16, span, rows, dtype=F32)] * 3,
        ordered_after=[up_early[1], up_late[1], down_late[1], down_over_early],
        us=25,
    )
    up_late = late_sum(*up_late, (d_qkv,))
    down_over = over_y(down_late, (d_qkv,))
    up_over = over_y(up_early)
    attend_keep, attend_send = pair_grads(
        d_qkv_rel.reshape(2, 24 * span, rows), h1, 0.02, [down_over, up_late[1], up_over]
    )
    cut_attend = lambda v: (v[0], v[1], v[2])
    shape = (3, 2, 4, span, width)
    first_early, *first_late = core_sum(
        attend_keep.reshape(shape), attend_send.reshape(shape), cut_attend, x
    )
    down_late_part = over_z(after(down_over, down_part))
    up_part = over_z(after(up_over, down_late_part))

    input_grad, sums_one = run_kernel(
        input_back_kernel,
        [spot] + in_vmem(d_qkv, tokens, d_middle, mods) + in_place(firsts),
        [((rows, width), BF16), ((8, width), F32)],
        [vmem(48, span, width), vmem(rows, width, dtype=F32)]
        + [vmem(8, width, dtype=F32)] * 2
        + [sems(48)],
        ordered_after=[first_early[1], first_late[1]],
        us=3,
    )
    up_late_over = over_y(up_late, (input_grad,))
    early_total = jnp.concatenate(
        [over_y(halves, (input_grad,)) for halves in (first_early, merge_halves)], axis=2
    )
    block_out, sums_out = run_kernel(
        output_kernel,
        [spot] + in_vmem(act, tokens, branch, grad_out, mods) + in_place(downs),
        [((rows, width), BF16), ((8, width), F32)],
        [
            vmem(16, span, FF),
            vmem(rows, width, dtype=F32),
            vmem(8, width, dtype=F32),
            sems(48),
        ],
        ordered_after=[up_late_over, early_total],
        us=3,
    )
    up_late_part = over_z(after(up_late_over, up_part))
    first_late = late_sum(*first_late, (block_out,))
    early_part = over_z(after(early_total, up_late_part))
    first_late_over = over_y(first_late)
    late_part = over_z(after(first_late_over, early_part))

    def ends(part, late):
        early = part.astype(F32) + swap(part, "x").astype(F32)
        other = swap(late, "x")
        first = x == 0
        return early, jnp.where(first, late, other), jnp.where(first, other, late)

    down_ends = ends(down_part, down_late_part)
    up_ends = ends(up_part, up_late_part)
    first_ends = ends(early_part, late_part)

    d_vector = jnp.concatenate([sums_one[:2], sums_two[:3], sums_out[:1]]).reshape(6 * width)
    d_mod = sum_plane(after(d_vector, first_late_over).reshape(4, 4, mod_span))
    d_mod = lax.dynamic_index_in_dim(d_mod, y * 2 + c, 1, keepdims=False)
    d_mod = turn_z(d_mod, z)
    rates = [
        0.5 * FREQ ** (-0.5),
        0.5,
        0.5 * D ** (-0.5),
        0.5 * D ** (-0.5),
        D ** (-0.5),
        0.5 * D ** (-0.5),
        0.5 * FF ** (-0.5),
    ]

    def updated(number, grad):
        results = adamw_step(
            masters[number][0].T, means[number][0].T, squares[number][0].T, grad, rates[number]
        )
        return [jnp.where(own[number], result, 0.0).T[None] for result in results]

    updated_mod = updated(2, contract_rows(d_mod, cond_act.astype(F32), HIGHEST))
    d_cond_part = jnp.dot(
        d_mod, own_low[2].astype(F32), precision=HIGHEST, preferred_element_type=F32
    )
    d_cond_part = after(jnp.where(own[2], d_cond_part, 0.0), early_part)
    d_cond_part = d_cond_part.reshape(clips, 4, 4 * span)
    d_cond_act = jnp.sum(turn_z(d_cond_part.transpose(1, 0, 2), z), axis=0)
    d_cond_act = sum_plane(after(d_cond_act, late_part, updated_mod[0]))
    d_cond_act = lax.dynamic_slice_in_dim(d_cond_act, (y * 2 + c) * span, span, 1)
    time_block = lax.dynamic_slice_in_dim(time_pre, block * span, span, 1)
    cond_block = lax.dynamic_slice_in_dim(cond_vec, block * span, span, 1)
    d_cond_block = jax.vjp(jax.nn.silu, cond_block)[1](d_cond_act)[0]
    d_time_block = jax.vjp(jax.nn.silu, time_block)[1](d_cond_block)[0]
    grad_table = contract_rows(d_cond_block, one_hot.astype(F32), HIGHEST)
    grad_time = contract_rows(d_time_block, features.astype(F32), HIGHEST)

    grads = (
        grad_time,
        grad_table,
        None,
        jnp.concatenate([first_ends[0][:, :width], *first_ends[1:]]),
        first_ends[0][:, width:],
        jnp.concatenate(up_ends),
        jnp.concatenate(down_ends, axis=1),
    )
    new_list, first_list, second_list, copy_list = ([], [], [], [])
    for number in range(7):
        fresh, mean, square = updated_mod if number == 2 else updated(number, grads[number])
        new_list.append(fresh)
        first_list.append(mean)
        second_list.append(square)
        copy_list.append(fresh.astype(BF16))
    return (
        block_out.reshape(inputs.shape),
        input_grad.reshape(inputs.shape),
        *new_list,
        *first_list,
        *second_list,
        *copy_list,
    )


def on_device(
    inputs,
    out_grad,
    frame_counts,
    timesteps,
    labels,
    owners,
    w_time,
    w_table,
    w_modulate,
    w_attend,
    w_merge,
    w_up,
    w_down,
    mean_time,
    mean_table,
    mean_modulate,
    mean_attend,
    mean_merge,
    mean_up,
    mean_down,
    square_time,
    square_table,
    square_modulate,
    square_attend,
    square_merge,
    square_up,
    square_down,
):
    masters = (w_time, w_table, w_modulate, w_attend, w_merge, w_up, w_down)
    means = (mean_time, mean_table, mean_modulate, mean_attend, mean_merge, mean_up, mean_down)
    squares = (
        square_time,
        square_table,
        square_modulate,
        square_attend,
        square_merge,
        square_up,
        square_down,
    )
    n_dp = lax.axis_size("dp")
    n_cond = lax.axis_size("cond")
    cond_index = lax.axis_index("cond")
    dp_index = lax.axis_index("dp")
    device = dp_index * n_cond + cond_index
    positions, frames, width = inputs.shape
    clips = timesteps.shape[0]
    clip_index = device * positions // PATCHES
    frame_count = lax.dynamic_index_in_dim(frame_counts, clip_index, 0, keepdims=False)
    both = (
        lax.all_gather(w_time.astype(jnp.bfloat16), "cond", axis=0, tiled=True),
        lax.all_gather(w_table.astype(jnp.bfloat16), "cond", axis=0, tiled=True),
        lax.all_gather(w_modulate.astype(jnp.bfloat16), "cond", axis=0, tiled=True),
        lax.all_gather(w_attend.astype(jnp.bfloat16), "cond", axis=0, tiled=True),
        lax.all_gather(w_merge.astype(jnp.bfloat16), "cond", axis=0, tiled=True),
        lax.all_gather(w_up.astype(jnp.bfloat16), "cond", axis=0, tiled=True),
        lax.all_gather(w_down.astype(jnp.bfloat16), "cond", axis=0, tiled=True),
    )
    owned = [
        lax.dynamic_index_in_dim(pair, owners[number], 0, keepdims=False)
        for number, pair in enumerate(both)
    ]
    time_w, table_w, attend_w, merge_w, up_w, down_w = (
        lax.all_gather(owned[0], "dp", axis=1, tiled=True),
        lax.all_gather(owned[1], "dp", axis=1, tiled=True),
        lax.all_gather(owned[3], "dp", axis=1, tiled=True),
        lax.all_gather(owned[4], "dp", axis=1, tiled=True),
        lax.all_gather(owned[5], "dp", axis=1, tiled=True),
        lax.all_gather(owned[6], "dp", axis=1, tiled=True),
    )
    half_width = owned[2].shape[1] // n_cond
    modulate_half = lax.dynamic_slice_in_dim(owned[2], cond_index * half_width, half_width, 1)
    features = timestep_features(timesteps).astype(jnp.bfloat16)
    time_pre = jnp.dot(features, time_w, preferred_element_type=jnp.float32)
    one_hot = (labels[:, None] == jnp.arange(LABELS)[None, :]).astype(jnp.bfloat16)
    cond_vec = jnp.dot(one_hot, table_w, preferred_element_type=jnp.float32) + jax.nn.silu(time_pre)
    cond_act, silu_back = jax.vjp(jax.nn.silu, cond_vec)
    cond_act = cond_act.astype(jnp.bfloat16)
    mod_part = jnp.dot(cond_act, modulate_half, preferred_element_type=jnp.float32)
    modulation = lax.all_gather(mod_part, ("dp", "cond"), axis=1, tiled=True)
    mod_row = lax.dynamic_index_in_dim(modulation, clip_index, 0, keepdims=False)
    shift_one, scale_one, gate_one, shift_two, scale_two, gate_two = [
        mod_row[part * width : (part + 1) * width] for part in range(6)
    ]
    rows = positions * frames
    tokens = inputs.reshape(rows, width).astype(jnp.float32)
    frame_ids = jnp.tile(jnp.arange(frames), positions)
    row_mask = (frame_ids < frame_count).astype(jnp.float32)[:, None]
    key_valid = jnp.arange(frames) < frame_count
    inv_scale = 1.0 / math.sqrt(HEAD)
    norm_one, rstd_one = normalize(tokens)
    hidden_one = (norm_one * (1.0 + scale_one) + shift_one).astype(jnp.bfloat16)
    qkv = jnp.dot(hidden_one, attend_w, preferred_element_type=jnp.float32).astype(jnp.bfloat16)
    queries = qkv[:, :width].reshape(positions, frames, HEADS, HEAD)
    key_rows = qkv[:, width : 2 * width].reshape(positions, frames, HEADS, HEAD)
    value_rows = qkv[:, 2 * width :].reshape(positions, frames, HEADS, HEAD)
    scores = (
        jnp.einsum("pfhe,pghe->phfg", queries, key_rows, preferred_element_type=jnp.float32)
        * inv_scale
    )
    scores = jnp.where(key_valid[None, None, None, :], scores, -1e30)
    top = jnp.max(scores, axis=-1, keepdims=True)
    expo = jnp.exp(scores - top)
    probs = expo / jnp.sum(expo, axis=-1, keepdims=True)
    probs_low = probs.astype(jnp.bfloat16)
    attended = jnp.einsum(
        "phfg,pghe->pfhe", probs_low, value_rows, preferred_element_type=jnp.float32
    )
    attended = attended.reshape(rows, width).astype(jnp.bfloat16)
    branch = jnp.dot(attended, merge_w, preferred_element_type=jnp.float32)
    middle = tokens + gate_one * branch
    norm_two, rstd_two = normalize(middle)
    hidden_two = (norm_two * (1.0 + scale_two) + shift_two).astype(jnp.bfloat16)
    upper = jnp.dot(hidden_two, up_w, preferred_element_type=jnp.float32)
    activ, gelu_back = jax.vjp(partial(jax.nn.gelu, approximate=True), upper)
    activ = activ.astype(jnp.bfloat16)
    mlp_out = jnp.dot(activ, down_w, preferred_element_type=jnp.float32)
    block_out = (
        (row_mask * (middle + gate_two * mlp_out))
        .reshape(positions, frames, width)
        .astype(jnp.bfloat16)
    )
    attend_b, merge_b, up_b, down_b = (
        lax.all_gather(owned[3], "dp", axis=1, tiled=True),
        lax.all_gather(owned[4], "dp", axis=1, tiled=True),
        lax.all_gather(owned[5], "dp", axis=1, tiled=True),
        lax.all_gather(owned[6], "dp", axis=1, tiled=True),
    )
    grad_out = out_grad.reshape(rows, width).astype(jnp.float32) * row_mask
    d_mlp = (grad_out * gate_two).astype(jnp.bfloat16)
    grad_down = contract_rows(activ, d_mlp)
    d_activ = contract_cols(d_mlp, down_b)
    d_upper = gelu_back(d_activ)[0].astype(jnp.bfloat16)
    grad_up = contract_rows(hidden_two, d_upper)
    d_hidden_two = contract_cols(d_upper, up_b)
    d_middle = grad_out + normalize_back(d_hidden_two * (1.0 + scale_two), norm_two, rstd_two)
    d_branch = (d_middle * gate_one).astype(jnp.bfloat16)
    grad_merge = contract_rows(attended, d_branch)
    d_attended = (
        contract_cols(d_branch, merge_b)
        .astype(jnp.bfloat16)
        .reshape(positions, frames, HEADS, HEAD)
    )
    d_probs = jnp.einsum(
        "pfhe,pghe->phfg", d_attended, value_rows, preferred_element_type=jnp.float32
    )
    d_values = jnp.einsum(
        "phfg,pfhe->pghe", probs_low, d_attended, preferred_element_type=jnp.float32
    )
    d_scores = (probs * (d_probs - jnp.sum(probs * d_probs, axis=-1, keepdims=True))).astype(
        jnp.bfloat16
    )
    d_queries = (
        jnp.einsum("phfg,pghe->pfhe", d_scores, key_rows, preferred_element_type=jnp.float32)
        * inv_scale
    )
    d_keys = (
        jnp.einsum("phfg,pfhe->pghe", d_scores, queries, preferred_element_type=jnp.float32)
        * inv_scale
    )
    d_qkv = jnp.concatenate(
        [
            d_queries.reshape(rows, width),
            d_keys.reshape(rows, width),
            d_values.reshape(rows, width),
        ],
        axis=1,
    ).astype(jnp.bfloat16)
    grad_attend = contract_rows(hidden_one, d_qkv)
    d_hidden_one = contract_cols(d_qkv, attend_b)
    d_tokens = d_middle + normalize_back(d_hidden_one * (1.0 + scale_one), norm_one, rstd_one)
    input_grad = d_tokens.reshape(positions, frames, width).astype(jnp.bfloat16)
    d_vector = jnp.concatenate(
        [
            jnp.sum(d_hidden_one, axis=0),
            jnp.sum(d_hidden_one * norm_one, axis=0),
            jnp.sum(d_middle * branch, axis=0),
            jnp.sum(d_hidden_two, axis=0),
            jnp.sum(d_hidden_two * norm_two, axis=0),
            jnp.sum(grad_out * mlp_out, axis=0),
        ]
    )
    clip_pick = (jnp.arange(clips) == clip_index).astype(jnp.float32)
    d_mod_local = clip_pick[:, None] * d_vector[None, :]
    d_mod_half = lax.psum_scatter(d_mod_local, ("dp", "cond"), scatter_dimension=1, tiled=True)
    grad_mod_half = contract_rows(cond_act.astype(jnp.float32), d_mod_half, HIGHEST)
    d_cond_part = contract_cols(d_mod_half, modulate_half.astype(jnp.float32), HIGHEST)
    d_cond_act = lax.psum(d_cond_part, ("dp", "cond"))
    d_cond = silu_back(d_cond_act)[0]
    grad_table = contract_rows(one_hot.astype(jnp.float32), d_cond, HIGHEST)
    d_time_pre = jax.vjp(jax.nn.silu, time_pre)[1](d_cond)[0]
    grad_time = contract_rows(features.astype(jnp.float32), d_time_pre, HIGHEST)
    span = width // n_dp
    grad_time_block = lax.dynamic_slice_in_dim(grad_time, dp_index * span, span, 1)
    grad_table_block = lax.dynamic_slice_in_dim(grad_table, dp_index * span, span, 1)
    blocks = (
        lax.psum_scatter(grad_attend, "dp", scatter_dimension=1, tiled=True),
        lax.psum_scatter(grad_merge, "dp", scatter_dimension=1, tiled=True),
        lax.psum_scatter(grad_up, "dp", scatter_dimension=1, tiled=True),
        lax.psum_scatter(grad_down, "dp", scatter_dimension=1, tiled=True),
    )
    placed = lax.dynamic_update_slice_in_dim(
        jnp.zeros((width, half_width * n_cond), jnp.float32),
        grad_mod_half,
        cond_index * half_width,
        1,
    )
    row_halves = (
        lax.psum_scatter(
            blocks[0].astype(jnp.bfloat16), "cond", scatter_dimension=0, tiled=True
        ).astype(jnp.float32),
        lax.psum_scatter(
            blocks[1].astype(jnp.bfloat16), "cond", scatter_dimension=0, tiled=True
        ).astype(jnp.float32),
        lax.psum_scatter(
            blocks[2].astype(jnp.bfloat16), "cond", scatter_dimension=0, tiled=True
        ).astype(jnp.float32),
        lax.psum_scatter(
            blocks[3].astype(jnp.bfloat16), "cond", scatter_dimension=0, tiled=True
        ).astype(jnp.float32),
        lax.psum_scatter(
            placed.astype(jnp.bfloat16), "cond", scatter_dimension=0, tiled=True
        ).astype(jnp.float32),
    )
    joined = (
        lax.all_gather(row_halves[0].astype(jnp.bfloat16), "cond", axis=0, tiled=True).astype(
            jnp.float32
        ),
        lax.all_gather(row_halves[1].astype(jnp.bfloat16), "cond", axis=0, tiled=True).astype(
            jnp.float32
        ),
        lax.all_gather(row_halves[2].astype(jnp.bfloat16), "cond", axis=0, tiled=True).astype(
            jnp.float32
        ),
        lax.all_gather(row_halves[3].astype(jnp.bfloat16), "cond", axis=0, tiled=True).astype(
            jnp.float32
        ),
        lax.all_gather(row_halves[4].astype(jnp.bfloat16), "cond", axis=0, tiled=True).astype(
            jnp.float32
        ),
    )
    grads = (
        grad_time_block,
        grad_table_block,
        joined[4],
        joined[0],
        joined[1],
        joined[2],
        joined[3],
    )
    rates = [
        0.5 * FREQ ** (-0.5),
        0.5,
        0.5 * D ** (-0.5),
        0.5 * D ** (-0.5),
        D ** (-0.5),
        0.5 * D ** (-0.5),
        0.5 * FF ** (-0.5),
    ]
    new_list, first_list, second_list, copy_list = ([], [], [], [])
    for number in range(7):
        fresh, first, second = adamw_step(
            masters[number][0], means[number][0], squares[number][0], grads[number], rates[number]
        )
        is_owner = cond_index == owners[number]
        fresh = jnp.where(is_owner, fresh, 0.0)[None]
        new_list.append(fresh)
        first_list.append(jnp.where(is_owner, first, 0.0)[None])
        second_list.append(jnp.where(is_owner, second, 0.0)[None])
        copy_list.append(fresh.astype(jnp.bfloat16))
    return (block_out, input_grad, *new_list, *first_list, *second_list, *copy_list)


def solution(mesh):
    n_dp, n_cond = mesh.shape["dp"], mesh.shape["cond"]
    if (n_dp, n_cond) == (16, 2):
        token_spec = P(("z", "y", "c", "x"), None, None)
        matrix_spec = P("x", None, ("z", "y", "c"))
        return jax.shard_map(
            on_grid,
            mesh=flat_mesh(mesh),
            in_specs=(token_spec,) * 2 + (P(),) * 4 + (matrix_spec,) * 21,
            out_specs=(token_spec,) * 2 + (matrix_spec,) * 28,
            check_vma=False,
        )
    token_spec = P(("dp", "cond"), None, None)
    matrix_spec = P("cond", None, "dp")
    return jax.shard_map(
        on_device,
        mesh=mesh,
        in_specs=(token_spec,) * 2 + (P(),) * 4 + (matrix_spec,) * 21,
        out_specs=(token_spec,) * 2 + (matrix_spec,) * 28,
        check_vma=False,
    )
```
